32 devices in a mesh: grp: 2 (over y), dev: 16 (over z, x, core).
Axes of the slice: x: 2, y: 2, z: 4, core: 2. Of those that a mesh axis runs over, the one named last changes fastest.
Arguments:
- offsets: float32 [128, 3, 512], P(('grp', 'dev')), may hold values from 0 to 1
- sketch: bfloat16 [128, 512, 256], P(('grp', 'dev')), may hold values from -6 to 6
- pattern: int32 [128, 6], P(('grp', 'dev')), may hold values 0 or 1
- point_order: int32 [128, 512], P(('grp', 'dev')), may hold values from 0 to 511, each once within a row
Outputs:
- basis: bfloat16 [128, 512, 256], P(('grp', 'dev'))
- basis_factor: float32 [128, 256, 256], P(('grp', 'dev'))
The draws below stay inside these ranges and needn't reach their ends.
Inputs may be any that keep to these rules, and one draw needn't show every extreme that they name: `point_order`: each row is a permutation of 0 .. 511.
All inputs are finite; a program needn't handle non-finite values. No bound on the sum of `pattern` on one device may be relied on, other than what follows from the above.
Results may differ from the reference program's by a relative error of at most 0.0082.
Values may be sent and summed in bfloat16 or wider, within the bound.
No kernel may reach another device: no remote copies, remote signals or barrier semaphores. Data moves between devices by JAX's collectives and lax.ppermute only.
A program may use at most 64 MiB of HBM per device.

```python
import math
import jax
import jax.numpy as jnp
from jax import lax

M = 512
R = 256
W = 4
NADM = 6
NCL = 128


def place_ends(entries, stream_key, smallest, high):
    longest = entries.shape.index(max(entries.shape))
    spots = []
    for shift in (0, 1):
        where = [jax.random.randint(jax.random.fold_in(stream_key, axis), (), 0, length) for axis, length in enumerate(entries.shape)]
        where[longest] = (where[longest] + shift) % entries.shape[longest]
        spots.append(tuple(where))
    return entries.at[spots[0]].set(smallest).at[spots[1]].set(high)


def level_of(own_key, extent, pieces, smallest, top_value):
    loudness, own = 1.0, jax.random.fold_in(own_key, 6)
    for position, blocks in pieces:
        draws = jnp.exp(jax.random.uniform(jax.random.fold_in(own, position), (blocks,), jnp.float32, smallest / len(pieces), top_value / len(pieces)))
        loudness = loudness * jnp.repeat(draws, extent[position] // blocks).reshape([-1 if axis == position else 1 for axis in range(len(extent))])
    return loudness


def gaussian(own_key, shape, scale, limit, cuts=(), kind=jnp.bfloat16):
    result = scale * jax.random.normal(own_key, shape, jnp.float32)
    if cuts:
        result = result * level_of(own_key, shape, cuts, -0.22, 0.18)
    return jnp.clip(result, -limit, limit).astype(kind)


def setup_inputs(seed: int = 0) -> dict:
    seeds = jax.random.split(jax.random.key(seed), 5)
    offsets = jnp.clip(1.0 * jax.random.uniform(seeds[0], (NCL, 3, M), jnp.float32) ** level_of(seeds[0], (NCL, 3, M), ((0, 32),), -0.2, 0.2), 0.0, 1.0)
    sketch = gaussian(seeds[1], (NCL, M, R), 1.0, 6.0, ((0, 32),))
    pattern = place_ends((jax.random.randint(seeds[2], (NCL, NADM), 0, 3) < 2).astype(jnp.int32), jax.random.fold_in(seeds[2], 1), 0, 1)
    point_order = jax.vmap(lambda own: jax.random.permutation(own, M))(jax.random.split(seeds[3], NCL)).reshape((NCL, M)).astype(jnp.int32)
    return dict(offsets=offsets, sketch=sketch, pattern=pattern, point_order=point_order)


wave_number = 40.0
decay_length = 4.0
softening = 0.5

def offset_table(reach):
    return [-value for value in range(reach, 1, -1)] + list(range(2, reach + 1))

def with_index(points, start):
    count = points.shape[0]
    index = (start + jnp.arange(count, dtype=jnp.int32)).astype(points.dtype)
    unit = jnp.zeros((1, 3, 1), points.dtype).at[0, 0, 0].set(1.0)
    return points + index[:, None, None] * unit

def kernel_block(target_side, source_side, weight):
    squared = (target_side[0][:, None] - source_side[0][None, :]) ** 2
    squared = squared + (target_side[1][:, None] - source_side[1][None, :]) ** 2
    squared = squared + (target_side[2][:, None] - source_side[2][None, :]) ** 2
    distance = jnp.sqrt(squared)
    values = jnp.cos(wave_number * distance) * jnp.exp(-distance / decay_length) / (distance + softening)
    scale = weight * (1.0 / math.sqrt(target_side.shape[1]))
    return (values * scale).astype(jnp.bfloat16)

def basis_of(samples):
    gram = jnp.dot(samples.T.astype(jnp.float32), samples.astype(jnp.float32), precision=lax.Precision.HIGHEST, preferred_element_type=jnp.float32)
    width = gram.shape[0]
    shift = 0.01 * jnp.trace(gram) / width + 1e-05
    lower = jnp.linalg.cholesky(gram + shift * jnp.eye(width, dtype=jnp.float32))
    rows = jax.scipy.linalg.solve_triangular(lower, samples.T, lower=True)
    return (rows.T.astype(jnp.bfloat16), lower.T)

def reference(offsets, sketch, pattern, point_order):
    total_clusters = offsets.shape[0]
    places = with_index(offsets, 0)
    order = jnp.broadcast_to(point_order[:, None, :], places.shape)
    targets = jnp.take_along_axis(places, order, axis=2)
    padded_offsets = jnp.pad(offsets, ((W, W), (0, 0), (0, 0)))
    window_places = with_index(padded_offsets, -W)
    window_sketch = jnp.pad(sketch, ((W, W), (0, 0), (0, 0)))
    table = offset_table(W)

    def one_cluster(cluster):
        target_side = lax.dynamic_index_in_dim(targets, cluster, 0, keepdims=False)
        total = jnp.zeros((sketch.shape[1], sketch.shape[2]), jnp.float32)
        for column, shift_value in enumerate(table):
            source = cluster + W + shift_value
            source_side = lax.dynamic_index_in_dim(window_places, source, 0, keepdims=False)
            source_rows = lax.dynamic_index_in_dim(window_sketch, source, 0, keepdims=False)
            weight = lax.dynamic_index_in_dim(pattern[:, column], cluster, 0, keepdims=False).astype(jnp.float32)
            block = kernel_block(target_side, source_side, weight)
            total = total + jnp.dot(block.astype(jnp.float32), source_rows.astype(jnp.float32), preferred_element_type=jnp.float32)
        return basis_of(total)
    basis, basis_factor = lax.map(one_cluster, jnp.arange(total_clusters, dtype=jnp.int32), batch_size=8)
    return (basis, basis_factor)
```

```python
import functools
import math

import numpy as np
import jax
import jax.numpy as jnp
from jax import lax
from jax.experimental import pallas as pl
from jax.experimental.pallas import tpu as pltpu
from jax.sharding import PartitionSpec as P

W = 4
AXES = ("grp", "dev")
f32 = jnp.float32
bf16 = jnp.bfloat16

wave_number = 40.0
decay_length = 4.0
softening = 0.5
turns = wave_number / (2.0 * math.pi)

SINE = (4.44288292, -7.30824569, 3.60635423, -0.84611167, 0.10982452)


def passed_along(array, by):
    peers = lax.axis_size(AXES)
    pairs = [(i, i + by) for i in range(peers) if 0 <= i + by < peers]
    return lax.ppermute(array, AXES, pairs)


def offset_table(reach):
    return [-value for value in range(reach, 1, -1)] + list(range(2, reach + 1))


def kernel_values(turn_squared, points):
    turn = turn_squared * lax.rsqrt(turn_squared)
    part = turn - jnp.round(turn)
    square = part * part
    sine = f32(SINE[-1])
    for value in SINE[-2::-1]:
        sine = sine * square + f32(value)
    sine = sine * part
    decay = jnp.exp2(
        turn * f32(-math.log2(math.e) / (decay_length * turns)) + f32(math.log2(turns / math.sqrt(points)))
    )
    level = decay * pltpu.reciprocal(turn + f32(softening * turns), approx=True)
    return level - level * (sine * sine)


def pieces(x):
    high = x.astype(bf16).astype(f32)
    middle = (x - high).astype(bf16).astype(f32)
    low = (x - high - middle).astype(bf16).astype(f32)
    return high, middle, low


def turn_squares(target, source, distance):
    row = lax.broadcasted_iota(jnp.int32, target.shape, 0)
    half = distance.astype(f32) * f32(0.5)

    def shifted(x, along):
        moved = x + jnp.where(row == 0, along, jnp.where(row < 3, f32(-0.5), f32(0)))
        moved = moved * f32(turns)
        return moved, jnp.sum(moved * moved, axis=0, keepdims=True)

    left, left_norm = shifted(target, -half - f32(0.5))
    right, right_norm = shifted(source, half - f32(0.5))
    left = jnp.where(row == 3, left_norm, jnp.where(row == 4, f32(1), left))
    right = jnp.where(row == 4, right_norm, jnp.where(row == 3, f32(1), f32(-2) * right))
    lh, lm, ll = pieces(left)
    rh, rm, rl = pieces(right)
    a = jnp.concatenate([lh, lh, lm, lm, lh, ll, lm, ll], axis=0).astype(bf16)
    b = jnp.concatenate([rh, rm, rh, rm, rl, rh, rl, rm], axis=0).astype(bf16)
    return contract(a, b, 0, 0)


def halves(x):
    hi = x.astype(bf16)
    return hi, (x - hi.astype(f32)).astype(bf16)

def contract(a, b, da, db):
    return lax.dot_general(a, b, (((da,), (db,)), ((), ())), preferred_element_type=f32)

def lane_of(x, lane):
    return jnp.broadcast_to(x[:, lane:lane + 1], x.shape)

def factor_panel(rows, ups, first, panel, micro):
    half = first // 128
    base = first % 128
    lanes = lax.broadcasted_iota(jnp.int32, (8, 128), 1)
    for start in range(0, panel, micro):
        lane0 = base + start
        inside = (lanes >= lane0) & (lanes < lane0 + micro)
        raw = [rows[half, 8 * (start + j):8 * (start + j) + 8, :] for j in range(micro)]
        other = [rows[1 - half, 8 * (start + j):8 * (start + j) + 8, :] for j in range(micro)]
        a = [[lane_of(raw[i], lane0 + k) for k in range(i + 1)] for i in range(micro)]
        low = [[None] * micro for _ in range(micro)]
        inv = [None] * micro
        for k in range(micro):
            inv[k] = lax.rsqrt(a[k][k])
            for i in range(k + 1, micro):
                low[i][k] = a[i][k] * inv[k]
            for i in range(k + 1, micro):
                for m in range(k + 1, i + 1):
                    a[i][m] = a[i][m] - low[i][k] * low[m][k]
        solved = [jnp.where(inside, jnp.where(lanes == lane0 + j, f32(1), f32(0)), raw[j]) for j in range(micro)]
        for k in range(micro):
            raw[k] = raw[k] * inv[k]
            solved[k] = solved[k] * inv[k]
            other[k] = other[k] * inv[k]
            for i in range(k + 1, micro):
                raw[i] = raw[i] - low[i][k] * raw[k]
                solved[i] = solved[i] - low[i][k] * solved[k]
                other[i] = other[i] - low[i][k] * other[k]
        for j in range(micro):
            at = slice(8 * (start + j), 8 * (start + j) + 8)
            ups[at, :] = raw[j]
            rows[half, at, :] = solved[j]
            rows[1 - half, at, :] = other[j]
        for i in range(start + micro, panel):
            at = slice(8 * i, 8 * i + 8)
            x = jnp.where(inside, f32(0), rows[half, at, :])
            y = rows[1 - half, at, :]
            tx = ty = None
            for j in range(micro):
                c = lane_of(raw[j], base + i)
                tx = c * solved[j] if tx is None else tx + c * solved[j]
                ty = c * other[j] if ty is None else ty + c * other[j]
            rows[half, at, :] = x - tx
            rows[1 - half, at, :] = y - ty

def chol_body(s_ref, order_ref, basis_ref, factor_ref, mat, inv_ref, rows, ups, *, panel, micro):
    count, points, width = s_ref.shape
    row_id = lax.broadcasted_iota(jnp.int32, (width, width), 0)
    col_id = lax.broadcasted_iota(jnp.int32, (width, width), 1)
    for c in range(count):
        hi, lo = halves(s_ref[c])
        gram = contract(hi, hi, 0, 0)
        cross = contract(hi, lo, 0, 0)
        gram = gram + (cross + cross.T)
        shift = f32(0.01) * jnp.sum(jnp.where(row_id == col_id, gram, f32(0))) / f32(width) + f32(1e-5)
        mat[c] = gram + jnp.where(row_id == col_id, shift, f32(0))
    for first in range(0, width, panel):
        half = first // 128
        base = first % 128
        for c in range(count):
            for h in range(2):
                for t in range(0, panel, 8):
                    tile = mat[c, first + t:first + t + 8, 128 * h:128 * h + 128]
                    rows[h, pl.ds(8 * t + c, 8, stride=8), :] = tile
        factor_panel(rows, ups, first, panel, micro)
        prow = lax.broadcasted_iota(jnp.int32, (panel, 128), 0) + base
        pcol = lax.broadcasted_iota(jnp.int32, (panel, 128), 1)
        for c in range(count):
            z = [rows[h, pl.ds(c, panel, stride=8), :] for h in range(2)]
            u = ups[pl.ds(c, panel, stride=8), :]
            u = jnp.where(pcol >= prow, u, f32(0))
            wz = jnp.where((pcol <= prow) | (pcol >= base + panel), z[half], f32(0))
            w = jnp.where(pcol <= prow, z[half], f32(0))
            z[half] = wz
            factor_ref[c, first:first + panel, 128 * half:128 * half + 128] = u
            factor_ref[c, first:first + panel, 128 * (1 - half):128 * (1 - half) + 128] = z[1] if half == 0 else jnp.zeros_like(u)
            inv_ref[c, first:first + panel, 128 * half:128 * half + 128] = w
            inv_ref[c, first:first + panel, 128 * (1 - half):128 * (1 - half) + 128] = z[0] if half == 1 else jnp.zeros_like(u)
            rest = first + panel
            if rest < width:
                zz = jnp.concatenate(z, axis=1)
                hi, lo = halves(zz)
                left = jnp.concatenate([hi, hi, lo], axis=0)
                right = jnp.concatenate([hi, lo, hi], axis=0)
                off = (rest // 128) * 128
                prod = contract(left[:, off:], right, 0, 0)[rest - off:, :]
                old = mat[c, rest:, :]
                cc = col_id[rest:, :]
                old = jnp.where((cc >= first) & (cc < rest), f32(0), old)
                mat[c, rest:, :] = old - prod
    for c in range(count):
        hi, lo = halves(s_ref[c])
        wh, wl = halves(inv_ref[c])
        b = contract(jnp.concatenate([hi, hi, lo], axis=1), jnp.concatenate([wh, wl, wh], axis=1), 1, 1)
        b = b.astype(bf16)
        order = order_ref[c:c + 1, :].astype(f32)
        order_t = jnp.broadcast_to(order, (128, points)).T
        place = lax.broadcasted_iota(jnp.int32, (points, 128), 1).astype(f32)
        pick = jnp.concatenate([jnp.where(order_t == place + f32(128 * q), f32(1), f32(0)).astype(bf16) for q in range(points // 128)], axis=1)
        basis_ref[c] = jnp.dot(pick, b, preferred_element_type=f32).astype(bf16)

def chol_call(s, order, panel=64, micro=8, interpret=False):
    count, points, width = s.shape
    return pl.pallas_call(
        functools.partial(chol_body, panel=panel, micro=micro),
        out_shape=(jax.ShapeDtypeStruct((count, points, width), bf16), jax.ShapeDtypeStruct((count, width, width), f32)),
        scratch_shapes=[pltpu.VMEM((count, width, width), f32), pltpu.VMEM((count, width, width), f32),
            pltpu.VMEM((2, 8 * panel, 128), f32), pltpu.VMEM((8 * panel, 128), f32)],
        compiler_params=pltpu.CompilerParams(vmem_limit_bytes=48 * 2**20),
    )(s, order)


def active(first, pattern, cluster, column, distance, total):
    source = first + cluster + distance
    return (pattern != 0) & (source >= 0) & (source < total)


def blocks_body(cl_ref, co_ref, di_ref, first_ref, pattern_ref, prev_ref, own_ref, next_ref, out_ref, window, *, total):
    step = pl.program_id(0)
    count, _, points = own_ref.shape
    first = first_ref[0]

    @pl.when(step == 0)
    def _():
        window[...] = jnp.zeros_like(window)
        for slot in range(3 * count):
            ref = (prev_ref, own_ref, next_ref)[slot // count]
            index = (first + (slot - count)).astype(f32)
            xs = ref[slot % count]
            along = (xs[0:1] + index) - index
            window[slot, 0:1, :] = along
            window[slot, 1:3, :] = xs[1:3]

    cluster = cl_ref[step]
    column = co_ref[step]
    distance = di_ref[step]

    @pl.when(active(first, pattern_ref[cluster, column], cluster, column, distance, total))
    def _():
        squares = turn_squares(window[count + cluster], window[count + cluster + distance], distance)
        out_ref[0] = kernel_values(squares, points).astype(bf16)


def blocks_of(pairs, first, pattern, prev, own, after, total):
    count, _, points = own.shape
    table = offset_table(W)
    tabs = [jnp.asarray(np.array(x, np.int32)) for x in zip(*[(c, k, table[k]) for c, k in pairs])]
    whole = pl.BlockSpec(memory_space=pltpu.VMEM)
    return pl.pallas_call(
        functools.partial(blocks_body, total=total),
        grid_spec=pltpu.PrefetchScalarGridSpec(
            num_scalar_prefetch=5,
            grid=(len(pairs),),
            in_specs=[whole, whole, whole],
            out_specs=pl.BlockSpec((1, points, points), lambda i, *_: (i, 0, 0)),
            scratch_shapes=[pltpu.VMEM((3 * count, 8, points), f32)],
        ),
        out_shape=jax.ShapeDtypeStruct((len(pairs), points, points), bf16),
        compiler_params=pltpu.CompilerParams(vmem_limit_bytes=32 * 2**20),
        name="blocks",
    )(*tabs, first, pattern, prev, own, after)


def samples_body(first_ref, pattern_ref, k_ref, prev_ref, own_ref, next_ref, out_ref, *, total, count, table):
    cluster = pl.program_id(0)
    first = first_ref[0]
    for column, distance in enumerate(table):
        if column == 0:
            out_ref[...] = jnp.zeros_like(out_ref)

        @pl.when(active(first, pattern_ref[cluster, column], cluster, column, distance, total))
        def _():
            slot = cluster + distance

            def add(ref, index):
                out_ref[0] += jnp.dot(k_ref[column], ref[index], preferred_element_type=f32)

            @pl.when(slot < 0)
            def _():
                add(prev_ref, slot + count)

            @pl.when((slot >= 0) & (slot < count))
            def _():
                add(own_ref, slot)

            @pl.when(slot >= count)
            def _():
                add(next_ref, slot - count)


def samples_of(first, pattern, blocks, prev, own, after, total):
    count, points, width = own.shape
    table = offset_table(W)
    whole = pl.BlockSpec(memory_space=pltpu.VMEM)
    return pl.pallas_call(
        functools.partial(samples_body, total=total, count=count, table=table),
        grid_spec=pltpu.PrefetchScalarGridSpec(
            num_scalar_prefetch=2,
            grid=(count,),
            in_specs=[pl.BlockSpec((len(table), points, points), lambda c, *_: (c, 0, 0)), whole, whole, whole],
            out_specs=pl.BlockSpec((1, points, width), lambda c, *_: (c, 0, 0)),
        ),
        out_shape=jax.ShapeDtypeStruct((count, points, width), f32),
        compiler_params=pltpu.CompilerParams(vmem_limit_bytes=40 * 2**20),
        name="samples",
    )(first, pattern, blocks, prev, own, after)


def body(offsets, sketch, pattern, point_order):
    count = offsets.shape[0]
    total = count * lax.axis_size(AXES)
    first = (lax.axis_index(AXES) * count).astype(jnp.int32).reshape(1)
    prev_offsets = passed_along(offsets, 1)
    next_offsets = passed_along(offsets, -1)
    prev_sketch = passed_along(sketch, 1)
    next_sketch = passed_along(sketch, -1)
    pairs = [(c, k) for c in range(count) for k in range(len(offset_table(W)))]
    blocks = blocks_of(pairs, first, pattern, prev_offsets, offsets, next_offsets, total)
    samples = samples_of(first, pattern, blocks, prev_sketch, sketch, next_sketch, total)
    return chol_call(samples, point_order)


def solution(mesh):
    rows = P(AXES, None, None)
    flat = P(AXES, None)
    return jax.shard_map(
        body,
        mesh=mesh,
        in_specs=(rows, rows, flat, flat),
        out_specs=(rows, rows),
        check_vma=False,
    )
```

```python
import functools
import math

import jax
import jax.numpy as jnp
from jax import lax
from jax.experimental import pallas as pl
from jax.experimental.pallas import tpu as pltpu
from jax.sharding import PartitionSpec as P

W = 4
AXES = ("grp", "dev")
f32 = jnp.float32
bf16 = jnp.bfloat16

wave_number = 40.0
decay_length = 4.0
softening = 0.5
turns = wave_number / (2.0 * math.pi)

SINE = (4.44288292, -7.30824569, 3.60635423, -0.84611167, 0.10982452)


def passed_along(array, by):
    peers = lax.axis_size(AXES)
    pairs = [(i, i + by) for i in range(peers) if 0 <= i + by < peers]
    return lax.ppermute(array, AXES, pairs)


def offset_table(reach):
    return [-value for value in range(reach, 1, -1)] + list(range(2, reach + 1))


def kernel_values(turn_squared, points):
    turn = turn_squared * lax.rsqrt(turn_squared)
    part = turn - jnp.round(turn)
    square = part * part
    sine = f32(SINE[-1])
    for value in SINE[-2::-1]:
        sine = sine * square + f32(value)
    sine = sine * part
    decay = jnp.exp2(
        turn * f32(-math.log2(math.e) / (decay_length * turns)) + f32(math.log2(turns / math.sqrt(points)))
    )
    level = decay * pltpu.reciprocal(turn + f32(softening * turns), approx=True)
    return level - level * (sine * sine)


def pieces(x):
    high = x.astype(bf16).astype(f32)
    middle = (x - high).astype(bf16).astype(f32)
    low = (x - high - middle).astype(bf16).astype(f32)
    return high, middle, low


def turn_squares(target, source, distance):
    row = lax.broadcasted_iota(jnp.int32, target.shape, 0)
    half = distance.astype(f32) * f32(0.5)

    def shifted(x, along):
        moved = x + jnp.where(row == 0, along, jnp.where(row < 3, f32(-0.5), f32(0)))
        moved = moved * f32(turns)
        return moved, jnp.sum(moved * moved, axis=0, keepdims=True)

    left, left_norm = shifted(target, -half - f32(0.5))
    right, right_norm = shifted(source, half - f32(0.5))
    left = jnp.where(row == 3, left_norm, jnp.where(row == 4, f32(1), left))
    right = jnp.where(row == 4, right_norm, jnp.where(row == 3, f32(1), f32(-2) * right))
    lh, lm, ll = pieces(left)
    rh, rm, rl = pieces(right)
    a = jnp.concatenate([lh, lh, lm, lm, lh, ll, lm, ll], axis=0).astype(bf16)
    b = jnp.concatenate([rh, rm, rh, rm, rl, rh, rl, rm], axis=0).astype(bf16)
    return contract(a, b, 0, 0)


def halves(x):
    hi = x.astype(bf16)
    return hi, (x - hi.astype(f32)).astype(bf16)

def contract(a, b, da, db):
    return lax.dot_general(a, b, (((da,), (db,)), ((), ())), preferred_element_type=f32)

def lane_of(x, lane):
    return jnp.broadcast_to(x[:, lane:lane + 1], x.shape)

def factor_panel(rows, ups, first, panel, micro):
    half = first // 128
    base = first % 128
    lanes = lax.broadcasted_iota(jnp.int32, (8, 128), 1)
    for start in range(0, panel, micro):
        lane0 = base + start
        inside = (lanes >= lane0) & (lanes < lane0 + micro)
        raw = [rows[half, 8 * (start + j):8 * (start + j) + 8, :] for j in range(micro)]
        other = [rows[1 - half, 8 * (start + j):8 * (start + j) + 8, :] for j in range(micro)]
        a = [[lane_of(raw[i], lane0 + k) for k in range(i + 1)] for i in range(micro)]
        low = [[None] * micro for _ in range(micro)]
        inv = [None] * micro
        for k in range(micro):
            inv[k] = lax.rsqrt(a[k][k])
            for i in range(k + 1, micro):
                low[i][k] = a[i][k] * inv[k]
            for i in range(k + 1, micro):
                for m in range(k + 1, i + 1):
                    a[i][m] = a[i][m] - low[i][k] * low[m][k]
        solved = [jnp.where(inside, jnp.where(lanes == lane0 + j, f32(1), f32(0)), raw[j]) for j in range(micro)]
        for k in range(micro):
            raw[k] = raw[k] * inv[k]
            solved[k] = solved[k] * inv[k]
            other[k] = other[k] * inv[k]
            for i in range(k + 1, micro):
                raw[i] = raw[i] - low[i][k] * raw[k]
                solved[i] = solved[i] - low[i][k] * solved[k]
                other[i] = other[i] - low[i][k] * other[k]
        for j in range(micro):
            at = slice(8 * (start + j), 8 * (start + j) + 8)
            ups[at, :] = raw[j]
            rows[half, at, :] = solved[j]
            rows[1 - half, at, :] = other[j]
        for i in range(start + micro, panel):
            at = slice(8 * i, 8 * i + 8)
            x = jnp.where(inside, f32(0), rows[half, at, :])
            y = rows[1 - half, at, :]
            tx = ty = None
            for j in range(micro):
                c = lane_of(raw[j], base + i)
                tx = c * solved[j] if tx is None else tx + c * solved[j]
                ty = c * other[j] if ty is None else ty + c * other[j]
            rows[half, at, :] = x - tx
            rows[1 - half, at, :] = y - ty

def finish_body(k_ref, prev_ref, own_ref, next_ref, order_ref, basis_ref, factor_ref, s_ref, mat, inv_ref, rows, ups, *, panel, micro):
    count, points, width = s_ref.shape
    row_id = lax.broadcasted_iota(jnp.int32, (width, width), 0)
    col_id = lax.broadcasted_iota(jnp.int32, (width, width), 1)
    refs = (prev_ref, own_ref, next_ref)
    for c in range(count):
        samples = None
        for column, distance in enumerate(offset_table(W)):
            slot = c + count + distance
            term = jnp.dot(
                k_ref[c, :, column * points:(column + 1) * points],
                refs[slot // count][slot % count],
                preferred_element_type=f32,
            )
            samples = term if samples is None else samples + term
        s_ref[c] = samples
        hi, lo = halves(samples)
        gram = contract(hi, hi, 0, 0)
        cross = contract(hi, lo, 0, 0)
        gram = gram + (cross + cross.T)
        shift = f32(0.01) * jnp.sum(jnp.where(row_id == col_id, gram, f32(0))) / f32(width) + f32(1e-5)
        mat[c] = gram + jnp.where(row_id == col_id, shift, f32(0))
    for first in range(0, width, panel):
        half = first // 128
        base = first % 128
        for c in range(count):
            for h in range(2):
                for t in range(0, panel, 8):
                    tile = mat[c, first + t:first + t + 8, 128 * h:128 * h + 128]
                    rows[h, pl.ds(8 * t + c, 8, stride=8), :] = tile
        factor_panel(rows, ups, first, panel, micro)
        prow = lax.broadcasted_iota(jnp.int32, (panel, 128), 0) + base
        pcol = lax.broadcasted_iota(jnp.int32, (panel, 128), 1)
        for c in range(count):
            z = [rows[h, pl.ds(c, panel, stride=8), :] for h in range(2)]
            u = ups[pl.ds(c, panel, stride=8), :]
            u = jnp.where(pcol >= prow, u, f32(0))
            wz = jnp.where((pcol <= prow) | (pcol >= base + panel), z[half], f32(0))
            w = jnp.where(pcol <= prow, z[half], f32(0))
            z[half] = wz
            factor_ref[c, first:first + panel, 128 * half:128 * half + 128] = u
            factor_ref[c, first:first + panel, 128 * (1 - half):128 * (1 - half) + 128] = z[1] if half == 0 else jnp.zeros_like(u)
            inv_ref[c, first:first + panel, 128 * half:128 * half + 128] = w
            inv_ref[c, first:first + panel, 128 * (1 - half):128 * (1 - half) + 128] = z[0] if half == 1 else jnp.zeros_like(u)
            rest = first + panel
            if rest < width:
                zz = jnp.concatenate(z, axis=1)
                hi, lo = halves(zz)
                left = jnp.concatenate([hi, hi, lo], axis=0)
                right = jnp.concatenate([hi, lo, hi], axis=0)
                off = (rest // 128) * 128
                prod = contract(left[:, off:], right, 0, 0)[rest - off:, :]
                old = mat[c, rest:, :]
                cc = col_id[rest:, :]
                old = jnp.where((cc >= first) & (cc < rest), f32(0), old)
                mat[c, rest:, :] = old - prod
    for c in range(count):
        hi, lo = halves(s_ref[c])
        wh, wl = halves(inv_ref[c])
        b = contract(jnp.concatenate([hi, hi, lo], axis=1), jnp.concatenate([wh, wl, wh], axis=1), 1, 1)
        b = b.astype(bf16)
        order = order_ref[c:c + 1, :].astype(f32)
        order_t = jnp.broadcast_to(order, (128, points)).T
        place = lax.broadcasted_iota(jnp.int32, (points, 128), 1).astype(f32)
        pick = jnp.concatenate([jnp.where(order_t == place + f32(128 * q), f32(1), f32(0)).astype(bf16) for q in range(points // 128)], axis=1)
        basis_ref[c] = jnp.dot(pick, b, preferred_element_type=f32).astype(bf16)

def finish(blocks, prev, own, after, order, panel=64, micro=8):
    count, points, width = own.shape
    whole = pl.BlockSpec(memory_space=pltpu.VMEM)
    return pl.pallas_call(
        functools.partial(finish_body, panel=panel, micro=micro),
        in_specs=[whole] * 5,
        out_shape=(
            jax.ShapeDtypeStruct((count, points, width), bf16),
            jax.ShapeDtypeStruct((count, width, width), f32),
        ),
        scratch_shapes=[
            pltpu.VMEM((count, points, width), f32),
            pltpu.VMEM((count, width, width), f32),
            pltpu.VMEM((count, width, width), f32),
            pltpu.VMEM((2, 8 * panel, 128), f32),
            pltpu.VMEM((8 * panel, 128), f32),
        ],
        compiler_params=pltpu.CompilerParams(vmem_limit_bytes=28 * 2**20),
        name="finish",
    )(*(pltpu.with_memory_space_constraint(x, pltpu.VMEM) for x in (blocks, prev, own, after)), order)


def active(first, pattern, cluster, distance, total):
    source = first + cluster + distance
    return (pattern != 0) & (source >= 0) & (source < total)


def blocks_body(pattern_ref, prev_ref, own_ref, next_ref, out_ref, window, *, total):
    cluster, column = pl.program_id(0), pl.program_id(1)
    count, points = own_ref.shape[1:]
    first = lax.axis_index(AXES) * count

    @pl.when((cluster == 0) & (column == 0))
    def _():
        window[...] = jnp.zeros_like(window)
        for slot in range(3 * count):
            ref = (prev_ref, own_ref, next_ref)[slot // count]
            index = (first + (slot - count)).astype(f32)
            at = slot % count
            window[slot, 0:1, :] = (ref[0, at:at + 1, :] + index) - index
            window[slot, 1:2, :] = ref[1, at:at + 1, :]
            window[slot, 2:3, :] = ref[2, at:at + 1, :]

    distance = column - W + jnp.where(column >= W - 1, 3, 0)
    counted = active(first, pattern_ref[cluster, column], cluster, distance, total)

    @pl.when(counted)
    def _():
        squares = turn_squares(window[count + cluster], window[count + cluster + distance], distance)
        out_ref[0] = kernel_values(squares, points).astype(bf16)

    @pl.when(jnp.logical_not(counted))
    def _():
        out_ref[...] = jnp.zeros_like(out_ref)


def blocks_of(pattern, prev, own, after, total):
    count, points = own.shape[1:]
    columns = pattern.shape[1]
    values = count * columns * points * points
    whole = pl.BlockSpec(memory_space=pltpu.VMEM)
    return pl.pallas_call(
        functools.partial(blocks_body, total=total),
        grid=(count, columns),
        in_specs=[pl.BlockSpec(memory_space=pltpu.SMEM), whole, whole, whole],
        out_specs=pl.BlockSpec((1, points, points), lambda c, k: (c, 0, k)),
        scratch_shapes=[pltpu.VMEM((3 * count, 8, points), f32)],
        out_shape=pltpu.VMEM((count, points, columns * points), bf16),
        cost_estimate=pl.CostEstimate(flops=40 * values, bytes_accessed=2 * values, transcendentals=3 * values),
        compiler_params=pltpu.CompilerParams(vmem_limit_bytes=16 * 2**20),
        name="blocks",
    )(pattern, prev, own, after)


def body(offsets, sketch, pattern, point_order):
    count = offsets.shape[0]
    total = count * lax.axis_size(AXES)
    offsets = offsets.transpose(1, 0, 2)
    prev_offsets = passed_along(offsets, 1)
    next_offsets = passed_along(offsets, -1)
    upward, prev_offsets = lax.optimization_barrier((sketch, prev_offsets))
    downward, next_offsets = lax.optimization_barrier((sketch, next_offsets))
    prev_sketch = passed_along(upward, 1)
    next_sketch = passed_along(downward, -1)
    blocks = blocks_of(pattern, prev_offsets, offsets, next_offsets, total)
    return finish(blocks, prev_sketch, sketch, next_sketch, point_order)


def solution(mesh):
    rows = P(AXES, None, None)
    flat = P(AXES, None)
    return jax.shard_map(
        body,
        mesh=mesh,
        in_specs=(rows, rows, flat, flat),
        out_specs=(rows, rows),
        check_vma=False,
    )
```

```python
import functools
import math

import jax
import jax.numpy as jnp
from jax import lax
from jax.experimental import pallas as pl
from jax.experimental.pallas import tpu as pltpu
from jax.sharding import PartitionSpec as P

W = 4
AXES = ("grp", "dev")
f32 = jnp.float32
bf16 = jnp.bfloat16

wave_number = 40.0
decay_length = 4.0
softening = 0.5
turns = wave_number / (2.0 * math.pi)

SINE = (4.44288292, -7.30824569, 3.60635423, -0.84611167, 0.10982452)


def exchanged(array, start):
    peers = lax.axis_size(AXES)
    pairs = [(i, i + 1) for i in range(start, peers - 1, 2)]
    return lax.ppermute(array, AXES, pairs + [(j, i) for i, j in pairs])


def offset_table(reach):
    return [-value for value in range(reach, 1, -1)] + list(range(2, reach + 1))


def kernel_values(turn_squared, points):
    turn = turn_squared * lax.rsqrt(turn_squared)
    part = turn - jnp.round(turn)
    square = part * part
    sine = f32(SINE[-1])
    for value in SINE[-2::-1]:
        sine = sine * square + f32(value)
    sine = sine * part
    decay = jnp.exp2(
        turn * f32(-math.log2(math.e) / (decay_length * turns)) + f32(math.log2(turns / math.sqrt(points)))
    )
    level = decay * pltpu.reciprocal(turn + f32(softening * turns), approx=True)
    return level - level * (sine * sine)


def pieces(x):
    high = x.astype(bf16).astype(f32)
    middle = (x - high).astype(bf16).astype(f32)
    low = (x - high - middle).astype(bf16).astype(f32)
    return high, middle, low


def turn_squares(target, source, distance):
    row = lax.broadcasted_iota(jnp.int32, target.shape, 0)
    half = distance.astype(f32) * f32(0.5)

    def shifted(x, along):
        moved = x + jnp.where(row == 0, along, jnp.where(row < 3, f32(-0.5), f32(0)))
        moved = moved * f32(turns)
        return moved, jnp.sum(moved * moved, axis=0, keepdims=True)

    left, left_norm = shifted(target, -half - f32(0.5))
    right, right_norm = shifted(source, half - f32(0.5))
    left = jnp.where(row == 3, left_norm, jnp.where(row == 4, f32(1), left))
    right = jnp.where(row == 4, right_norm, jnp.where(row == 3, f32(1), f32(-2) * right))
    lh, lm, ll = pieces(left)
    rh, rm, rl = pieces(right)
    a = jnp.concatenate([lh, lh, lm, lm, lh, ll, lm, ll], axis=0).astype(bf16)
    b = jnp.concatenate([rh, rm, rh, rm, rl, rh, rl, rm], axis=0).astype(bf16)
    return contract(a, b, 0, 0)


def halves(x):
    hi = x.astype(bf16)
    return hi, (x - hi.astype(f32)).astype(bf16)

def contract(a, b, da, db):
    return lax.dot_general(a, b, (((da,), (db,)), ((), ())), preferred_element_type=f32)

def lane_of(x, lane):
    return jnp.broadcast_to(x[:, lane:lane + 1], x.shape)

def factor_panel(rows, ups, first, panel, micro):
    half = first // 128
    base = first % 128
    lanes = lax.broadcasted_iota(jnp.int32, (8, 128), 1)
    for start in range(0, panel, micro):
        lane0 = base + start
        inside = (lanes >= lane0) & (lanes < lane0 + micro)
        raw = [rows[half, 8 * (start + j):8 * (start + j) + 8, :] for j in range(micro)]
        other = [rows[1 - half, 8 * (start + j):8 * (start + j) + 8, :] for j in range(micro)]
        a = [[lane_of(raw[i], lane0 + k) for k in range(i + 1)] for i in range(micro)]
        low = [[None] * micro for _ in range(micro)]
        inv = [None] * micro
        for k in range(micro):
            inv[k] = lax.rsqrt(a[k][k])
            for i in range(k + 1, micro):
                low[i][k] = a[i][k] * inv[k]
            for i in range(k + 1, micro):
                for m in range(k + 1, i + 1):
                    a[i][m] = a[i][m] - low[i][k] * low[m][k]
        solved = [jnp.where(inside, jnp.where(lanes == lane0 + j, f32(1), f32(0)), raw[j]) for j in range(micro)]
        for k in range(micro):
            raw[k] = raw[k] * inv[k]
            solved[k] = solved[k] * inv[k]
            other[k] = other[k] * inv[k]
            for i in range(k + 1, micro):
                raw[i] = raw[i] - low[i][k] * raw[k]
                solved[i] = solved[i] - low[i][k] * solved[k]
                other[i] = other[i] - low[i][k] * other[k]
        for j in range(micro):
            at = slice(8 * (start + j), 8 * (start + j) + 8)
            ups[at, :] = raw[j]
            rows[half, at, :] = solved[j]
            rows[1 - half, at, :] = other[j]
        for i in range(start + micro, panel):
            at = slice(8 * i, 8 * i + 8)
            x = jnp.where(inside, f32(0), rows[half, at, :])
            y = rows[1 - half, at, :]
            tx = ty = None
            for j in range(micro):
                c = lane_of(raw[j], base + i)
                tx = c * solved[j] if tx is None else tx + c * solved[j]
                ty = c * other[j] if ty is None else ty + c * other[j]
            rows[half, at, :] = x - tx
            rows[1 - half, at, :] = y - ty

def finish_body(k_ref, even_ref, own_ref, odd_ref, order_ref, basis_ref, factor_ref, s_ref, mat, inv_ref, rows, ups, *, panel, micro):
    count, points, width = s_ref.shape
    row_id = lax.broadcasted_iota(jnp.int32, (width, width), 0)
    col_id = lax.broadcasted_iota(jnp.int32, (width, width), 1)

    def fill(refs):
        for c in range(count):
            samples = None
            for column, distance in enumerate(offset_table(W)):
                slot = c + count + distance
                term = jnp.dot(
                    k_ref[c, :, column * points:(column + 1) * points],
                    refs[slot // count][slot % count],
                    preferred_element_type=f32,
                )
                samples = term if samples is None else samples + term
            s_ref[c] = samples

    side = lax.rem(lax.axis_index(AXES), 2)
    pl.when(side == 1)(lambda: fill((even_ref, own_ref, odd_ref)))
    pl.when(side == 0)(lambda: fill((odd_ref, own_ref, even_ref)))
    for c in range(count):
        samples = s_ref[c]
        hi, lo = halves(samples)
        gram = contract(hi, hi, 0, 0)
        cross = contract(hi, lo, 0, 0)
        gram = gram + (cross + cross.T)
        shift = f32(0.01) * jnp.sum(jnp.where(row_id == col_id, gram, f32(0))) / f32(width) + f32(1e-5)
        mat[c] = gram + jnp.where(row_id == col_id, shift, f32(0))
    for first in range(0, width, panel):
        half = first // 128
        base = first % 128
        for c in range(count):
            for h in range(2):
                for t in range(0, panel, 8):
                    tile = mat[c, first + t:first + t + 8, 128 * h:128 * h + 128]
                    rows[h, pl.ds(8 * t + c, 8, stride=8), :] = tile
        factor_panel(rows, ups, first, panel, micro)
        prow = lax.broadcasted_iota(jnp.int32, (panel, 128), 0) + base
        pcol = lax.broadcasted_iota(jnp.int32, (panel, 128), 1)
        for c in range(count):
            z = [rows[h, pl.ds(c, panel, stride=8), :] for h in range(2)]
            u = ups[pl.ds(c, panel, stride=8), :]
            u = jnp.where(pcol >= prow, u, f32(0))
            wz = jnp.where((pcol <= prow) | (pcol >= base + panel), z[half], f32(0))
            w = jnp.where(pcol <= prow, z[half], f32(0))
            z[half] = wz
            factor_ref[c, first:first + panel, 128 * half:128 * half + 128] = u
            factor_ref[c, first:first + panel, 128 * (1 - half):128 * (1 - half) + 128] = z[1] if half == 0 else jnp.zeros_like(u)
            inv_ref[c, first:first + panel, 128 * half:128 * half + 128] = w
            inv_ref[c, first:first + panel, 128 * (1 - half):128 * (1 - half) + 128] = z[0] if half == 1 else jnp.zeros_like(u)
            rest = first + panel
            if rest < width:
                zz = jnp.concatenate(z, axis=1)
                hi, lo = halves(zz)
                left = jnp.concatenate([hi, hi, lo], axis=0)
                right = jnp.concatenate([hi, lo, hi], axis=0)
                off = (rest // 128) * 128
                prod = contract(left[:, off:], right, 0, 0)[rest - off:, :]
                old = mat[c, rest:, :]
                cc = col_id[rest:, :]
                old = jnp.where((cc >= first) & (cc < rest), f32(0), old)
                mat[c, rest:, :] = old - prod
    for c in range(count):
        hi, lo = halves(s_ref[c])
        wh, wl = halves(inv_ref[c])
        b = contract(jnp.concatenate([hi, hi, lo], axis=1), jnp.concatenate([wh, wl, wh], axis=1), 1, 1)
        b = b.astype(bf16)
        order = order_ref[c:c + 1, :].astype(f32)
        order_t = jnp.broadcast_to(order, (128, points)).T
        place = lax.broadcasted_iota(jnp.int32, (points, 128), 1).astype(f32)
        pick = jnp.concatenate([jnp.where(order_t == place + f32(128 * q), f32(1), f32(0)).astype(bf16) for q in range(points // 128)], axis=1)
        basis_ref[c] = jnp.dot(pick, b, preferred_element_type=f32).astype(bf16)

def finish(blocks, even, own, odd, order, panel=64, micro=8):
    count, points, width = own.shape
    whole = pl.BlockSpec(memory_space=pltpu.VMEM)
    return pl.pallas_call(
        functools.partial(finish_body, panel=panel, micro=micro),
        in_specs=[whole] * 5,
        out_shape=(
            jax.ShapeDtypeStruct((count, points, width), bf16),
            jax.ShapeDtypeStruct((count, width, width), f32),
        ),
        scratch_shapes=[
            pltpu.VMEM((count, points, width), f32),
            pltpu.VMEM((count, width, width), f32),
            pltpu.VMEM((count, width, width), f32),
            pltpu.VMEM((2, 8 * panel, 128), f32),
            pltpu.VMEM((8 * panel, 128), f32),
        ],
        compiler_params=pltpu.CompilerParams(vmem_limit_bytes=28 * 2**20),
        name="finish",
    )(*(pltpu.with_memory_space_constraint(x, pltpu.VMEM) for x in (blocks, even, own, odd)), order)


def active(first, pattern, cluster, distance, total):
    source = first + cluster + distance
    return (pattern != 0) & (source >= 0) & (source < total)


def blocks_body(pattern_ref, even_ref, own_ref, odd_ref, out_ref, window, *, total):
    cluster, column = pl.program_id(0), pl.program_id(1)
    count, points = own_ref.shape[1:]
    me = lax.axis_index(AXES)
    first = me * count
    side = lax.rem(me, 2)

    @pl.when((cluster == 0) & (column == 0))
    def _():
        window[...] = jnp.zeros_like(window)
        for group, ref in ((2 - 2 * side, even_ref), (1, own_ref), (2 * side, odd_ref)):
            for at in range(count):
                slot = group * count + at
                index = (first + (slot - count)).astype(f32)
                window[slot, 0:1, :] = (ref[0, at:at + 1, :] + index) - index
                window[slot, 1:2, :] = ref[1, at:at + 1, :]
                window[slot, 2:3, :] = ref[2, at:at + 1, :]

    distance = column - W + jnp.where(column >= W - 1, 3, 0)
    counted = active(first, pattern_ref[cluster, column], cluster, distance, total)

    @pl.when(counted)
    def _():
        squares = turn_squares(window[count + cluster], window[count + cluster + distance], distance)
        out_ref[0] = kernel_values(squares, points).astype(bf16)

    @pl.when(jnp.logical_not(counted))
    def _():
        out_ref[...] = jnp.zeros_like(out_ref)


def blocks_of(pattern, even, own, odd, total):
    count, points = own.shape[1:]
    columns = pattern.shape[1]
    values = count * columns * points * points
    whole = pl.BlockSpec(memory_space=pltpu.VMEM)
    return pl.pallas_call(
        functools.partial(blocks_body, total=total),
        grid=(count, columns),
        in_specs=[pl.BlockSpec(memory_space=pltpu.SMEM), whole, whole, whole],
        out_specs=pl.BlockSpec((1, points, points), lambda c, k: (c, 0, k)),
        scratch_shapes=[pltpu.VMEM((3 * count, 8, points), f32)],
        out_shape=pltpu.VMEM((count, points, columns * points), bf16),
        cost_estimate=pl.CostEstimate(flops=40 * values, bytes_accessed=2 * values, transcendentals=3 * values),
        compiler_params=pltpu.CompilerParams(vmem_limit_bytes=16 * 2**20),
        name="blocks",
    )(pattern, even, own, odd)


def body(offsets, sketch, pattern, point_order):
    count = offsets.shape[0]
    total = count * lax.axis_size(AXES)
    offsets = offsets.transpose(1, 0, 2)
    odd_offsets = exchanged(offsets, 1)
    sent, odd_offsets = lax.optimization_barrier((sketch, odd_offsets))
    odd_sketch = exchanged(sent, 1)
    even_offsets = exchanged(offsets, 0)
    even_sketch = exchanged(sketch, 0)
    blocks = blocks_of(pattern, even_offsets, offsets, odd_offsets, total)
    return finish(blocks, even_sketch, sketch, odd_sketch, point_order)


def solution(mesh):
    rows = P(AXES, None, None)
    flat = P(AXES, None)
    return jax.shard_map(
        body,
        mesh=mesh,
        in_specs=(rows, rows, flat, flat),
        out_specs=(rows, rows),
        check_vma=False,
    )
```

```python
import functools
import math

import jax
import jax.numpy as jnp
from jax import lax
from jax.experimental import pallas as pl
from jax.experimental.pallas import tpu as pltpu
from jax.sharding import PartitionSpec as P

W = 4
AXES = ("grp", "dev")
f32 = jnp.float32
bf16 = jnp.bfloat16

wave_number = 40.0
decay_length = 4.0
softening = 0.5
turns = wave_number / (2.0 * math.pi)

SINE = (4.44288292, -7.30824569, 3.60635423, -0.84611167, 0.10982452)


def exchanged(array, start):
    peers = lax.axis_size(AXES)
    pairs = [(i, i + 1) for i in range(start, peers - 1, 2)]
    return lax.ppermute(array, AXES, pairs + [(j, i) for i, j in pairs])


def offset_table(reach):
    return [-value for value in range(reach, 1, -1)] + list(range(2, reach + 1))


def kernel_values(turn_squared, points):
    turn = turn_squared * lax.rsqrt(turn_squared)
    part = turn - jnp.round(turn)
    square = part * part
    sine = f32(SINE[-1])
    for value in SINE[-2::-1]:
        sine = sine * square + f32(value)
    sine = sine * part
    decay = jnp.exp2(
        turn * f32(-math.log2(math.e) / (decay_length * turns)) + f32(math.log2(turns / math.sqrt(points)))
    )
    level = decay * pltpu.reciprocal(turn + f32(softening * turns), approx=True)
    return level - level * (sine * sine)


def pieces(x):
    high = x.astype(bf16).astype(f32)
    middle = (x - high).astype(bf16).astype(f32)
    low = (x - high - middle).astype(bf16).astype(f32)
    return high, middle, low


def split_points(target, source, distance):
    row = lax.broadcasted_iota(jnp.int32, target.shape, 0)
    half = distance.astype(f32) * f32(0.5)

    def shifted(x, along):
        moved = x + jnp.where(row == 0, along, jnp.where(row < 3, f32(-0.5), f32(0)))
        moved = moved * f32(turns)
        return moved, jnp.sum(moved * moved, axis=0, keepdims=True)

    left, left_norm = shifted(target, -half - f32(0.5))
    right, right_norm = shifted(source, half - f32(0.5))
    left = jnp.where(row == 3, left_norm, jnp.where(row == 4, f32(1), left))
    right = jnp.where(row == 4, right_norm, jnp.where(row == 3, f32(1), f32(-2) * right))
    lh, lm, ll = pieces(left)
    rh, rm, rl = pieces(right)
    a = jnp.concatenate([lh, lh, lm, lm, lh, ll, lm, ll], axis=0).astype(bf16)
    b = jnp.concatenate([rh, rm, rh, rm, rl, rh, rl, rm], axis=0).astype(bf16)
    return a, b


def halves(x):
    hi = x.astype(bf16)
    return hi, (x - hi.astype(f32)).astype(bf16)

def contract(a, b, da, db):
    return lax.dot_general(a, b, (((da,), (db,)), ((), ())), preferred_element_type=f32)

def lane_of(x, lane):
    return jnp.broadcast_to(x[:, lane:lane + 1], x.shape)

def factor_panel(rows, ups, first, panel, micro):
    half = first // 128
    base = first % 128
    lanes = lax.broadcasted_iota(jnp.int32, (8, 128), 1)
    for start in range(0, panel, micro):
        lane0 = base + start
        inside = (lanes >= lane0) & (lanes < lane0 + micro)
        raw = [rows[half, 8 * (start + j):8 * (start + j) + 8, :] for j in range(micro)]
        other = [rows[1 - half, 8 * (start + j):8 * (start + j) + 8, :] for j in range(micro)]
        a = [[lane_of(raw[i], lane0 + k) for k in range(i + 1)] for i in range(micro)]
        low = [[None] * micro for _ in range(micro)]
        inv = [None] * micro
        for k in range(micro):
            inv[k] = lax.rsqrt(a[k][k])
            for i in range(k + 1, micro):
                low[i][k] = a[i][k] * inv[k]
            for i in range(k + 1, micro):
                for m in range(k + 1, i + 1):
                    a[i][m] = a[i][m] - low[i][k] * low[m][k]
        solved = [jnp.where(inside, jnp.where(lanes == lane0 + j, f32(1), f32(0)), raw[j]) for j in range(micro)]
        for k in range(micro):
            raw[k] = raw[k] * inv[k]
            solved[k] = solved[k] * inv[k]
            other[k] = other[k] * inv[k]
            for i in range(k + 1, micro):
                raw[i] = raw[i] - low[i][k] * raw[k]
                solved[i] = solved[i] - low[i][k] * solved[k]
                other[i] = other[i] - low[i][k] * other[k]
        for j in range(micro):
            at = slice(8 * (start + j), 8 * (start + j) + 8)
            ups[at, :] = raw[j]
            rows[half, at, :] = solved[j]
            rows[1 - half, at, :] = other[j]
        for i in range(start + micro, panel):
            at = slice(8 * i, 8 * i + 8)
            x = jnp.where(inside, f32(0), rows[half, at, :])
            y = rows[1 - half, at, :]
            tx = ty = None
            for j in range(micro):
                c = lane_of(raw[j], base + i)
                tx = c * solved[j] if tx is None else tx + c * solved[j]
                ty = c * other[j] if ty is None else ty + c * other[j]
            rows[half, at, :] = x - tx
            rows[1 - half, at, :] = y - ty

def finish_body(k_ref, even_ref, own_ref, odd_ref, order_ref, basis_ref, factor_ref, t_ref, mat, inv_ref, rows, ups, *, panel, micro):
    count, width, points = own_ref.shape
    row_id = lax.broadcasted_iota(jnp.int32, (width, width), 0)
    col_id = lax.broadcasted_iota(jnp.int32, (width, width), 1)

    def fill(refs):
        for c in range(count):
            samples = None
            for column, distance in enumerate(offset_table(W)):
                slot = c + count + distance
                block = k_ref[len(offset_table(W)) * c + column]
                term = jnp.dot(refs[slot // count][slot % count], block, preferred_element_type=f32)
                samples = term if samples is None else samples + term
            t_ref[c] = samples

    side = lax.rem(lax.axis_index(AXES), 2)
    pl.when(side == 1)(lambda: fill((even_ref, own_ref, odd_ref)))
    pl.when(side == 0)(lambda: fill((odd_ref, own_ref, even_ref)))
    for c in range(count):
        hi, lo = halves(t_ref[c])
        gram = contract(jnp.concatenate([hi, hi, lo], axis=1), jnp.concatenate([hi, lo, hi], axis=1), 1, 1)
        shift = f32(0.01) * jnp.sum(jnp.where(row_id == col_id, gram, f32(0))) / f32(width) + f32(1e-5)
        mat[c] = gram + jnp.where(row_id == col_id, shift, f32(0))
    for first in range(0, width, panel):
        half = first // 128
        base = first % 128
        for c in range(count):
            for h in range(2):
                for t in range(0, panel, 8):
                    tile = mat[c, first + t:first + t + 8, 128 * h:128 * h + 128]
                    rows[h, pl.ds(8 * t + c, 8, stride=8), :] = tile
        factor_panel(rows, ups, first, panel, micro)
        prow = lax.broadcasted_iota(jnp.int32, (panel, 128), 0) + base
        pcol = lax.broadcasted_iota(jnp.int32, (panel, 128), 1)
        for c in range(count):
            z = [rows[h, pl.ds(c, panel, stride=8), :] for h in range(2)]
            u = ups[pl.ds(c, panel, stride=8), :]
            u = jnp.where(pcol >= prow, u, f32(0))
            wz = jnp.where((pcol <= prow) | (pcol >= base + panel), z[half], f32(0))
            w = jnp.where(pcol <= prow, z[half], f32(0))
            z[half] = wz
            factor_ref[c, first:first + panel, 128 * half:128 * half + 128] = u
            factor_ref[c, first:first + panel, 128 * (1 - half):128 * (1 - half) + 128] = z[1] if half == 0 else jnp.zeros_like(u)
            inv_ref[c, first:first + panel, 128 * half:128 * half + 128] = w
            inv_ref[c, first:first + panel, 128 * (1 - half):128 * (1 - half) + 128] = z[0] if half == 1 else jnp.zeros_like(u)
            rest = first + panel
            if rest < width:
                zz = jnp.concatenate(z, axis=1)
                hi, lo = halves(zz)
                left = jnp.concatenate([hi, hi, lo], axis=0)
                right = jnp.concatenate([hi, lo, hi], axis=0)
                off = (rest // 128) * 128
                prod = contract(left[:, off:], right, 0, 0)[rest - off:, :]
                old = mat[c, rest:, :]
                cc = col_id[rest:, :]
                old = jnp.where((cc >= first) & (cc < rest), f32(0), old)
                mat[c, rest:, :] = old - prod
    for c in range(count):
        hi, lo = halves(t_ref[c])
        wh, wl = halves(inv_ref[c])
        b = jnp.dot(jnp.concatenate([wh, wh, wl], axis=1), jnp.concatenate([hi, lo, hi], axis=0), preferred_element_type=f32).astype(bf16)
        order_t = jnp.broadcast_to(order_ref[c:c + 1, :].astype(f32), (128, points)).T
        place = lax.broadcasted_iota(jnp.int32, (points, 128), 1).astype(f32)
        pick = jnp.concatenate([jnp.where(order_t == place + f32(128 * q), f32(1), f32(0)).astype(bf16) for q in range(points // 128)], axis=1)
        basis_ref[c] = contract(pick, b, 1, 1).astype(bf16)

def finish(blocks, even, own, odd, order, panel=16, micro=8):
    count, width, points = own.shape
    whole = pl.BlockSpec(memory_space=pltpu.VMEM)
    return pl.pallas_call(
        functools.partial(finish_body, panel=panel, micro=micro),
        in_specs=[whole] * 5,
        out_shape=(
            jax.ShapeDtypeStruct((count, points, width), bf16),
            jax.ShapeDtypeStruct((count, width, width), f32),
        ),
        scratch_shapes=[
            pltpu.VMEM((count, width, points), f32),
            pltpu.VMEM((count, width, width), f32),
            pltpu.VMEM((count, width, width), f32),
            pltpu.VMEM((2, 8 * panel, 128), f32),
            pltpu.VMEM((8 * panel, 128), f32),
        ],
        compiler_params=pltpu.CompilerParams(vmem_limit_bytes=28 * 2**20),
        name="finish",
    )(*(pltpu.with_memory_space_constraint(x, pltpu.VMEM) for x in (blocks, even, own, odd)), order)


def blocks_body(pattern_ref, even_ref, own_ref, odd_ref, out_ref, window, squares, listed, *, total):
    count, points = own_ref.shape[1:]
    columns = pattern_ref.shape[1]
    me = lax.axis_index(AXES)
    first = me * count
    side = lax.rem(me, 2)
    window[...] = jnp.zeros_like(window)
    for group, ref in ((2 - 2 * side, even_ref), (1, own_ref), (2 * side, odd_ref)):
        for at in range(count):
            slot = group * count + at
            index = (first + (slot - count)).astype(f32)
            window[slot, 0:1, :] = (ref[0, at:at + 1, :] + index) - index
            window[slot, 1:2, :] = ref[1, at:at + 1, :]
            window[slot, 2:3, :] = ref[2, at:at + 1, :]

    def reach(column):
        return column - W + jnp.where(column >= W - 1, 3, 0)

    def note(pair, found):
        cluster, column = pair // columns, lax.rem(pair, columns)
        source = first + cluster + reach(column)
        counted = (pattern_ref[cluster, column] != 0) & (source >= 0) & (source < total)
        listed[found] = pair

        @pl.when(jnp.logical_not(counted))
        def _():
            out_ref[pair] = jnp.zeros_like(out_ref[pair])

        return found + counted.astype(jnp.int32)

    found = lax.fori_loop(0, count * columns, note, jnp.int32(0))

    def measure(step):
        pair = listed[jnp.minimum(step, jnp.maximum(found - 1, 0))]
        cluster, column = pair // columns, lax.rem(pair, columns)
        distance = reach(column)
        a, b = split_points(window[count + cluster], window[count + cluster + distance], distance)
        return contract(b, a, 0, 0)

    squares[0] = measure(jnp.int32(0))

    def step(at, carry):
        after = measure(at + 1)
        out_ref[listed[at]] = kernel_values(squares[lax.rem(at, 2)], points).astype(bf16)
        squares[lax.rem(at + 1, 2)] = after
        return carry

    lax.fori_loop(0, found, step, 0)


def blocks_of(pattern, even, own, odd, total):
    count, points = own.shape[1:]
    columns = pattern.shape[1]
    pairs = count * columns
    values = pairs * points * points
    whole = pl.BlockSpec(memory_space=pltpu.VMEM)
    return pl.pallas_call(
        functools.partial(blocks_body, total=total),
        in_specs=[pl.BlockSpec(memory_space=pltpu.SMEM), whole, whole, whole],
        out_specs=whole,
        scratch_shapes=[
            pltpu.VMEM((3 * count, 8, points), f32),
            pltpu.VMEM((2, points, points), f32),
            pltpu.SMEM((pairs + 1,), jnp.int32),
        ],
        out_shape=pltpu.VMEM((pairs, points, points), bf16),
        cost_estimate=pl.CostEstimate(flops=40 * values, bytes_accessed=2 * values, transcendentals=3 * values),
        compiler_params=pltpu.CompilerParams(vmem_limit_bytes=16 * 2**20),
        name="blocks",
    )(pattern, even, own, odd)


def body(offsets, sketch, pattern, point_order):
    count = offsets.shape[0]
    total = count * lax.axis_size(AXES)
    offsets = offsets.transpose(1, 0, 2)
    odd_offsets = exchanged(offsets, 1)
    turned = sketch.transpose(0, 2, 1)
    sent, odd_offsets = lax.optimization_barrier((turned, odd_offsets))
    odd_sketch = exchanged(sent, 1)
    even_offsets = exchanged(offsets, 0)
    even_sketch = exchanged(turned, 0)
    blocks = blocks_of(pattern, even_offsets, offsets, odd_offsets, total)
    return finish(blocks, even_sketch, turned, odd_sketch, point_order)


def solution(mesh):
    rows = P(AXES, None, None)
    flat = P(AXES, None)
    return jax.shard_map(
        body,
        mesh=mesh,
        in_specs=(rows, rows, flat, flat),
        out_specs=(rows, rows),
        check_vma=False,
    )
```

```python
import functools
import math

import jax
import jax.numpy as jnp
from jax import lax
from jax.experimental import pallas as pl
from jax.experimental.pallas import tpu as pltpu
from jax.sharding import PartitionSpec as P

W = 4
AXES = ("grp", "dev")
f32 = jnp.float32
bf16 = jnp.bfloat16

wave_number = 40.0
decay_length = 4.0
softening = 0.5
turns = wave_number / (2.0 * math.pi)

SINE = (4.44287957, -7.30781674, 3.5977744, -0.79119941)


def exchanged(array, start):
    peers = lax.axis_size(AXES)
    pairs = [(i, i + 1) for i in range(start, peers - 1, 2)]
    return lax.ppermute(array, AXES, pairs + [(j, i) for i, j in pairs])


def offset_table(reach):
    return [-value for value in range(reach, 1, -1)] + list(range(2, reach + 1))


def kernel_values(turn_squared, points):
    scale = turns / math.sqrt(points)
    turn = turn_squared * lax.rsqrt(turn_squared)
    part = turn - jnp.round(turn)
    square = part * part
    sine = f32(SINE[-1] * math.sqrt(scale))
    for value in SINE[-2::-1]:
        sine = sine * square + f32(value * math.sqrt(scale))
    sine = sine * part
    level = jnp.exp2(turn * f32(-math.log2(math.e) / (decay_length * turns)))
    level = level * pltpu.reciprocal(turn + f32(softening * turns), approx=True)
    return level * (f32(scale) - sine * sine)


def pieces(x):
    high = x.astype(bf16).astype(f32)
    middle = (x - high).astype(bf16).astype(f32)
    low = (x - high - middle).astype(bf16).astype(f32)
    return high, middle, low


def split_points(target, source, distance):
    row = lax.broadcasted_iota(jnp.int32, target.shape, 0)
    half = distance.astype(f32) * f32(0.5)

    def shifted(x, along):
        moved = x + jnp.where(row == 0, along, jnp.where(row < 3, f32(-0.5), f32(0)))
        moved = moved * f32(turns)
        return moved, jnp.sum(moved * moved, axis=0, keepdims=True)

    left, left_norm = shifted(target, -half - f32(0.5))
    right, right_norm = shifted(source, half - f32(0.5))
    left = jnp.where(row == 3, left_norm, jnp.where(row == 4, f32(1), left))
    right = jnp.where(row == 4, right_norm, jnp.where(row == 3, f32(1), f32(-2) * right))
    lh, lm, ll = pieces(left)
    rh, rm, rl = pieces(right)
    a = jnp.concatenate([lh, lh, lm, lm, lh, ll, lm, ll], axis=0).astype(bf16)
    b = jnp.concatenate([rh, rm, rh, rm, rl, rh, rl, rm], axis=0).astype(bf16)
    return a, b


def halves(x):
    hi = x.astype(bf16)
    return hi, (x - hi.astype(f32)).astype(bf16)

def contract(a, b, da, db):
    return lax.dot_general(a, b, (((da,), (db,)), ((), ())), preferred_element_type=f32)

def lane_of(x, lane):
    return jnp.broadcast_to(x[:, lane:lane + 1], x.shape)

def factor_panel(rows, ups, first, panel, micro):
    half = first // 128
    base = first % 128
    lanes = lax.broadcasted_iota(jnp.int32, (8, 128), 1)
    for start in range(0, panel, micro):
        lane0 = base + start
        inside = (lanes >= lane0) & (lanes < lane0 + micro)
        raw = [rows[half, 8 * (start + j):8 * (start + j) + 8, :] for j in range(micro)]
        other = [rows[1 - half, 8 * (start + j):8 * (start + j) + 8, :] for j in range(micro)]
        a = [[lane_of(raw[i], lane0 + k) for k in range(i + 1)] for i in range(micro)]
        low = [[None] * micro for _ in range(micro)]
        inv = [None] * micro
        for k in range(micro):
            inv[k] = lax.rsqrt(a[k][k])
            for i in range(k + 1, micro):
                low[i][k] = a[i][k] * inv[k]
            for i in range(k + 1, micro):
                for m in range(k + 1, i + 1):
                    a[i][m] = a[i][m] - low[i][k] * low[m][k]
        solved = [jnp.where(inside, jnp.where(lanes == lane0 + j, f32(1), f32(0)), raw[j]) for j in range(micro)]
        for k in range(micro):
            raw[k] = raw[k] * inv[k]
            solved[k] = solved[k] * inv[k]
            other[k] = other[k] * inv[k]
            for i in range(k + 1, micro):
                raw[i] = raw[i] - low[i][k] * raw[k]
                solved[i] = solved[i] - low[i][k] * solved[k]
                other[i] = other[i] - low[i][k] * other[k]
        for j in range(micro):
            at = slice(8 * (start + j), 8 * (start + j) + 8)
            ups[at, :] = raw[j]
            rows[half, at, :] = solved[j]
            rows[1 - half, at, :] = other[j]
        for i in range(start + micro, panel):
            at = slice(8 * i, 8 * i + 8)
            x = jnp.where(inside, f32(0), rows[half, at, :])
            y = rows[1 - half, at, :]
            tx = ty = None
            for j in range(micro):
                c = lane_of(raw[j], base + i)
                tx = c * solved[j] if tx is None else tx + c * solved[j]
                ty = c * other[j] if ty is None else ty + c * other[j]
            rows[half, at, :] = x - tx
            rows[1 - half, at, :] = y - ty

def finish_body(k_ref, even_ref, own_ref, odd_ref, order_ref, basis_ref, factor_ref, t_ref, mat, inv_ref, rows, ups, *, panel, micro):
    count, width, points = own_ref.shape
    row_id = lax.broadcasted_iota(jnp.int32, (width, width), 0)
    col_id = lax.broadcasted_iota(jnp.int32, (width, width), 1)

    def fill(refs):
        for c in range(count):
            samples = None
            for column, distance in enumerate(offset_table(W)):
                slot = c + count + distance
                block = k_ref[len(offset_table(W)) * c + column]
                term = jnp.dot(refs[slot // count][slot % count], block, preferred_element_type=f32)
                samples = term if samples is None else samples + term
            t_ref[c] = samples

    side = lax.rem(lax.axis_index(AXES), 2)
    pl.when(side == 1)(lambda: fill((even_ref, own_ref, odd_ref)))
    pl.when(side == 0)(lambda: fill((odd_ref, own_ref, even_ref)))
    for c in range(count):
        hi, lo = halves(t_ref[c])
        gram = contract(jnp.concatenate([hi, hi, lo], axis=1), jnp.concatenate([hi, lo, hi], axis=1), 1, 1)
        shift = f32(0.01) * jnp.sum(jnp.where(row_id == col_id, gram, f32(0))) / f32(width) + f32(1e-5)
        mat[c] = gram + jnp.where(row_id == col_id, shift, f32(0))
    for first in range(0, width, panel):
        half = first // 128
        base = first % 128
        for c in range(count):
            for h in range(2):
                for t in range(0, panel, 8):
                    tile = mat[c, first + t:first + t + 8, 128 * h:128 * h + 128]
                    rows[h, pl.ds(8 * t + c, 8, stride=8), :] = tile
        factor_panel(rows, ups, first, panel, micro)
        prow = lax.broadcasted_iota(jnp.int32, (panel, 128), 0) + base
        pcol = lax.broadcasted_iota(jnp.int32, (panel, 128), 1)
        for c in range(count):
            z = [rows[h, pl.ds(c, panel, stride=8), :] for h in range(2)]
            u = ups[pl.ds(c, panel, stride=8), :]
            u = jnp.where(pcol >= prow, u, f32(0))
            wz = jnp.where((pcol <= prow) | (pcol >= base + panel), z[half], f32(0))
            w = jnp.where(pcol <= prow, z[half], f32(0))
            z[half] = wz
            factor_ref[c, first:first + panel, 128 * half:128 * half + 128] = u
            factor_ref[c, first:first + panel, 128 * (1 - half):128 * (1 - half) + 128] = z[1] if half == 0 else jnp.zeros_like(u)
            inv_ref[c, first:first + panel, 128 * half:128 * half + 128] = w
            inv_ref[c, first:first + panel, 128 * (1 - half):128 * (1 - half) + 128] = z[0] if half == 1 else jnp.zeros_like(u)
            rest = first + panel
            if rest < width:
                zz = jnp.concatenate(z, axis=1)
                hi, lo = halves(zz)
                left = jnp.concatenate([hi, hi, lo], axis=0)
                right = jnp.concatenate([hi, lo, hi], axis=0)
                off = (rest // 128) * 128
                prod = contract(left[:, off:], right, 0, 0)[rest - off:, :]
                old = mat[c, rest:, :]
                cc = col_id[rest:, :]
                old = jnp.where((cc >= first) & (cc < rest), f32(0), old)
                mat[c, rest:, :] = old - prod
    for c in range(count):
        hi, lo = halves(t_ref[c])
        wh, wl = halves(inv_ref[c])
        b = jnp.dot(jnp.concatenate([wh, wh, wl], axis=1), jnp.concatenate([hi, lo, hi], axis=0), preferred_element_type=f32).astype(bf16)
        order_t = jnp.broadcast_to(order_ref[c:c + 1, :].astype(f32), (128, points)).T
        place = lax.broadcasted_iota(jnp.int32, (points, 128), 1).astype(f32)
        pick = jnp.concatenate([jnp.where(order_t == place + f32(128 * q), f32(1), f32(0)).astype(bf16) for q in range(points // 128)], axis=1)
        basis_ref[c] = contract(pick, b, 1, 1).astype(bf16)

def finish(blocks, even, own, odd, order, panel=16, micro=8):
    count, width, points = own.shape
    whole = pl.BlockSpec(memory_space=pltpu.VMEM)
    return pl.pallas_call(
        functools.partial(finish_body, panel=panel, micro=micro),
        in_specs=[whole] * 5,
        out_shape=(
            jax.ShapeDtypeStruct((count, points, width), bf16),
            jax.ShapeDtypeStruct((count, width, width), f32),
        ),
        scratch_shapes=[
            pltpu.VMEM((count, width, points), f32),
            pltpu.VMEM((count, width, width), f32),
            pltpu.VMEM((count, width, width), f32),
            pltpu.VMEM((2, 8 * panel, 128), f32),
            pltpu.VMEM((8 * panel, 128), f32),
        ],
        compiler_params=pltpu.CompilerParams(vmem_limit_bytes=28 * 2**20),
        name="finish",
    )(*(pltpu.with_memory_space_constraint(x, pltpu.VMEM) for x in (blocks, even, own, odd)), order)


def blocks_body(pattern_any, even_ref, own_any, odd_ref, out_ref, window, here, there, listed, own_ref, pattern_ref, sems, *, total):
    count, points = own_ref.shape[1:]
    columns = pattern_ref.shape[1]
    fetch_own = pltpu.make_async_copy(own_any, own_ref, sems.at[0])
    fetch_pattern = pltpu.make_async_copy(pattern_any, pattern_ref, sems.at[1])
    fetch_own.start()
    fetch_pattern.start()
    me = lax.axis_index(AXES)
    first = me * count
    side = lax.rem(me, 2)
    window[...] = jnp.zeros_like(window)
    fetch_own.wait()
    fetch_pattern.wait()
    for group, ref in ((2 - 2 * side, even_ref), (1, own_ref), (2 * side, odd_ref)):
        for at in range(count):
            slot = group * count + at
            index = (first + (slot - count)).astype(f32)
            window[slot, 0:1, :] = (ref[0, at:at + 1, :] + index) - index
            window[slot, 1:2, :] = ref[1, at:at + 1, :]
            window[slot, 2:3, :] = ref[2, at:at + 1, :]

    def reach(column):
        return column - W + jnp.where(column >= W - 1, 3, 0)

    def note(pair, found):
        cluster, column = pair // columns, lax.rem(pair, columns)
        source = first + cluster + reach(column)
        counted = (pattern_ref[cluster, column] != 0) & (source >= 0) & (source < total)
        listed[found] = pair

        @pl.when(jnp.logical_not(counted))
        def _():
            out_ref[pair] = jnp.zeros_like(out_ref[pair])

        return found + counted.astype(jnp.int32)

    found = lax.fori_loop(0, count * columns, note, jnp.int32(0))

    def measure(step):
        pair = listed[jnp.minimum(step, jnp.maximum(found - 1, 0))]
        cluster, column = pair // columns, lax.rem(pair, columns)
        distance = reach(column)
        a, b = split_points(window[count + cluster], window[count + cluster + distance], distance)
        return contract(b, a, 0, 0)

    here[...] = measure(jnp.int32(0))

    def two_steps(twice, carry):
        at = 2 * twice
        there[...] = measure(at + 1)
        out_ref[listed[at]] = kernel_values(here[...], points).astype(bf16)

        @pl.when(at + 1 < found)
        def _():
            here[...] = measure(at + 2)
            out_ref[listed[at + 1]] = kernel_values(there[...], points).astype(bf16)

        return carry

    lax.fori_loop(0, (found + 1) // 2, two_steps, 0)


def blocks_of(pattern, even, own, odd, total):
    count, points = own.shape[1:]
    columns = pattern.shape[1]
    pairs = count * columns
    values = pairs * points * points
    whole = pl.BlockSpec(memory_space=pltpu.VMEM)
    far = pl.BlockSpec(memory_space=pl.ANY)
    return pl.pallas_call(
        functools.partial(blocks_body, total=total),
        in_specs=[far, whole, far, whole],
        out_specs=whole,
        scratch_shapes=[
            pltpu.VMEM((3 * count, 8, points), f32),
            pltpu.VMEM((points, points), f32),
            pltpu.VMEM((points, points), f32),
            pltpu.SMEM((pairs + 1,), jnp.int32),
            pltpu.VMEM(own.shape, f32),
            pltpu.SMEM(pattern.shape, jnp.int32),
            pltpu.SemaphoreType.DMA((2,)),
        ],
        out_shape=pltpu.VMEM((pairs, points, points), bf16),
        cost_estimate=pl.CostEstimate(flops=40 * values, bytes_accessed=2 * values, transcendentals=3 * values),
        compiler_params=pltpu.CompilerParams(vmem_limit_bytes=16 * 2**20),
        name="blocks",
    )(pltpu.with_memory_space_constraint(pattern, pltpu.HBM), even, pltpu.with_memory_space_constraint(own, pltpu.HBM), odd)


def body(offsets, sketch, pattern, point_order):
    count = offsets.shape[0]
    total = count * lax.axis_size(AXES)
    offsets = offsets.transpose(1, 0, 2)
    odd_offsets = exchanged(offsets, 1)
    turned = sketch.transpose(0, 2, 1)
    sent, odd_offsets = lax.optimization_barrier((turned, odd_offsets))
    odd_sketch = exchanged(sent, 1)
    even_offsets = exchanged(offsets, 0)
    even_sketch = exchanged(turned, 0)
    blocks = blocks_of(pattern, even_offsets, offsets, odd_offsets, total)
    return finish(blocks, even_sketch, turned, odd_sketch, point_order)


def solution(mesh):
    rows = P(AXES, None, None)
    flat = P(AXES, None)
    return jax.shard_map(
        body,
        mesh=mesh,
        in_specs=(rows, rows, flat, flat),
        out_specs=(rows, rows),
        check_vma=False,
    )
```

```python
import functools
import math

import jax
import jax.numpy as jnp
from jax import lax
from jax.experimental import pallas as pl
from jax.experimental.pallas import tpu as pltpu
from jax.sharding import PartitionSpec as P

W = 4
AXES = ("grp", "dev")
f32 = jnp.float32
bf16 = jnp.bfloat16

wave_number = 40.0
decay_length = 4.0
softening = 0.5
turns = wave_number / (2.0 * math.pi)

SINE = (4.44287957, -7.30781674, 3.5977744, -0.79119941)


def exchanged(array, start):
    peers = lax.axis_size(AXES)
    pairs = [(i, i + 1) for i in range(start, peers - 1, 2)]
    return lax.ppermute(array, AXES, pairs + [(j, i) for i, j in pairs])


def offset_table(reach):
    return [-value for value in range(reach, 1, -1)] + list(range(2, reach + 1))


def kernel_values(turn_squared, points):
    scale = turns / math.sqrt(points)
    turn = turn_squared * lax.rsqrt(turn_squared)
    part = turn - jnp.round(turn)
    square = part * part
    sine = f32(SINE[-1] * math.sqrt(scale))
    for value in SINE[-2::-1]:
        sine = sine * square + f32(value * math.sqrt(scale))
    sine = sine * part
    level = jnp.exp2(turn * f32(-math.log2(math.e) / (decay_length * turns)))
    level = level * pltpu.reciprocal(turn + f32(softening * turns), approx=True)
    return level * (f32(scale) - sine * sine)


def pieces(x):
    high = x.astype(bf16).astype(f32)
    middle = (x - high).astype(bf16).astype(f32)
    low = (x - high - middle).astype(bf16).astype(f32)
    return high, middle, low


def split_points(target, source, distance):
    row = lax.broadcasted_iota(jnp.int32, target.shape, 0)
    half = distance.astype(f32) * f32(0.5)

    def shifted(x, along):
        moved = x + jnp.where(row == 0, along, jnp.where(row < 3, f32(-0.5), f32(0)))
        moved = moved * f32(turns)
        return moved, jnp.sum(moved * moved, axis=0, keepdims=True)

    left, left_norm = shifted(target, -half - f32(0.5))
    right, right_norm = shifted(source, half - f32(0.5))
    left = jnp.where(row == 3, left_norm, jnp.where(row == 4, f32(1), left))
    right = jnp.where(row == 4, right_norm, jnp.where(row == 3, f32(1), f32(-2) * right))
    lh, lm, ll = pieces(left)
    rh, rm, rl = pieces(right)
    a = jnp.concatenate([lh, lh, lm, lm, lh, ll, lm, ll], axis=0).astype(bf16)
    b = jnp.concatenate([rh, rm, rh, rm, rl, rh, rl, rm], axis=0).astype(bf16)
    return a, b


def halves(x):
    hi = x.astype(bf16)
    return hi, (x - hi.astype(f32)).astype(bf16)

def contract(a, b, da, db):
    return lax.dot_general(a, b, (((da,), (db,)), ((), ())), preferred_element_type=f32)

def lane_of(x, lane):
    return jnp.broadcast_to(x[:, lane:lane + 1], x.shape)

def factor_panel(rows, ups, first, panel, micro):
    half = first // 128
    base = first % 128
    pair = micro // 2
    lanes = lax.broadcasted_iota(jnp.int32, (8, 128), 1)
    lower = lax.broadcasted_iota(jnp.int32, (8, 128), 0) < 4

    def packed(x, y):
        return jnp.where(lower, x, pltpu.roll(y, 4, axis=0))

    for start in range(0, panel, micro):
        lane0 = base + start
        inside = (lanes >= lane0) & (lanes < lane0 + micro)
        raw = [rows[half, 8 * (start + j):8 * (start + j) + 8, :] for j in range(micro)]
        other = [rows[1 - half, 8 * (start + j):8 * (start + j) + 8, :] for j in range(micro)]
        a = [[None] * micro for _ in range(micro)]
        for i in range(pair):
            both = packed(raw[i], raw[i + pair])
            for k in range(i + pair + 1):
                value = lane_of(both, lane0 + k)
                if k <= i:
                    a[i][k] = value
                a[i + pair][k] = pltpu.roll(value, 4, axis=0)
        low = [[None] * micro for _ in range(micro)]
        inv = [None] * micro
        for k in range(micro):
            inv[k] = lax.rsqrt(a[k][k])
            for i in range(k + 1, micro):
                low[i][k] = a[i][k] * inv[k]
            for i in range(k + 1, micro):
                for m in range(k + 1, i + 1):
                    a[i][m] = a[i][m] - low[i][k] * low[m][k]
        solved = [jnp.where(inside, jnp.where(lanes == lane0 + j, f32(1), f32(0)), raw[j]) for j in range(micro)]
        for k in range(micro):
            raw[k] = raw[k] * inv[k]
            solved[k] = solved[k] * inv[k]
            other[k] = other[k] * inv[k]
            for i in range(k + 1, micro):
                raw[i] = raw[i] - low[i][k] * raw[k]
                solved[i] = solved[i] - low[i][k] * solved[k]
                other[i] = other[i] - low[i][k] * other[k]
        for j in range(micro):
            at = slice(8 * (start + j), 8 * (start + j) + 8)
            ups[at, :] = raw[j]
            rows[half, at, :] = solved[j]
            rows[1 - half, at, :] = other[j]
        if start + micro < panel:
            raw = [packed(raw[j], raw[j + pair]) for j in range(pair)]
            solved = [packed(solved[j], solved[j + pair]) for j in range(pair)]
            other = [packed(other[j], other[j + pair]) for j in range(pair)]
        for i in range(start + micro, panel):
            at = slice(8 * i, 8 * i + 8)
            x = jnp.where(inside, f32(0), rows[half, at, :])
            y = rows[1 - half, at, :]
            tx = ty = None
            for j in range(pair):
                c = lane_of(raw[j], base + i)
                tx = c * solved[j] if tx is None else tx + c * solved[j]
                ty = c * other[j] if ty is None else ty + c * other[j]
            rows[half, at, :] = x - (tx + pltpu.roll(tx, 4, axis=0))
            rows[1 - half, at, :] = y - (ty + pltpu.roll(ty, 4, axis=0))

def finish_body(k_ref, even_ref, own_ref, odd_ref, order_ref, basis_ref, factor_ref, t_ref, mat, inv_ref, rows, ups, *, panel, micro):
    count, width, points = own_ref.shape
    row_id = lax.broadcasted_iota(jnp.int32, (width, width), 0)
    col_id = lax.broadcasted_iota(jnp.int32, (width, width), 1)

    def fill(refs):
        for c in range(count):
            samples = None
            for column, distance in enumerate(offset_table(W)):
                slot = c + count + distance
                block = k_ref[len(offset_table(W)) * c + column]
                term = jnp.dot(refs[slot // count][slot % count], block, preferred_element_type=f32)
                samples = term if samples is None else samples + term
            t_ref[c] = samples

    side = lax.rem(lax.axis_index(AXES), 2)
    pl.when(side == 1)(lambda: fill((even_ref, own_ref, odd_ref)))
    pl.when(side == 0)(lambda: fill((odd_ref, own_ref, even_ref)))
    for c in range(count):
        hi, lo = halves(t_ref[c])
        gram = contract(jnp.concatenate([hi, hi, lo], axis=1), jnp.concatenate([hi, lo, hi], axis=1), 1, 1)
        shift = f32(0.01) * jnp.sum(jnp.where(row_id == col_id, gram, f32(0))) / f32(width) + f32(1e-5)
        mat[c] = gram + jnp.where(row_id == col_id, shift, f32(0))
    for first in range(0, width, panel):
        half = first // 128
        base = first % 128
        for c in range(count):
            for h in range(2):
                for t in range(0, panel, 8):
                    tile = mat[c, first + t:first + t + 8, 128 * h:128 * h + 128]
                    rows[h, pl.ds(8 * t + c, 8, stride=8), :] = tile
        factor_panel(rows, ups, first, panel, micro)
        prow = lax.broadcasted_iota(jnp.int32, (panel, 128), 0) + base
        pcol = lax.broadcasted_iota(jnp.int32, (panel, 128), 1)
        for c in range(count):
            z = [rows[h, pl.ds(c, panel, stride=8), :] for h in range(2)]
            u = ups[pl.ds(c, panel, stride=8), :]
            u = jnp.where(pcol >= prow, u, f32(0))
            wz = jnp.where((pcol <= prow) | (pcol >= base + panel), z[half], f32(0))
            w = jnp.where(pcol <= prow, z[half], f32(0))
            z[half] = wz
            factor_ref[c, first:first + panel, 128 * half:128 * half + 128] = u
            factor_ref[c, first:first + panel, 128 * (1 - half):128 * (1 - half) + 128] = z[1] if half == 0 else jnp.zeros_like(u)
            inv_ref[c, first:first + panel, 128 * half:128 * half + 128] = w
            inv_ref[c, first:first + panel, 128 * (1 - half):128 * (1 - half) + 128] = z[0] if half == 1 else jnp.zeros_like(u)
            rest = first + panel
            if rest < width:
                zz = jnp.concatenate(z, axis=1)
                hi, lo = halves(zz)
                left = jnp.concatenate([hi, hi, lo], axis=0)
                right = jnp.concatenate([hi, lo, hi], axis=0)
                off = (rest // 128) * 128
                prod = contract(left[:, off:], right, 0, 0)[rest - off:, :]
                old = mat[c, rest:, :]
                cc = col_id[rest:, :]
                old = jnp.where((cc >= first) & (cc < rest), f32(0), old)
                mat[c, rest:, :] = old - prod
    for c in range(count):
        hi, lo = halves(t_ref[c])
        wh, wl = halves(inv_ref[c])
        b = jnp.dot(jnp.concatenate([wh, wh, wl], axis=1), jnp.concatenate([hi, lo, hi], axis=0), preferred_element_type=f32).astype(bf16)
        order_t = jnp.broadcast_to(order_ref[c:c + 1, :].astype(f32), (128, points)).T
        place = lax.broadcasted_iota(jnp.int32, (points, 128), 1).astype(f32)
        pick = jnp.concatenate([jnp.where(order_t == place + f32(128 * q), f32(1), f32(0)).astype(bf16) for q in range(points // 128)], axis=1)
        basis_ref[c] = contract(pick, b, 1, 1).astype(bf16)

def finish(blocks, even, own, odd, order, panel=32, micro=8):
    count, width, points = own.shape
    whole = pl.BlockSpec(memory_space=pltpu.VMEM)
    return pl.pallas_call(
        functools.partial(finish_body, panel=panel, micro=micro),
        in_specs=[whole] * 5,
        out_shape=(
            jax.ShapeDtypeStruct((count, points, width), bf16),
            jax.ShapeDtypeStruct((count, width, width), f32),
        ),
        scratch_shapes=[
            pltpu.VMEM((count, width, points), f32),
            pltpu.VMEM((count, width, width), f32),
            pltpu.VMEM((count, width, width), f32),
            pltpu.VMEM((2, 8 * panel, 128), f32),
            pltpu.VMEM((8 * panel, 128), f32),
        ],
        compiler_params=pltpu.CompilerParams(vmem_limit_bytes=28 * 2**20),
        name="finish",
    )(*(pltpu.with_memory_space_constraint(x, pltpu.VMEM) for x in (blocks, even, own, odd)), order)


def blocks_body(pattern_any, even_ref, own_any, odd_ref, out_ref, window, here, there, listed, own_ref, pattern_ref, sems, *, total):
    count, points = own_ref.shape[1:]
    columns = pattern_ref.shape[1]
    fetch_own = pltpu.make_async_copy(own_any, own_ref, sems.at[0])
    fetch_pattern = pltpu.make_async_copy(pattern_any, pattern_ref, sems.at[1])
    fetch_own.start()
    fetch_pattern.start()
    me = lax.axis_index(AXES)
    first = me * count
    side = lax.rem(me, 2)
    window[...] = jnp.zeros_like(window)
    fetch_own.wait()
    fetch_pattern.wait()
    for group, ref in ((2 - 2 * side, even_ref), (1, own_ref), (2 * side, odd_ref)):
        for at in range(count):
            slot = group * count + at
            index = (first + (slot - count)).astype(f32)
            window[slot, 0:1, :] = (ref[0, at:at + 1, :] + index) - index
            window[slot, 1:2, :] = ref[1, at:at + 1, :]
            window[slot, 2:3, :] = ref[2, at:at + 1, :]

    def reach(column):
        return column - W + jnp.where(column >= W - 1, 3, 0)

    def note(pair, found):
        cluster, column = pair // columns, lax.rem(pair, columns)
        source = first + cluster + reach(column)
        counted = (pattern_ref[cluster, column] != 0) & (source >= 0) & (source < total)
        listed[found] = pair

        @pl.when(jnp.logical_not(counted))
        def _():
            out_ref[pair] = jnp.zeros_like(out_ref[pair])

        return found + counted.astype(jnp.int32)

    found = lax.fori_loop(0, count * columns, note, jnp.int32(0))

    def measure(step):
        pair = listed[jnp.minimum(step, jnp.maximum(found - 1, 0))]
        cluster, column = pair // columns, lax.rem(pair, columns)
        distance = reach(column)
        a, b = split_points(window[count + cluster], window[count + cluster + distance], distance)
        return contract(b, a, 0, 0)

    here[...] = measure(jnp.int32(0))

    def two_steps(twice, carry):
        at = 2 * twice
        there[...] = measure(at + 1)
        out_ref[listed[at]] = kernel_values(here[...], points).astype(bf16)
        here[...] = measure(at + 2)
        out_ref[listed[at + 1]] = kernel_values(there[...], points).astype(bf16)
        return carry

    lax.fori_loop(0, found // 2, two_steps, 0)

    @pl.when(lax.rem(found, 2) == 1)
    def _():
        out_ref[listed[found - 1]] = kernel_values(here[...], points).astype(bf16)


def blocks_of(pattern, even, own, odd, total):
    count, points = own.shape[1:]
    columns = pattern.shape[1]
    pairs = count * columns
    values = pairs * points * points
    whole = pl.BlockSpec(memory_space=pltpu.VMEM)
    far = pl.BlockSpec(memory_space=pl.ANY)
    return pl.pallas_call(
        functools.partial(blocks_body, total=total),
        in_specs=[far, whole, far, whole],
        out_specs=whole,
        scratch_shapes=[
            pltpu.VMEM((3 * count, 8, points), f32),
            pltpu.VMEM((points, points), f32),
            pltpu.VMEM((points, points), f32),
            pltpu.SMEM((pairs + 1,), jnp.int32),
            pltpu.VMEM(own.shape, f32),
            pltpu.SMEM(pattern.shape, jnp.int32),
            pltpu.SemaphoreType.DMA((2,)),
        ],
        out_shape=pltpu.VMEM((pairs, points, points), bf16),
        cost_estimate=pl.CostEstimate(flops=40 * values, bytes_accessed=2 * values, transcendentals=3 * values),
        compiler_params=pltpu.CompilerParams(vmem_limit_bytes=16 * 2**20),
        name="blocks",
    )(pltpu.with_memory_space_constraint(pattern, pltpu.HBM), even, pltpu.with_memory_space_constraint(own, pltpu.HBM), odd)


def body(offsets, sketch, pattern, point_order):
    count = offsets.shape[0]
    total = count * lax.axis_size(AXES)
    offsets = offsets.transpose(1, 0, 2)
    odd_offsets = exchanged(offsets, 1)
    turned = sketch.transpose(0, 2, 1)
    sent, odd_offsets = lax.optimization_barrier((turned, odd_offsets))
    odd_sketch = exchanged(sent, 1)
    even_offsets = exchanged(offsets, 0)
    even_sketch = exchanged(turned, 0)
    blocks = blocks_of(pattern, even_offsets, offsets, odd_offsets, total)
    return finish(blocks, even_sketch, turned, odd_sketch, point_order)


def solution(mesh):
    rows = P(AXES, None, None)
    flat = P(AXES, None)
    return jax.shard_map(
        body,
        mesh=mesh,
        in_specs=(rows, rows, flat, flat),
        out_specs=(rows, rows),
        check_vma=False,
    )
```

```python
import functools
import math

import jax
import jax.numpy as jnp
from jax import lax
from jax.experimental import pallas as pl
from jax.experimental.pallas import tpu as pltpu
from jax.sharding import PartitionSpec as P

W = 4
AXES = ("grp", "dev")
f32 = jnp.float32
bf16 = jnp.bfloat16

wave_number = 40.0
decay_length = 4.0
softening = 0.5
turns = wave_number / (2.0 * math.pi)

SINE = (4.44287957, -7.30781674, 3.5977744, -0.79119941)


def exchanged(array, start):
    peers = lax.axis_size(AXES)
    pairs = [(i, i + 1) for i in range(start, peers - 1, 2)]
    return lax.ppermute(array, AXES, pairs + [(j, i) for i, j in pairs])


def offset_table(reach):
    return [-value for value in range(reach, 1, -1)] + list(range(2, reach + 1))


def kernel_values(turn_squared, points):
    scale = turns / math.sqrt(points)
    turn = turn_squared * lax.rsqrt(turn_squared)
    part = turn - jnp.round(turn)
    square = part * part
    sine = f32(SINE[-1] * math.sqrt(scale))
    for value in SINE[-2::-1]:
        sine = sine * square + f32(value * math.sqrt(scale))
    sine = sine * part
    level = jnp.exp2(turn * f32(-math.log2(math.e) / (decay_length * turns)))
    level = level * pltpu.reciprocal(turn + f32(softening * turns), approx=True)
    return level * (f32(scale) - sine * sine)


def pieces(x):
    high = x.astype(bf16).astype(f32)
    middle = (x - high).astype(bf16).astype(f32)
    low = (x - high - middle).astype(bf16).astype(f32)
    return high, middle, low


def split_points(target, source, distance):
    row = lax.broadcasted_iota(jnp.int32, target.shape, 0)
    half = distance.astype(f32) * f32(0.5)

    def shifted(x, along):
        moved = x + jnp.where(row == 0, along, jnp.where(row < 3, f32(-0.5), f32(0)))
        moved = moved * f32(turns)
        return moved, jnp.sum(moved * moved, axis=0, keepdims=True)

    left, left_norm = shifted(target, -half - f32(0.5))
    right, right_norm = shifted(source, half - f32(0.5))
    left = jnp.where(row == 3, left_norm, jnp.where(row == 4, f32(1), left))
    right = jnp.where(row == 4, right_norm, jnp.where(row == 3, f32(1), f32(-2) * right))
    lh, lm, ll = pieces(left)
    rh, rm, rl = pieces(right)
    a = jnp.concatenate([lh, lh, lm, lm, lh, ll, lm, ll], axis=0).astype(bf16)
    b = jnp.concatenate([rh, rm, rh, rm, rl, rh, rl, rm], axis=0).astype(bf16)
    return a, b


def halves(x):
    hi = x.astype(bf16)
    return hi, (x - hi.astype(f32)).astype(bf16)

def contract(a, b, da, db):
    return lax.dot_general(a, b, (((da,), (db,)), ((), ())), preferred_element_type=f32)

def lane_of(x, lane):
    return jnp.broadcast_to(x[:, lane:lane + 1], x.shape)

def factor_panel(rows, ups, first, panel, micro):
    half = first // 128
    base = first % 128
    pair = micro // 2
    lanes = lax.broadcasted_iota(jnp.int32, (8, 128), 1)
    lower = lax.broadcasted_iota(jnp.int32, (8, 128), 0) < 4

    def packed(x, y):
        return jnp.where(lower, x, pltpu.roll(y, 4, axis=0))

    for start in range(0, panel, micro):
        lane0 = base + start
        inside = (lanes >= lane0) & (lanes < lane0 + micro)
        raw = [rows[half, 8 * (start + j):8 * (start + j) + 8, :] for j in range(micro)]
        other = [rows[1 - half, 8 * (start + j):8 * (start + j) + 8, :] for j in range(micro)]
        a = [[None] * micro for _ in range(micro)]
        for i in range(pair):
            both = packed(raw[i], raw[i + pair])
            for k in range(i + pair + 1):
                value = lane_of(both, lane0 + k)
                if k <= i:
                    a[i][k] = value
                a[i + pair][k] = pltpu.roll(value, 4, axis=0)
        low = [[None] * micro for _ in range(micro)]
        inv = [None] * micro
        for k in range(micro):
            inv[k] = lax.rsqrt(a[k][k])
            for i in range(k + 1, micro):
                low[i][k] = a[i][k] * inv[k]
            for i in range(k + 1, micro):
                for m in range(k + 1, i + 1):
                    a[i][m] = a[i][m] - low[i][k] * low[m][k]
        solved = [jnp.where(inside, jnp.where(lanes == lane0 + j, f32(1), f32(0)), raw[j]) for j in range(micro)]
        for k in range(micro):
            raw[k] = raw[k] * inv[k]
            solved[k] = solved[k] * inv[k]
            other[k] = other[k] * inv[k]
            for i in range(k + 1, micro):
                raw[i] = raw[i] - low[i][k] * raw[k]
                solved[i] = solved[i] - low[i][k] * solved[k]
                other[i] = other[i] - low[i][k] * other[k]
        for j in range(micro):
            at = slice(8 * (start + j), 8 * (start + j) + 8)
            ups[at, :] = raw[j]
            rows[half, at, :] = solved[j]
            rows[1 - half, at, :] = other[j]
        if start + micro < panel:
            raw = [packed(raw[j], raw[j + pair]) for j in range(pair)]
            solved = [packed(solved[j], solved[j + pair]) for j in range(pair)]
            other = [packed(other[j], other[j + pair]) for j in range(pair)]
        for i in range(start + micro, panel):
            at = slice(8 * i, 8 * i + 8)
            x = jnp.where(inside, f32(0), rows[half, at, :])
            y = rows[1 - half, at, :]
            tx = ty = None
            for j in range(pair):
                c = lane_of(raw[j], base + i)
                tx = c * solved[j] if tx is None else tx + c * solved[j]
                ty = c * other[j] if ty is None else ty + c * other[j]
            rows[half, at, :] = x - (tx + pltpu.roll(tx, 4, axis=0))
            rows[1 - half, at, :] = y - (ty + pltpu.roll(ty, 4, axis=0))

def finish_body(k_ref, early_ref, some_ref, most_ref, order_ref, basis_ref, factor_ref, t_ref, mat, inv_ref, rows, ups, *, panel, micro):
    count, width, points = early_ref.shape
    row_id = lax.broadcasted_iota(jnp.int32, (width, width), 0)
    col_id = lax.broadcasted_iota(jnp.int32, (width, width), 1)

    def fill(columns, shift):
        for c in range(count):
            samples = early_ref[c]
            for column in columns:
                slot = c + offset_table(W)[column] + shift
                if 0 <= slot < count:
                    ref, at = (some_ref, slot) if slot < count // 2 else (most_ref, slot - count // 2)
                    rows_of = ref[at * width:(at + 1) * width, :]
                    block = k_ref[len(columns) * c + column % len(columns)]
                    samples = samples + jnp.dot(rows_of, block, preferred_element_type=f32)
            t_ref[c] = samples

    side = lax.rem(lax.axis_index(AXES), 2)
    reach = len(offset_table(W)) // 2
    pl.when(side == 1)(lambda: fill(range(reach, 2 * reach), -count))
    pl.when(side == 0)(lambda: fill(range(reach), count))
    for c in range(count):
        hi, lo = halves(t_ref[c])
        gram = contract(jnp.concatenate([hi, hi, lo], axis=1), jnp.concatenate([hi, lo, hi], axis=1), 1, 1)
        shift = f32(0.01) * jnp.sum(jnp.where(row_id == col_id, gram, f32(0))) / f32(width) + f32(1e-5)
        mat[c] = gram + jnp.where(row_id == col_id, shift, f32(0))
    for first in range(0, width, panel):
        half = first // 128
        base = first % 128
        for c in range(count):
            for h in range(2):
                for t in range(0, panel, 8):
                    tile = mat[c, first + t:first + t + 8, 128 * h:128 * h + 128]
                    rows[h, pl.ds(8 * t + c, 8, stride=8), :] = tile
        factor_panel(rows, ups, first, panel, micro)
        prow = lax.broadcasted_iota(jnp.int32, (panel, 128), 0) + base
        pcol = lax.broadcasted_iota(jnp.int32, (panel, 128), 1)
        for c in range(count):
            z = [rows[h, pl.ds(c, panel, stride=8), :] for h in range(2)]
            u = ups[pl.ds(c, panel, stride=8), :]
            u = jnp.where(pcol >= prow, u, f32(0))
            wz = jnp.where((pcol <= prow) | (pcol >= base + panel), z[half], f32(0))
            w = jnp.where(pcol <= prow, z[half], f32(0))
            z[half] = wz
            factor_ref[c, first:first + panel, 128 * half:128 * half + 128] = u
            factor_ref[c, first:first + panel, 128 * (1 - half):128 * (1 - half) + 128] = z[1] if half == 0 else jnp.zeros_like(u)
            inv_ref[c, first:first + panel, 128 * half:128 * half + 128] = w
            inv_ref[c, first:first + panel, 128 * (1 - half):128 * (1 - half) + 128] = z[0] if half == 1 else jnp.zeros_like(u)
            rest = first + panel
            if rest < width:
                zz = jnp.concatenate(z, axis=1)
                hi, lo = halves(zz)
                left = jnp.concatenate([hi, hi, lo], axis=0)
                right = jnp.concatenate([hi, lo, hi], axis=0)
                off = (rest // 128) * 128
                prod = contract(left[:, off:], right, 0, 0)[rest - off:, :]
                old = mat[c, rest:, :]
                cc = col_id[rest:, :]
                old = jnp.where((cc >= first) & (cc < rest), f32(0), old)
                mat[c, rest:, :] = old - prod
    for c in range(count):
        hi, lo = halves(t_ref[c])
        wh, wl = halves(inv_ref[c])
        b = jnp.dot(jnp.concatenate([wh, wh, wl], axis=1), jnp.concatenate([hi, lo, hi], axis=0), preferred_element_type=f32).astype(bf16)
        order_t = jnp.broadcast_to(order_ref[c:c + 1, :].astype(f32), (128, points)).T
        place = lax.broadcasted_iota(jnp.int32, (points, 128), 1).astype(f32)
        pick = jnp.concatenate([jnp.where(order_t == place + f32(128 * q), f32(1), f32(0)).astype(bf16) for q in range(points // 128)], axis=1)
        basis_ref[c] = contract(pick, b, 1, 1).astype(bf16)

def finish(blocks, early, some, most, order, panel=32, micro=8):
    count, width, points = early.shape
    whole = pl.BlockSpec(memory_space=pltpu.VMEM)
    return pl.pallas_call(
        functools.partial(finish_body, panel=panel, micro=micro),
        in_specs=[whole] * 5,
        out_shape=(
            jax.ShapeDtypeStruct((count, points, width), bf16),
            jax.ShapeDtypeStruct((count, width, width), f32),
        ),
        scratch_shapes=[
            pltpu.VMEM((count, width, points), f32),
            pltpu.VMEM((count, width, width), f32),
            pltpu.VMEM((count, width, width), f32),
            pltpu.VMEM((2, 8 * panel, 128), f32),
            pltpu.VMEM((8 * panel, 128), f32),
        ],
        compiler_params=pltpu.CompilerParams(vmem_limit_bytes=28 * 2**20),
        name="finish",
    )(*(in_vmem(x) for x in (blocks, early, some, most)), order)


def in_vmem(x):
    return pltpu.with_memory_space_constraint(x, pltpu.VMEM)


def in_hbm(x):
    return pltpu.with_memory_space_constraint(x, pltpu.HBM)


PIECE_ROWS = 16


def prepare_body(offsets_any, sketch_any, full_ref, some_ref, most_ref, offsets_ref, sketch_ref, sems):
    count, points, width = sketch_ref.shape
    fetch = pltpu.make_async_copy(offsets_any, offsets_ref, sems.at[count])
    copies = [pltpu.make_async_copy(sketch_any.at[c], sketch_ref.at[c], sems.at[c]) for c in range(count)]
    fetch.start()
    for copy in copies:
        copy.start()
    fetch.wait()
    stacked = jnp.concatenate([offsets_ref[axis] for axis in range(3)], axis=0)
    stacked = jnp.concatenate([stacked, jnp.zeros((PIECE_ROWS - 3 * count, points), f32)], axis=0)
    parts = jnp.concatenate(pieces(stacked), axis=0).astype(bf16)
    full_ref[count * width:, :] = parts
    some_ref[count // 2 * width:, :] = parts
    for c in range(count):
        copies[c].wait()
        turned = sketch_ref[c].T
        full_ref[c * width:(c + 1) * width, :] = turned
        ref, at = (some_ref, c) if c < count // 2 else (most_ref, c - count // 2)
        ref[at * width:(at + 1) * width, :] = turned


def prepare(offsets, sketch):
    count, points, width = sketch.shape
    whole = pl.BlockSpec(memory_space=pltpu.VMEM)
    far = pl.BlockSpec(memory_space=pl.ANY)
    extra = 3 * PIECE_ROWS
    return pl.pallas_call(
        prepare_body,
        in_specs=[far, far],
        out_specs=[whole] * 3,
        out_shape=tuple(
            pltpu.VMEM((n, points), bf16) for n in (count * width + extra, count // 2 * width + extra, (count - count // 2) * width)
        ),
        scratch_shapes=[
            pltpu.VMEM(offsets.shape, f32),
            pltpu.VMEM(sketch.shape, bf16),
            pltpu.SemaphoreType.DMA((count + 1,)),
        ],
        compiler_params=pltpu.CompilerParams(vmem_limit_bytes=16 * 2**20),
        name="prepare",
    )(in_hbm(offsets), in_hbm(sketch))


class Pairs:
    def __init__(self, own_any, own_ref, pattern_any, pattern_ref, sems, partner_ref, window, listed, odd, total):
        count, points = own_ref.shape[1:]
        self.columns = pattern_ref.shape[1]
        self.count, self.window, self.listed = count, window, listed
        copies = [
            pltpu.make_async_copy(own_any, own_ref, sems.at[0]),
            pltpu.make_async_copy(pattern_any, pattern_ref, sems.at[1]),
        ]
        for copy in copies:
            copy.start()
        me = lax.axis_index(AXES)
        first = me * count
        side = lax.rem(me, 2)
        odd_group = 2 * side
        window[...] = jnp.zeros_like(window)
        base = partner_ref.shape[0] - 3 * PIECE_ROWS
        parts = [
            partner_ref[base + PIECE_ROWS * i:base + PIECE_ROWS * (i + 1), :].astype(f32) for i in range(3)
        ]
        partner = (parts[0] + parts[1]) + parts[2]
        for copy in copies:
            copy.wait()
        partner_group = odd_group if odd else 2 - odd_group
        for group, get in (
            (partner_group, lambda axis, at: partner[count * axis + at:count * axis + at + 1, :]),
            (1, lambda axis, at: own_ref[axis, at:at + 1, :]),
        ):
            for at in range(count):
                slot = group * count + at
                index = (first + (slot - count)).astype(f32)
                window[slot, 0:1, :] = (get(0, at) + index) - index
                window[slot, 1:2, :] = get(1, at)
                window[slot, 2:3, :] = get(2, at)

        def note(pair, found):
            cluster, column, distance = self.of(pair)
            source = cluster + distance
            group = jnp.where(source < 0, 0, jnp.where(source < count, 1, 2))
            counted = (pattern_ref[cluster, column] != 0) & (first + source >= 0) & (first + source < total)
            counted = counted & ((group == odd_group) if odd else (group != odd_group))
            listed[found] = pair
            return found + counted.astype(jnp.int32)

        self.found = lax.fori_loop(0, count * self.columns, note, jnp.int32(0))

    def of(self, pair):
        cluster, column = pair // self.columns, lax.rem(pair, self.columns)
        return cluster, column, column - W + jnp.where(column >= W - 1, 3, 0)

    def at(self, step):
        return self.of(self.listed[jnp.clip(step, 0, jnp.maximum(self.found - 1, 0))])

    def measure(self, step):
        cluster, _, distance = self.at(step)
        target = self.count + cluster
        a, b = split_points(self.window[target], self.window[target + distance], distance)
        return contract(b, a, 0, 0)


def early_body(pattern_any, own_any, full_ref, even_ref, out_ref, window, here, there, ka, kb, sketches, listed, own_ref, pattern_ref, sems, *, total):
    count, width, points = out_ref.shape
    copies = [
        pltpu.make_async_copy(ref.at[pl.ds(0, count * width)], sketches.at[pl.ds(i * count * width, count * width)], sems.at[2 + i])
        for i, ref in enumerate((full_ref, even_ref))
    ]
    for copy in copies:
        copy.start()
    pairs = Pairs(own_any, own_ref, pattern_any, pattern_ref, sems, even_ref, window, listed, False, total)
    out_ref[...] = jnp.zeros_like(out_ref)
    kb[...] = jnp.zeros_like(kb)
    here[...] = pairs.measure(jnp.int32(0))
    for copy in copies:
        copy.wait()

    def evaluate(squares, block):
        block[...] = kernel_values(squares[...], points).astype(bf16)

    def add(step, block):
        cluster, _, distance = pairs.at(step)
        source = cluster + distance
        slot = jnp.where(source < 0, source + 2 * count, source)
        rows_of = sketches[pl.ds(pl.multiple_of(slot * width, width), width), :]
        out_ref[cluster] += jnp.dot(rows_of, block[...], preferred_element_type=f32)

    def two_steps(twice, carry):
        at = 2 * twice
        there[...] = pairs.measure(at + 1)
        evaluate(here, ka)
        add(at - 1, kb)
        here[...] = pairs.measure(at + 2)
        evaluate(there, kb)
        add(at, ka)
        return carry

    lax.fori_loop(0, pairs.found // 2, two_steps, 0)
    add(pairs.found // 2 * 2 - 1, kb)

    @pl.when(lax.rem(pairs.found, 2) == 1)
    def _():
        evaluate(here, ka)
        add(pairs.found - 1, ka)


def late_body(pattern_any, own_any, odd_ref, out_ref, window, here, there, listed, own_ref, pattern_ref, sems, *, total):
    points = out_ref.shape[1]
    pairs = Pairs(own_any, own_ref, pattern_any, pattern_ref, sems, odd_ref, window, listed, True, total)
    out_ref[...] = jnp.zeros_like(out_ref)
    here[...] = pairs.measure(jnp.int32(0))
    half = pairs.columns // 2

    def evaluate(step, squares):
        cluster, column, _ = pairs.at(step)
        out_ref[half * cluster + lax.rem(column, half)] = kernel_values(squares[...], points).astype(bf16)

    def two_steps(twice, carry):
        at = 2 * twice
        there[...] = pairs.measure(at + 1)
        evaluate(at, here)
        here[...] = pairs.measure(at + 2)
        evaluate(at + 1, there)
        return carry

    lax.fori_loop(0, pairs.found // 2, two_steps, 0)

    @pl.when(lax.rem(pairs.found, 2) == 1)
    def _():
        evaluate(pairs.found - 1, here)


def block_call(kernel, name, share, pattern, own, arrays, shape, dtype, extra):
    count, points = own.shape[1:]
    values = share * pattern.size * points * points // 8
    whole = pl.BlockSpec(memory_space=pltpu.VMEM)
    far = pl.BlockSpec(memory_space=pl.ANY)
    return pl.pallas_call(
        kernel,
        in_specs=[far, far] + [whole] * len(arrays),
        out_specs=whole,
        scratch_shapes=[
            pltpu.VMEM((3 * count, 8, points), f32),
            pltpu.VMEM((points, points), f32),
            pltpu.VMEM((points, points), f32),
            *extra,
            pltpu.SMEM((pattern.size + 1,), jnp.int32),
            pltpu.VMEM(own.shape, f32),
            pltpu.SMEM(pattern.shape, jnp.int32),
            pltpu.SemaphoreType.DMA((4,)),
        ],
        out_shape=pltpu.VMEM(shape, dtype),
        cost_estimate=pl.CostEstimate(flops=40 * values, bytes_accessed=2 * values, transcendentals=3 * values),
        compiler_params=pltpu.CompilerParams(vmem_limit_bytes=16 * 2**20),
        name=name,
    )(in_hbm(pattern), in_hbm(own), *(in_vmem(x) for x in arrays))


def body(offsets, sketch, pattern, point_order):
    count, points, width = sketch.shape
    total = count * lax.axis_size(AXES)
    offsets = offsets.transpose(1, 0, 2)
    full, some, most = prepare(offsets, sketch)
    even_full = exchanged(full, 0)
    odd_some = exchanged(some, 1)
    odd_most = exchanged(most, 1)
    block = pltpu.VMEM((points, points), bf16)
    early = block_call(
        functools.partial(early_body, total=total), "early", 5, pattern, offsets, (full, even_full),
        (count, width, points), f32, [block, block, pltpu.VMEM((2 * count * width, points), bf16)],
    )
    odd_some, early = lax.optimization_barrier((odd_some, early))
    late = block_call(
        functools.partial(late_body, total=total), "late", 3, pattern, offsets, (odd_some,),
        (pattern.size // 2, points, points), bf16, [],
    )
    return finish(late, early, odd_some, odd_most, point_order)


def solution(mesh):
    rows = P(AXES, None, None)
    flat = P(AXES, None)
    return jax.shard_map(
        body,
        mesh=mesh,
        in_specs=(rows, rows, flat, flat),
        out_specs=(rows, rows),
        check_vma=False,
    )
```

```python
import functools
import math

import jax
import jax.numpy as jnp
from jax import lax
from jax.experimental import pallas as pl
from jax.experimental.pallas import tpu as pltpu
from jax.sharding import PartitionSpec as P

W = 4
AXES = ("grp", "dev")
f32 = jnp.float32
bf16 = jnp.bfloat16

wave_number = 40.0
decay_length = 4.0
softening = 0.5
turns = wave_number / (2.0 * math.pi)

SINE = (4.44287957, -7.30781674, 3.5977744, -0.79119941)


def exchanged(array, start):
    peers = lax.axis_size(AXES)
    pairs = [(i, i + 1) for i in range(start, peers - 1, 2)]
    return lax.ppermute(array, AXES, pairs + [(j, i) for i, j in pairs])


def offset_table(reach):
    return [-value for value in range(reach, 1, -1)] + list(range(2, reach + 1))


def kernel_values(turn_squared, points):
    scale = turns / math.sqrt(points)
    turn = turn_squared * lax.rsqrt(turn_squared)
    part = turn - jnp.round(turn)
    square = part * part
    sine = f32(SINE[-1] * math.sqrt(scale))
    for value in SINE[-2::-1]:
        sine = sine * square + f32(value * math.sqrt(scale))
    sine = sine * part
    level = jnp.exp2(turn * f32(-math.log2(math.e) / (decay_length * turns)))
    level = level * pltpu.reciprocal(turn + f32(softening * turns), approx=True)
    return level * (f32(scale) - sine * sine)


def pieces(x):
    high = x.astype(bf16).astype(f32)
    middle = (x - high).astype(bf16).astype(f32)
    low = (x - high - middle).astype(bf16).astype(f32)
    return high, middle, low


def split_points(target, source, distance):
    row = lax.broadcasted_iota(jnp.int32, target.shape, 0)
    half = distance.astype(f32) * f32(0.5)

    def shifted(x, along):
        moved = x + jnp.where(row == 0, along, jnp.where(row < 3, f32(-0.5), f32(0)))
        moved = moved * f32(turns)
        return moved, jnp.sum(moved * moved, axis=0, keepdims=True)

    left, left_norm = shifted(target, -half - f32(0.5))
    right, right_norm = shifted(source, half - f32(0.5))
    left = jnp.where(row == 3, left_norm, jnp.where(row == 4, f32(1), left))
    right = jnp.where(row == 4, right_norm, jnp.where(row == 3, f32(1), f32(-2) * right))
    lh, lm, ll = pieces(left)
    rh, rm, rl = pieces(right)
    a = jnp.concatenate([lh, lh, lm, lm, lh, ll, lm, ll], axis=0).astype(bf16)
    b = jnp.concatenate([rh, rm, rh, rm, rl, rh, rl, rm], axis=0).astype(bf16)
    return a, b


def halves(x):
    hi = x.astype(bf16)
    return hi, (x - hi.astype(f32)).astype(bf16)

def contract(a, b, da, db):
    return lax.dot_general(a, b, (((da,), (db,)), ((), ())), preferred_element_type=f32)

def lane_of(x, lane):
    return jnp.broadcast_to(x[:, lane:lane + 1], x.shape)

def factor_panel(rows, ups, first, panel, micro):
    half = first // 128
    base = first % 128
    pair = micro // 2
    lanes = lax.broadcasted_iota(jnp.int32, (8, 128), 1)
    lower = lax.broadcasted_iota(jnp.int32, (8, 128), 0) < 4

    def packed(x, y):
        return jnp.where(lower, x, pltpu.roll(y, 4, axis=0))

    for start in range(0, panel, micro):
        lane0 = base + start
        inside = (lanes >= lane0) & (lanes < lane0 + micro)
        raw = [rows[half, 8 * (start + j):8 * (start + j) + 8, :] for j in range(micro)]
        other = [rows[1 - half, 8 * (start + j):8 * (start + j) + 8, :] for j in range(micro)]
        a = [[None] * micro for _ in range(micro)]
        for i in range(pair):
            both = packed(raw[i], raw[i + pair])
            for k in range(i + pair + 1):
                value = lane_of(both, lane0 + k)
                if k <= i:
                    a[i][k] = value
                a[i + pair][k] = pltpu.roll(value, 4, axis=0)
        low = [[None] * micro for _ in range(micro)]
        inv = [None] * micro
        for k in range(micro):
            inv[k] = lax.rsqrt(a[k][k])
            for i in range(k + 1, micro):
                low[i][k] = a[i][k] * inv[k]
            for i in range(k + 1, micro):
                for m in range(k + 1, i + 1):
                    a[i][m] = a[i][m] - low[i][k] * low[m][k]
        solved = [jnp.where(inside, jnp.where(lanes == lane0 + j, f32(1), f32(0)), raw[j]) for j in range(micro)]
        for k in range(micro):
            raw[k] = raw[k] * inv[k]
            solved[k] = solved[k] * inv[k]
            other[k] = other[k] * inv[k]
            for i in range(k + 1, micro):
                raw[i] = raw[i] - low[i][k] * raw[k]
                solved[i] = solved[i] - low[i][k] * solved[k]
                other[i] = other[i] - low[i][k] * other[k]
        for j in range(micro):
            at = slice(8 * (start + j), 8 * (start + j) + 8)
            ups[at, :] = raw[j]
            rows[half, at, :] = solved[j]
            rows[1 - half, at, :] = other[j]
        if start + micro < panel:
            raw = [packed(raw[j], raw[j + pair]) for j in range(pair)]
            solved = [packed(solved[j], solved[j + pair]) for j in range(pair)]
            other = [packed(other[j], other[j + pair]) for j in range(pair)]
        for i in range(start + micro, panel):
            at = slice(8 * i, 8 * i + 8)
            x = jnp.where(inside, f32(0), rows[half, at, :])
            y = rows[1 - half, at, :]
            tx = ty = None
            for j in range(pair):
                c = lane_of(raw[j], base + i)
                tx = c * solved[j] if tx is None else tx + c * solved[j]
                ty = c * other[j] if ty is None else ty + c * other[j]
            rows[half, at, :] = x - (tx + pltpu.roll(tx, 4, axis=0))
            rows[1 - half, at, :] = y - (ty + pltpu.roll(ty, 4, axis=0))

def finish_body(k_ref, early_ref, odd_ref, order_ref, basis_ref, factor_ref, t_ref, mat, inv_ref, rows, ups, *, panel, micro):
    count, width, points = early_ref.shape
    row_id = lax.broadcasted_iota(jnp.int32, (width, width), 0)
    col_id = lax.broadcasted_iota(jnp.int32, (width, width), 1)

    def fill(columns, shift):
        for c in range(count):
            samples = early_ref[c]
            for column in columns:
                slot = c + offset_table(W)[column] + shift
                if 0 <= slot < count:
                    rows_of = odd_ref[slot * width:(slot + 1) * width, :]
                    block = k_ref[len(columns) * c + column % len(columns)]
                    samples = samples + jnp.dot(rows_of, block, preferred_element_type=f32)
            t_ref[c] = samples

    side = lax.rem(lax.axis_index(AXES), 2)
    reach = len(offset_table(W)) // 2
    pl.when(side == 1)(lambda: fill(range(reach, 2 * reach), -count))
    pl.when(side == 0)(lambda: fill(range(reach), count))
    for c in range(count):
        hi, lo = halves(t_ref[c])
        gram = contract(jnp.concatenate([hi, hi, lo], axis=1), jnp.concatenate([hi, lo, hi], axis=1), 1, 1)
        shift = f32(0.01) * jnp.sum(jnp.where(row_id == col_id, gram, f32(0))) / f32(width) + f32(1e-5)
        mat[c] = gram + jnp.where(row_id == col_id, shift, f32(0))
    for first in range(0, width, panel):
        half = first // 128
        base = first % 128
        for c in range(count):
            for h in range(2):
                for t in range(0, panel, 8):
                    tile = mat[c, first + t:first + t + 8, 128 * h:128 * h + 128]
                    rows[h, pl.ds(8 * t + c, 8, stride=8), :] = tile
        factor_panel(rows, ups, first, panel, micro)
        prow = lax.broadcasted_iota(jnp.int32, (panel, 128), 0) + base
        pcol = lax.broadcasted_iota(jnp.int32, (panel, 128), 1)
        for c in range(count):
            z = [rows[h, pl.ds(c, panel, stride=8), :] for h in range(2)]
            u = ups[pl.ds(c, panel, stride=8), :]
            u = jnp.where(pcol >= prow, u, f32(0))
            wz = jnp.where((pcol <= prow) | (pcol >= base + panel), z[half], f32(0))
            w = jnp.where(pcol <= prow, z[half], f32(0))
            z[half] = wz
            factor_ref[c, first:first + panel, 128 * half:128 * half + 128] = u
            factor_ref[c, first:first + panel, 128 * (1 - half):128 * (1 - half) + 128] = z[1] if half == 0 else jnp.zeros_like(u)
            inv_ref[c, first:first + panel, 128 * half:128 * half + 128] = w
            inv_ref[c, first:first + panel, 128 * (1 - half):128 * (1 - half) + 128] = z[0] if half == 1 else jnp.zeros_like(u)
            rest = first + panel
            if rest < width:
                zz = jnp.concatenate(z, axis=1)
                hi, lo = halves(zz)
                left = jnp.concatenate([hi, hi, lo], axis=0)
                right = jnp.concatenate([hi, lo, hi], axis=0)
                off = (rest // 128) * 128
                prod = contract(left[:, off:], right, 0, 0)[rest - off:, :]
                old = mat[c, rest:, :]
                cc = col_id[rest:, :]
                old = jnp.where((cc >= first) & (cc < rest), f32(0), old)
                mat[c, rest:, :] = old - prod
    for c in range(count):
        hi, lo = halves(t_ref[c])
        wh, wl = halves(inv_ref[c])
        b = jnp.dot(jnp.concatenate([wh, wh, wl], axis=1), jnp.concatenate([hi, lo, hi], axis=0), preferred_element_type=f32).astype(bf16)
        order_t = jnp.broadcast_to(order_ref[c:c + 1, :].astype(f32), (128, points)).T
        place = lax.broadcasted_iota(jnp.int32, (points, 128), 1).astype(f32)
        pick = jnp.concatenate([jnp.where(order_t == place + f32(128 * q), f32(1), f32(0)).astype(bf16) for q in range(points // 128)], axis=1)
        basis_ref[c] = contract(pick, b, 1, 1).astype(bf16)

def finish(blocks, early, odd, order, panel=32, micro=8):
    count, width, points = early.shape
    whole = pl.BlockSpec(memory_space=pltpu.VMEM)
    return pl.pallas_call(
        functools.partial(finish_body, panel=panel, micro=micro),
        in_specs=[whole] * 4,
        out_shape=(
            jax.ShapeDtypeStruct((count, points, width), bf16),
            jax.ShapeDtypeStruct((count, width, width), f32),
        ),
        scratch_shapes=[
            pltpu.VMEM((count, width, points), f32),
            pltpu.VMEM((count, width, width), f32),
            pltpu.VMEM((count, width, width), f32),
            pltpu.VMEM((2, 8 * panel, 128), f32),
            pltpu.VMEM((8 * panel, 128), f32),
        ],
        compiler_params=pltpu.CompilerParams(vmem_limit_bytes=28 * 2**20),
        name="finish",
    )(*(in_vmem(x) for x in (blocks, early, odd)), order)


def in_vmem(x):
    return pltpu.with_memory_space_constraint(x, pltpu.VMEM)


def in_hbm(x):
    return pltpu.with_memory_space_constraint(x, pltpu.HBM)


PIECE_ROWS = 16


def prepare_body(offsets_any, sketch_any, full_ref, turned_ref, offsets_ref, sketch_ref, sems):
    count, points, width = sketch_ref.shape
    fetch = pltpu.make_async_copy(offsets_any, offsets_ref, sems.at[count])
    copies = [pltpu.make_async_copy(sketch_any.at[c], sketch_ref.at[c], sems.at[c]) for c in range(count)]
    fetch.start()
    for copy in copies:
        copy.start()
    fetch.wait()
    stacked = jnp.concatenate([offsets_ref[axis] for axis in range(3)], axis=0)
    stacked = jnp.concatenate([stacked, jnp.zeros((PIECE_ROWS - 3 * count, points), f32)], axis=0)
    parts = jnp.concatenate(pieces(stacked), axis=0).astype(bf16)
    full_ref[count * width:, :] = parts
    for c in range(count):
        copies[c].wait()
        turned = sketch_ref[c].T
        full_ref[c * width:(c + 1) * width, :] = turned
        turned_ref[c * width:(c + 1) * width, :] = turned


def prepare(offsets, sketch):
    count, points, width = sketch.shape
    whole = pl.BlockSpec(memory_space=pltpu.VMEM)
    far = pl.BlockSpec(memory_space=pl.ANY)
    return pl.pallas_call(
        prepare_body,
        in_specs=[far, far],
        out_specs=[whole] * 2,
        out_shape=tuple(pltpu.VMEM((count * width + more, points), bf16) for more in (3 * PIECE_ROWS, 0)),
        scratch_shapes=[
            pltpu.VMEM(offsets.shape, f32),
            pltpu.VMEM(sketch.shape, bf16),
            pltpu.SemaphoreType.DMA((count + 1,)),
        ],
        compiler_params=pltpu.CompilerParams(vmem_limit_bytes=16 * 2**20),
        name="prepare",
    )(in_hbm(offsets), in_hbm(sketch))


class Pairs:
    def __init__(self, own_any, own_ref, pattern_any, pattern_ref, sems, partner_ref, window, listed, odd, total):
        count, points = own_ref.shape[1:]
        self.columns = pattern_ref.shape[1]
        self.count, self.window, self.listed = count, window, listed
        copies = [
            pltpu.make_async_copy(own_any, own_ref, sems.at[0]),
            pltpu.make_async_copy(pattern_any, pattern_ref, sems.at[1]),
        ]
        for copy in copies:
            copy.start()
        me = lax.axis_index(AXES)
        first = me * count
        side = lax.rem(me, 2)
        odd_group = 2 * side
        window[...] = jnp.zeros_like(window)
        if odd:
            partner = [partner_ref[axis] for axis in range(3)]
        else:
            base = partner_ref.shape[0] - 3 * PIECE_ROWS
            parts = [
                partner_ref[base + PIECE_ROWS * i:base + PIECE_ROWS * (i + 1), :].astype(f32) for i in range(3)
            ]
            joined = (parts[0] + parts[1]) + parts[2]
            partner = [joined[count * axis:count * (axis + 1)] for axis in range(3)]
        for copy in copies:
            copy.wait()
        partner_group = odd_group if odd else 2 - odd_group
        for group, get in (
            (partner_group, lambda axis, at: partner[axis][at:at + 1, :]),
            (1, lambda axis, at: own_ref[axis, at:at + 1, :]),
        ):
            for at in range(count):
                slot = group * count + at
                index = (first + (slot - count)).astype(f32)
                window[slot, 0:1, :] = (get(0, at) + index) - index
                window[slot, 1:2, :] = get(1, at)
                window[slot, 2:3, :] = get(2, at)

        def note(pair, found):
            cluster, column, distance = self.of(pair)
            source = cluster + distance
            group = jnp.where(source < 0, 0, jnp.where(source < count, 1, 2))
            counted = (pattern_ref[cluster, column] != 0) & (first + source >= 0) & (first + source < total)
            counted = counted & ((group == odd_group) if odd else (group != odd_group))
            listed[found] = pair
            return found + counted.astype(jnp.int32)

        self.found = lax.fori_loop(0, count * self.columns, note, jnp.int32(0))

    def of(self, pair):
        cluster, column = pair // self.columns, lax.rem(pair, self.columns)
        return cluster, column, column - W + jnp.where(column >= W - 1, 3, 0)

    def at(self, step):
        return self.of(self.listed[jnp.clip(step, 0, jnp.maximum(self.found - 1, 0))])

    def measure(self, step):
        cluster, _, distance = self.at(step)
        target = self.count + cluster
        a, b = split_points(self.window[target], self.window[target + distance], distance)
        return contract(b, a, 0, 0)


def early_body(pattern_any, own_any, full_ref, even_ref, out_ref, window, here, there, ka, kb, sketches, listed, own_ref, pattern_ref, sems, *, total):
    count, width, points = out_ref.shape
    copies = [
        pltpu.make_async_copy(ref.at[pl.ds(0, count * width)], sketches.at[pl.ds(i * count * width, count * width)], sems.at[2 + i])
        for i, ref in enumerate((full_ref, even_ref))
    ]
    for copy in copies:
        copy.start()
    pairs = Pairs(own_any, own_ref, pattern_any, pattern_ref, sems, even_ref, window, listed, False, total)
    out_ref[...] = jnp.zeros_like(out_ref)
    kb[...] = jnp.zeros_like(kb)
    here[...] = pairs.measure(jnp.int32(0))
    for copy in copies:
        copy.wait()

    def evaluate(squares, block):
        block[...] = kernel_values(squares[...], points).astype(bf16)

    def add(step, block):
        cluster, _, distance = pairs.at(step)
        source = cluster + distance
        slot = jnp.where(source < 0, source + 2 * count, source)
        rows_of = sketches[pl.ds(pl.multiple_of(slot * width, width), width), :]
        out_ref[cluster] += jnp.dot(rows_of, block[...], preferred_element_type=f32)

    def two_steps(twice, carry):
        at = 2 * twice
        there[...] = pairs.measure(at + 1)
        evaluate(here, ka)
        add(at - 1, kb)
        here[...] = pairs.measure(at + 2)
        evaluate(there, kb)
        add(at, ka)
        return carry

    lax.fori_loop(0, pairs.found // 2, two_steps, 0)
    add(pairs.found // 2 * 2 - 1, kb)

    @pl.when(lax.rem(pairs.found, 2) == 1)
    def _():
        evaluate(here, ka)
        add(pairs.found - 1, ka)


def late_body(pattern_any, own_any, odd_ref, out_ref, window, here, there, listed, own_ref, pattern_ref, sems, *, total):
    points = out_ref.shape[1]
    pairs = Pairs(own_any, own_ref, pattern_any, pattern_ref, sems, odd_ref, window, listed, True, total)
    out_ref[...] = jnp.zeros_like(out_ref)
    here[...] = pairs.measure(jnp.int32(0))
    half = pairs.columns // 2

    def evaluate(step, squares):
        cluster, column, _ = pairs.at(step)
        out_ref[half * cluster + lax.rem(column, half)] = kernel_values(squares[...], points).astype(bf16)

    def two_steps(twice, carry):
        at = 2 * twice
        there[...] = pairs.measure(at + 1)
        evaluate(at, here)
        here[...] = pairs.measure(at + 2)
        evaluate(at + 1, there)
        return carry

    lax.fori_loop(0, pairs.found // 2, two_steps, 0)

    @pl.when(lax.rem(pairs.found, 2) == 1)
    def _():
        evaluate(pairs.found - 1, here)


def block_call(kernel, name, share, pattern, own, arrays, shape, dtype, extra):
    count, points = own.shape[1:]
    values = share * pattern.size * points * points // 8
    whole = pl.BlockSpec(memory_space=pltpu.VMEM)
    far = pl.BlockSpec(memory_space=pl.ANY)
    return pl.pallas_call(
        kernel,
        in_specs=[far, far] + [whole] * len(arrays),
        out_specs=whole,
        scratch_shapes=[
            pltpu.VMEM((3 * count, 8, points), f32),
            pltpu.VMEM((points, points), f32),
            pltpu.VMEM((points, points), f32),
            *extra,
            pltpu.SMEM((pattern.size + 1,), jnp.int32),
            pltpu.VMEM(own.shape, f32),
            pltpu.SMEM(pattern.shape, jnp.int32),
            pltpu.SemaphoreType.DMA((4,)),
        ],
        out_shape=pltpu.VMEM(shape, dtype),
        cost_estimate=pl.CostEstimate(flops=40 * values, bytes_accessed=2 * values, transcendentals=3 * values),
        compiler_params=pltpu.CompilerParams(vmem_limit_bytes=16 * 2**20),
        name=name,
    )(in_hbm(pattern), in_hbm(own), *(in_vmem(x) for x in arrays))


def body(offsets, sketch, pattern, point_order):
    count, points, width = sketch.shape
    total = count * lax.axis_size(AXES)
    offsets = offsets.transpose(1, 0, 2)
    odd_offsets = exchanged(offsets, 1)
    full, turned = prepare(offsets, sketch)
    full, turned, odd_offsets = lax.optimization_barrier((full, turned, odd_offsets))
    even_full = exchanged(full, 0)
    odd_turned = exchanged(turned, 1)
    block = pltpu.VMEM((points, points), bf16)
    early = block_call(
        functools.partial(early_body, total=total), "early", 5, pattern, offsets, (full, even_full),
        (count, width, points), f32, [block, block, pltpu.VMEM((2 * count * width, points), bf16)],
    )
    odd_offsets, early = lax.optimization_barrier((odd_offsets, early))
    late = block_call(
        functools.partial(late_body, total=total), "late", 3, pattern, offsets, (odd_offsets,),
        (pattern.size // 2, points, points), bf16, [],
    )
    return finish(late, early, odd_turned, point_order)


def solution(mesh):
    rows = P(AXES, None, None)
    flat = P(AXES, None)
    return jax.shard_map(
        body,
        mesh=mesh,
        in_specs=(rows, rows, flat, flat),
        out_specs=(rows, rows),
        check_vma=False,
    )
```

```python
import functools
import math

import jax
import jax.numpy as jnp
from jax import lax
from jax.experimental import pallas as pl
from jax.experimental.pallas import tpu as pltpu
from jax.sharding import PartitionSpec as P

W = 4
AXES = ("grp", "dev")
f32 = jnp.float32
bf16 = jnp.bfloat16

wave_number = 40.0
decay_length = 4.0
softening = 0.5
turns = wave_number / (2.0 * math.pi)

SINE = (4.44287957, -7.30781674, 3.5977744, -0.79119941)


def exchanged(array, start):
    peers = lax.axis_size(AXES)
    pairs = [(i, i + 1) for i in range(start, peers - 1, 2)]
    return lax.ppermute(array, AXES, pairs + [(j, i) for i, j in pairs])


def offset_table(reach):
    return [-value for value in range(reach, 1, -1)] + list(range(2, reach + 1))


def kernel_values(turn_squared, points):
    scale = turns / math.sqrt(points)
    turn = turn_squared * lax.rsqrt(turn_squared)
    part = turn - jnp.round(turn)
    square = part * part
    sine = f32(SINE[-1] * math.sqrt(scale))
    for value in SINE[-2::-1]:
        sine = sine * square + f32(value * math.sqrt(scale))
    sine = sine * part
    level = jnp.exp2(turn * f32(-math.log2(math.e) / (decay_length * turns)))
    level = level * pltpu.reciprocal(turn + f32(softening * turns), approx=True)
    return level * (f32(scale) - sine * sine)


def pieces(x):
    high = x.astype(bf16).astype(f32)
    middle = (x - high).astype(bf16).astype(f32)
    low = (x - high - middle).astype(bf16).astype(f32)
    return high, middle, low


def split_points(target, source, distance):
    row = lax.broadcasted_iota(jnp.int32, target.shape, 0)
    half = distance.astype(f32) * f32(0.5)

    def shifted(x, along):
        moved = x + jnp.where(row == 0, along, jnp.where(row < 3, f32(-0.5), f32(0)))
        moved = moved * f32(turns)
        return moved, jnp.sum(moved * moved, axis=0, keepdims=True)

    left, left_norm = shifted(target, -half - f32(0.5))
    right, right_norm = shifted(source, half - f32(0.5))
    left = jnp.where(row == 3, left_norm, jnp.where(row == 4, f32(1), left))
    right = jnp.where(row == 4, right_norm, jnp.where(row == 3, f32(1), f32(-2) * right))
    lh, lm, ll = pieces(left)
    rh, rm, rl = pieces(right)
    a = jnp.concatenate([lh, lh, lm, lm, lh, ll, lm, ll], axis=0).astype(bf16)
    b = jnp.concatenate([rh, rm, rh, rm, rl, rh, rl, rm], axis=0).astype(bf16)
    return a, b


def halves(x):
    hi = x.astype(bf16)
    return hi, (x - hi.astype(f32)).astype(bf16)

def contract(a, b, da, db):
    return lax.dot_general(a, b, (((da,), (db,)), ((), ())), preferred_element_type=f32)

def lane_of(x, lane):
    return jnp.broadcast_to(x[:, lane:lane + 1], x.shape)

def factor_panel(rows, ups, first, panel, micro):
    half = first // 128
    base = first % 128
    pair = micro // 2
    lanes = lax.broadcasted_iota(jnp.int32, (8, 128), 1)
    lower = lax.broadcasted_iota(jnp.int32, (8, 128), 0) < 4

    def packed(x, y):
        return jnp.where(lower, x, pltpu.roll(y, 4, axis=0))

    for start in range(0, panel, micro):
        lane0 = base + start
        inside = (lanes >= lane0) & (lanes < lane0 + micro)
        raw = [rows[half, 8 * (start + j):8 * (start + j) + 8, :] for j in range(micro)]
        other = [rows[1 - half, 8 * (start + j):8 * (start + j) + 8, :] for j in range(micro)]
        a = [[None] * micro for _ in range(micro)]
        for i in range(pair):
            both = packed(raw[i], raw[i + pair])
            for k in range(i + pair + 1):
                value = lane_of(both, lane0 + k)
                if k <= i:
                    a[i][k] = value
                a[i + pair][k] = pltpu.roll(value, 4, axis=0)
        low = [[None] * micro for _ in range(micro)]
        inv = [None] * micro
        for k in range(micro):
            inv[k] = lax.rsqrt(a[k][k])
            for i in range(k + 1, micro):
                low[i][k] = a[i][k] * inv[k]
            for i in range(k + 1, micro):
                for m in range(k + 1, i + 1):
                    a[i][m] = a[i][m] - low[i][k] * low[m][k]
        solved = [jnp.where(inside, jnp.where(lanes == lane0 + j, f32(1), f32(0)), raw[j]) for j in range(micro)]
        for k in range(micro):
            raw[k] = raw[k] * inv[k]
            solved[k] = solved[k] * inv[k]
            other[k] = other[k] * inv[k]
            for i in range(k + 1, micro):
                raw[i] = raw[i] - low[i][k] * raw[k]
                solved[i] = solved[i] - low[i][k] * solved[k]
                other[i] = other[i] - low[i][k] * other[k]
        for j in range(micro):
            at = slice(8 * (start + j), 8 * (start + j) + 8)
            ups[at, :] = raw[j]
            rows[half, at, :] = solved[j]
            rows[1 - half, at, :] = other[j]
        if start + micro < panel:
            raw = [packed(raw[j], raw[j + pair]) for j in range(pair)]
            solved = [packed(solved[j], solved[j + pair]) for j in range(pair)]
            other = [packed(other[j], other[j + pair]) for j in range(pair)]
        for i in range(start + micro, panel):
            at = slice(8 * i, 8 * i + 8)
            x = jnp.where(inside, f32(0), rows[half, at, :])
            y = rows[1 - half, at, :]
            tx = ty = None
            for j in range(pair):
                c = lane_of(raw[j], base + i)
                tx = c * solved[j] if tx is None else tx + c * solved[j]
                ty = c * other[j] if ty is None else ty + c * other[j]
            rows[half, at, :] = x - (tx + pltpu.roll(tx, 4, axis=0))
            rows[1 - half, at, :] = y - (ty + pltpu.roll(ty, 4, axis=0))

def finish_body(k_ref, early_ref, some_ref, most_ref, order_ref, basis_ref, factor_ref, t_ref, mat, inv_ref, rows, ups, *, panel, micro):
    count, width, points = early_ref.shape
    row_id = lax.broadcasted_iota(jnp.int32, (width, width), 0)
    col_id = lax.broadcasted_iota(jnp.int32, (width, width), 1)

    def fill(columns, shift):
        for c in range(count):
            samples = early_ref[c]
            for column in columns:
                slot = c + offset_table(W)[column] + shift
                if 0 <= slot < count:
                    at = slot * width
                    rows_of = most_ref[at:at + width, :] if slot < count - 1 else some_ref[:width, :]
                    block = k_ref[len(columns) * c + column % len(columns)]
                    samples = samples + jnp.dot(rows_of, block, preferred_element_type=f32)
            t_ref[c] = samples

    side = lax.rem(lax.axis_index(AXES), 2)
    reach = len(offset_table(W)) // 2
    pl.when(side == 1)(lambda: fill(range(reach, 2 * reach), -count))
    pl.when(side == 0)(lambda: fill(range(reach), count))
    for c in range(count):
        hi, lo = halves(t_ref[c])
        gram = contract(jnp.concatenate([hi, hi, lo], axis=1), jnp.concatenate([hi, lo, hi], axis=1), 1, 1)
        shift = f32(0.01) * jnp.sum(jnp.where(row_id == col_id, gram, f32(0))) / f32(width) + f32(1e-5)
        mat[c] = gram + jnp.where(row_id == col_id, shift, f32(0))
    for first in range(0, width, panel):
        half = first // 128
        base = first % 128
        for c in range(count):
            for h in range(2):
                for t in range(0, panel, 8):
                    tile = mat[c, first + t:first + t + 8, 128 * h:128 * h + 128]
                    rows[h, pl.ds(8 * t + c, 8, stride=8), :] = tile
        factor_panel(rows, ups, first, panel, micro)
        prow = lax.broadcasted_iota(jnp.int32, (panel, 128), 0) + base
        pcol = lax.broadcasted_iota(jnp.int32, (panel, 128), 1)
        for c in range(count):
            z = [rows[h, pl.ds(c, panel, stride=8), :] for h in range(2)]
            u = ups[pl.ds(c, panel, stride=8), :]
            u = jnp.where(pcol >= prow, u, f32(0))
            wz = jnp.where((pcol <= prow) | (pcol >= base + panel), z[half], f32(0))
            w = jnp.where(pcol <= prow, z[half], f32(0))
            z[half] = wz
            factor_ref[c, first:first + panel, 128 * half:128 * half + 128] = u
            factor_ref[c, first:first + panel, 128 * (1 - half):128 * (1 - half) + 128] = z[1] if half == 0 else jnp.zeros_like(u)
            inv_ref[c, first:first + panel, 128 * half:128 * half + 128] = w
            inv_ref[c, first:first + panel, 128 * (1 - half):128 * (1 - half) + 128] = z[0] if half == 1 else jnp.zeros_like(u)
            rest = first + panel
            if rest < width:
                zz = jnp.concatenate(z, axis=1)
                hi, lo = halves(zz)
                left = jnp.concatenate([hi, hi, lo], axis=0)
                right = jnp.concatenate([hi, lo, hi], axis=0)
                off = (rest // 128) * 128
                prod = contract(left[:, off:], right, 0, 0)[rest - off:, :]
                old = mat[c, rest:, :]
                cc = col_id[rest:, :]
                old = jnp.where((cc >= first) & (cc < rest), f32(0), old)
                mat[c, rest:, :] = old - prod
    for c in range(count):
        hi, lo = halves(t_ref[c])
        wh, wl = halves(inv_ref[c])
        b = jnp.dot(jnp.concatenate([wh, wh, wl], axis=1), jnp.concatenate([hi, lo, hi], axis=0), preferred_element_type=f32).astype(bf16)
        order_t = jnp.broadcast_to(order_ref[c:c + 1, :].astype(f32), (128, points)).T
        place = lax.broadcasted_iota(jnp.int32, (points, 128), 1).astype(f32)
        pick = jnp.concatenate([jnp.where(order_t == place + f32(128 * q), f32(1), f32(0)).astype(bf16) for q in range(points // 128)], axis=1)
        basis_ref[c] = contract(pick, b, 1, 1).astype(bf16)

def finish(blocks, early, some, most, order, panel=32, micro=8):
    count, width, points = early.shape
    whole = pl.BlockSpec(memory_space=pltpu.VMEM)
    return pl.pallas_call(
        functools.partial(finish_body, panel=panel, micro=micro),
        in_specs=[whole] * 5,
        out_shape=(
            jax.ShapeDtypeStruct((count, points, width), bf16),
            jax.ShapeDtypeStruct((count, width, width), f32),
        ),
        scratch_shapes=[
            pltpu.VMEM((count, width, points), f32),
            pltpu.VMEM((count, width, width), f32),
            pltpu.VMEM((count, width, width), f32),
            pltpu.VMEM((2, 8 * panel, 128), f32),
            pltpu.VMEM((8 * panel, 128), f32),
        ],
        compiler_params=pltpu.CompilerParams(vmem_limit_bytes=28 * 2**20),
        name="finish",
    )(*(in_vmem(x) for x in (blocks, early, some, most)), order)


def in_vmem(x):
    return pltpu.with_memory_space_constraint(x, pltpu.VMEM)


def in_hbm(x):
    return pltpu.with_memory_space_constraint(x, pltpu.HBM)


PIECE_ROWS = 16


def prepare_body(offsets_any, sketch_any, full_ref, some_ref, most_ref, offsets_ref, sketch_ref, sems):
    count, points, width = sketch_ref.shape
    fetch = pltpu.make_async_copy(offsets_any, offsets_ref, sems.at[count])
    copies = [pltpu.make_async_copy(sketch_any.at[c], sketch_ref.at[c], sems.at[c]) for c in range(count)]
    fetch.start()
    for copy in copies:
        copy.start()
    fetch.wait()
    stacked = jnp.concatenate([offsets_ref[axis] for axis in range(3)], axis=0)
    stacked = jnp.concatenate([stacked, jnp.zeros((PIECE_ROWS - 3 * count, points), f32)], axis=0)
    parts = jnp.concatenate(pieces(stacked), axis=0).astype(bf16)
    full_ref[count * width:, :] = parts
    some_ref[width:, :] = parts
    for c in range(count):
        copies[c].wait()
        turned = sketch_ref[c].T
        full_ref[c * width:(c + 1) * width, :] = turned
        if c < count - 1:
            most_ref[c * width:(c + 1) * width, :] = turned
        else:
            some_ref[:width, :] = turned


def prepare(offsets, sketch):
    count, points, width = sketch.shape
    whole = pl.BlockSpec(memory_space=pltpu.VMEM)
    far = pl.BlockSpec(memory_space=pl.ANY)
    extra = 3 * PIECE_ROWS
    return pl.pallas_call(
        prepare_body,
        in_specs=[far, far],
        out_specs=[whole] * 3,
        out_shape=tuple(
            pltpu.VMEM((n, points), bf16) for n in (count * width + extra, width + extra, (count - 1) * width)
        ),
        scratch_shapes=[
            pltpu.VMEM(offsets.shape, f32),
            pltpu.VMEM(sketch.shape, bf16),
            pltpu.SemaphoreType.DMA((count + 1,)),
        ],
        compiler_params=pltpu.CompilerParams(vmem_limit_bytes=16 * 2**20),
        name="prepare",
    )(in_hbm(offsets), in_hbm(sketch))


class Pairs:
    def __init__(self, own_any, own_ref, pattern_any, pattern_ref, sems, partner_ref, window, listed, odd, total):
        count, points = own_ref.shape[1:]
        self.columns = pattern_ref.shape[1]
        self.count, self.window, self.listed = count, window, listed
        copies = [
            pltpu.make_async_copy(own_any, own_ref, sems.at[0]),
            pltpu.make_async_copy(pattern_any, pattern_ref, sems.at[1]),
        ]
        for copy in copies:
            copy.start()
        me = lax.axis_index(AXES)
        first = me * count
        side = lax.rem(me, 2)
        odd_group = 2 * side
        window[...] = jnp.zeros_like(window)
        base = partner_ref.shape[0] - 3 * PIECE_ROWS
        parts = [
            partner_ref[base + PIECE_ROWS * i:base + PIECE_ROWS * (i + 1), :].astype(f32) for i in range(3)
        ]
        partner = (parts[0] + parts[1]) + parts[2]
        for copy in copies:
            copy.wait()
        partner_group = odd_group if odd else 2 - odd_group
        for group, get in (
            (partner_group, lambda axis, at: partner[count * axis + at:count * axis + at + 1, :]),
            (1, lambda axis, at: own_ref[axis, at:at + 1, :]),
        ):
            for at in range(count):
                slot = group * count + at
                index = (first + (slot - count)).astype(f32)
                window[slot, 0:1, :] = (get(0, at) + index) - index
                window[slot, 1:2, :] = get(1, at)
                window[slot, 2:3, :] = get(2, at)

        def note(pair, found):
            cluster, column, distance = self.of(pair)
            source = cluster + distance
            group = jnp.where(source < 0, 0, jnp.where(source < count, 1, 2))
            counted = (pattern_ref[cluster, column] != 0) & (first + source >= 0) & (first + source < total)
            counted = counted & ((group == odd_group) if odd else (group != odd_group))
            listed[found] = pair
            return found + counted.astype(jnp.int32)

        self.found = lax.fori_loop(0, count * self.columns, note, jnp.int32(0))

    def of(self, pair):
        cluster, column = pair // self.columns, lax.rem(pair, self.columns)
        return cluster, column, column - W + jnp.where(column >= W - 1, 3, 0)

    def at(self, step):
        return self.of(self.listed[jnp.clip(step, 0, jnp.maximum(self.found - 1, 0))])

    def measure(self, step):
        cluster, _, distance = self.at(step)
        target = self.count + cluster
        a, b = split_points(self.window[target], self.window[target + distance], distance)
        return contract(b, a, 0, 0)


def early_body(pattern_any, own_any, full_ref, even_ref, out_ref, window, here, there, ka, kb, sketches, listed, own_ref, pattern_ref, sems, *, total):
    count, width, points = out_ref.shape
    copies = [
        pltpu.make_async_copy(ref.at[pl.ds(0, count * width)], sketches.at[pl.ds(i * count * width, count * width)], sems.at[2 + i])
        for i, ref in enumerate((full_ref, even_ref))
    ]
    for copy in copies:
        copy.start()
    pairs = Pairs(own_any, own_ref, pattern_any, pattern_ref, sems, even_ref, window, listed, False, total)
    out_ref[...] = jnp.zeros_like(out_ref)
    kb[...] = jnp.zeros_like(kb)
    here[...] = pairs.measure(jnp.int32(0))
    for copy in copies:
        copy.wait()

    def evaluate(squares, block):
        block[...] = kernel_values(squares[...], points).astype(bf16)

    def add(step, block):
        cluster, _, distance = pairs.at(step)
        source = cluster + distance
        slot = jnp.where(source < 0, source + 2 * count, source)
        rows_of = sketches[pl.ds(pl.multiple_of(slot * width, width), width), :]
        out_ref[cluster] += jnp.dot(rows_of, block[...], preferred_element_type=f32)

    def two_steps(twice, carry):
        at = 2 * twice
        there[...] = pairs.measure(at + 1)
        evaluate(here, ka)
        add(at - 1, kb)
        here[...] = pairs.measure(at + 2)
        evaluate(there, kb)
        add(at, ka)
        return carry

    lax.fori_loop(0, pairs.found // 2, two_steps, 0)
    add(pairs.found // 2 * 2 - 1, kb)

    @pl.when(lax.rem(pairs.found, 2) == 1)
    def _():
        evaluate(here, ka)
        add(pairs.found - 1, ka)


def late_body(pattern_any, own_any, odd_ref, out_ref, window, here, there, listed, own_ref, pattern_ref, sems, *, total):
    points = out_ref.shape[1]
    pairs = Pairs(own_any, own_ref, pattern_any, pattern_ref, sems, odd_ref, window, listed, True, total)
    out_ref[...] = jnp.zeros_like(out_ref)
    here[...] = pairs.measure(jnp.int32(0))
    half = pairs.columns // 2

    def evaluate(step, squares):
        cluster, column, _ = pairs.at(step)
        out_ref[half * cluster + lax.rem(column, half)] = kernel_values(squares[...], points).astype(bf16)

    def two_steps(twice, carry):
        at = 2 * twice
        there[...] = pairs.measure(at + 1)
        evaluate(at, here)
        here[...] = pairs.measure(at + 2)
        evaluate(at + 1, there)
        return carry

    lax.fori_loop(0, pairs.found // 2, two_steps, 0)

    @pl.when(lax.rem(pairs.found, 2) == 1)
    def _():
        evaluate(pairs.found - 1, here)


def block_call(kernel, name, weight, pattern, own, arrays, shape, dtype, extra):
    count, points = own.shape[1:]
    values = weight * pattern.size * points * points // 16
    whole = pl.BlockSpec(memory_space=pltpu.VMEM)
    far = pl.BlockSpec(memory_space=pl.ANY)
    return pl.pallas_call(
        kernel,
        in_specs=[far, far] + [whole] * len(arrays),
        out_specs=whole,
        scratch_shapes=[
            pltpu.VMEM((3 * count, 8, points), f32),
            pltpu.VMEM((points, points), f32),
            pltpu.VMEM((points, points), f32),
            *extra,
            pltpu.SMEM((pattern.size + 1,), jnp.int32),
            pltpu.VMEM(own.shape, f32),
            pltpu.SMEM(pattern.shape, jnp.int32),
            pltpu.SemaphoreType.DMA((4,)),
        ],
        out_shape=pltpu.VMEM(shape, dtype),
        cost_estimate=pl.CostEstimate(flops=40 * values, bytes_accessed=2 * values, transcendentals=3 * values),
        compiler_params=pltpu.CompilerParams(vmem_limit_bytes=16 * 2**20),
        name=name,
    )(in_hbm(pattern), in_hbm(own), *(in_vmem(x) for x in arrays))


def body(offsets, sketch, pattern, point_order):
    count, points, width = sketch.shape
    total = count * lax.axis_size(AXES)
    offsets = offsets.transpose(1, 0, 2)
    full, some, most = prepare(offsets, sketch)
    even_full = exchanged(full, 0)
    odd_some = exchanged(some, 1)
    odd_most = exchanged(most, 1)
    block = pltpu.VMEM((points, points), bf16)
    early = block_call(
        functools.partial(early_body, total=total), "early", 1, pattern, offsets, (full, even_full),
        (count, width, points), f32, [block, block, pltpu.VMEM((2 * count * width, points), bf16)],
    )
    odd_some, early = lax.optimization_barrier((odd_some, early))
    late = block_call(
        functools.partial(late_body, total=total), "late", 400, pattern, offsets, (odd_some,),
        (pattern.size // 2, points, points), bf16, [],
    )
    return finish(late, early, odd_some, odd_most, point_order)


def solution(mesh):
    rows = P(AXES, None, None)
    flat = P(AXES, None)
    return jax.shard_map(
        body,
        mesh=mesh,
        in_specs=(rows, rows, flat, flat),
        out_specs=(rows, rows),
        check_vma=False,
    )
```

```python
import functools
import math

import jax
import jax.numpy as jnp
from jax import lax
from jax.experimental import pallas as pl
from jax.experimental.pallas import tpu as pltpu
from jax.sharding import PartitionSpec as P

W = 4
AXES = ("grp", "dev")
f32 = jnp.float32
bf16 = jnp.bfloat16

wave_number = 40.0
decay_length = 4.0
softening = 0.5
turns = wave_number / (2.0 * math.pi)

SINE = (4.44287957, -7.30781674, 3.5977744, -0.79119941)


def exchanged(array, start):
    peers = lax.axis_size(AXES)
    pairs = [(i, i + 1) for i in range(start, peers - 1, 2)]
    return lax.ppermute(array, AXES, pairs + [(j, i) for i, j in pairs])


def offset_table(reach):
    return [-value for value in range(reach, 1, -1)] + list(range(2, reach + 1))


def kernel_values(turn_squared, points):
    scale = turns / math.sqrt(points)
    turn = turn_squared * lax.rsqrt(turn_squared)
    part = turn - jnp.round(turn)
    square = part * part
    sine = f32(SINE[-1] * math.sqrt(scale))
    for value in SINE[-2::-1]:
        sine = sine * square + f32(value * math.sqrt(scale))
    sine = sine * part
    level = jnp.exp2(turn * f32(-math.log2(math.e) / (decay_length * turns)))
    level = level * pltpu.reciprocal(turn + f32(softening * turns), approx=True)
    return level * (f32(scale) - sine * sine)


def pieces(x):
    high = x.astype(bf16).astype(f32)
    middle = (x - high).astype(bf16).astype(f32)
    low = (x - high - middle).astype(bf16).astype(f32)
    return high, middle, low


def split_points(target, source, distance):
    row = lax.broadcasted_iota(jnp.int32, target.shape, 0)
    half = distance.astype(f32) * f32(0.5)

    def shifted(x, along):
        moved = x + jnp.where(row == 0, along, jnp.where(row < 3, f32(-0.5), f32(0)))
        moved = moved * f32(turns)
        return moved, jnp.sum(moved * moved, axis=0, keepdims=True)

    left, left_norm = shifted(target, -half - f32(0.5))
    right, right_norm = shifted(source, half - f32(0.5))
    left = jnp.where(row == 3, left_norm, jnp.where(row == 4, f32(1), left))
    right = jnp.where(row == 4, right_norm, jnp.where(row == 3, f32(1), f32(-2) * right))
    lh, lm, ll = pieces(left)
    rh, rm, rl = pieces(right)
    a = jnp.concatenate([lh, lh, lm, lm, lh, ll, lm, ll], axis=0).astype(bf16)
    b = jnp.concatenate([rh, rm, rh, rm, rl, rh, rl, rm], axis=0).astype(bf16)
    return a, b


def halves(x):
    hi = x.astype(bf16)
    return hi, (x - hi.astype(f32)).astype(bf16)

def contract(a, b, da, db):
    return lax.dot_general(a, b, (((da,), (db,)), ((), ())), preferred_element_type=f32)

def lane_of(x, lane):
    return jnp.broadcast_to(x[:, lane:lane + 1], x.shape)

def factor_panel(rows, ups, first, panel, micro):
    half = first // 128
    base = first % 128
    pair = micro // 2
    lanes = lax.broadcasted_iota(jnp.int32, (8, 128), 1)
    lower = lax.broadcasted_iota(jnp.int32, (8, 128), 0) < 4

    def packed(x, y):
        return jnp.where(lower, x, pltpu.roll(y, 4, axis=0))

    for start in range(0, panel, micro):
        lane0 = base + start
        inside = (lanes >= lane0) & (lanes < lane0 + micro)
        raw = [rows[half, 8 * (start + j):8 * (start + j) + 8, :] for j in range(micro)]
        other = [rows[1 - half, 8 * (start + j):8 * (start + j) + 8, :] for j in range(micro)]
        a = [[None] * micro for _ in range(micro)]
        for i in range(pair):
            both = packed(raw[i], raw[i + pair])
            for k in range(i + pair + 1):
                value = lane_of(both, lane0 + k)
                if k <= i:
                    a[i][k] = value
                a[i + pair][k] = pltpu.roll(value, 4, axis=0)
        low = [[None] * micro for _ in range(micro)]
        inv = [None] * micro
        for k in range(micro):
            inv[k] = lax.rsqrt(a[k][k])
            for i in range(k + 1, micro):
                low[i][k] = a[i][k] * inv[k]
            for i in range(k + 1, micro):
                for m in range(k + 1, i + 1):
                    a[i][m] = a[i][m] - low[i][k] * low[m][k]
        solved = [jnp.where(inside, jnp.where(lanes == lane0 + j, f32(1), f32(0)), raw[j]) for j in range(micro)]
        for k in range(micro):
            raw[k] = raw[k] * inv[k]
            solved[k] = solved[k] * inv[k]
            other[k] = other[k] * inv[k]
            for i in range(k + 1, micro):
                raw[i] = raw[i] - low[i][k] * raw[k]
                solved[i] = solved[i] - low[i][k] * solved[k]
                other[i] = other[i] - low[i][k] * other[k]
        for j in range(micro):
            at = slice(8 * (start + j), 8 * (start + j) + 8)
            ups[at, :] = raw[j]
            rows[half, at, :] = solved[j]
            rows[1 - half, at, :] = other[j]
        if start + micro < panel:
            raw = [packed(raw[j], raw[j + pair]) for j in range(pair)]
            solved = [packed(solved[j], solved[j + pair]) for j in range(pair)]
            other = [packed(other[j], other[j + pair]) for j in range(pair)]
        for i in range(start + micro, panel):
            at = slice(8 * i, 8 * i + 8)
            x = jnp.where(inside, f32(0), rows[half, at, :])
            y = rows[1 - half, at, :]
            tx = ty = None
            for j in range(pair):
                c = lane_of(raw[j], base + i)
                tx = c * solved[j] if tx is None else tx + c * solved[j]
                ty = c * other[j] if ty is None else ty + c * other[j]
            rows[half, at, :] = x - (tx + pltpu.roll(tx, 4, axis=0))
            rows[1 - half, at, :] = y - (ty + pltpu.roll(ty, 4, axis=0))

def finish_body(k_ref, early_ref, some_ref, most_ref, order_ref, basis_any, factor_any, t_ref, mat, inv_ref, rows, ups, basis_ref, factor_ref, sems, *, panel, micro):
    count, width, points = early_ref.shape
    row_id = lax.broadcasted_iota(jnp.int32, (width, width), 0)
    col_id = lax.broadcasted_iota(jnp.int32, (width, width), 1)

    def fill(columns, shift):
        for c in range(count):
            samples = early_ref[c]
            for column in columns:
                slot = c + offset_table(W)[column] + shift
                if 0 <= slot < count:
                    at = slot * width
                    cut = min(max(SOME_ROWS - at, 0), width)
                    rows_of = [some_ref[at:at + cut, :]] if cut > 0 else []
                    if cut < width:
                        rows_of.append(most_ref[at + cut - SOME_ROWS:at + width - SOME_ROWS, :])
                    rows_of = jnp.concatenate(rows_of, axis=0)
                    block = k_ref[len(columns) * c + column % len(columns)]
                    samples = samples + jnp.dot(rows_of, block, preferred_element_type=f32)
            t_ref[c] = samples

    side = lax.rem(lax.axis_index(AXES), 2)
    reach = len(offset_table(W)) // 2
    pl.when(side == 1)(lambda: fill(range(reach, 2 * reach), -count))
    pl.when(side == 0)(lambda: fill(range(reach), count))
    for c in range(count):
        hi, lo = halves(t_ref[c])
        gram = contract(jnp.concatenate([hi, hi, lo], axis=1), jnp.concatenate([hi, lo, hi], axis=1), 1, 1)
        shift = f32(0.01) * jnp.sum(jnp.where(row_id == col_id, gram, f32(0))) / f32(width) + f32(1e-5)
        mat[c] = gram + jnp.where(row_id == col_id, shift, f32(0))
    for first in range(0, width, panel):
        half = first // 128
        base = first % 128
        for c in range(count):
            for h in range(2):
                for t in range(0, panel, 8):
                    tile = mat[c, first + t:first + t + 8, 128 * h:128 * h + 128]
                    rows[h, pl.ds(8 * t + c, 8, stride=8), :] = tile
        factor_panel(rows, ups, first, panel, micro)
        prow = lax.broadcasted_iota(jnp.int32, (panel, 128), 0) + base
        pcol = lax.broadcasted_iota(jnp.int32, (panel, 128), 1)
        for c in range(count):
            z = [rows[h, pl.ds(c, panel, stride=8), :] for h in range(2)]
            u = ups[pl.ds(c, panel, stride=8), :]
            u = jnp.where(pcol >= prow, u, f32(0))
            wz = jnp.where((pcol <= prow) | (pcol >= base + panel), z[half], f32(0))
            w = jnp.where(pcol <= prow, z[half], f32(0))
            z[half] = wz
            factor_ref[c, first:first + panel, 128 * half:128 * half + 128] = u
            factor_ref[c, first:first + panel, 128 * (1 - half):128 * (1 - half) + 128] = z[1] if half == 0 else jnp.zeros_like(u)
            inv_ref[c, first:first + panel, 128 * half:128 * half + 128] = w
            inv_ref[c, first:first + panel, 128 * (1 - half):128 * (1 - half) + 128] = z[0] if half == 1 else jnp.zeros_like(u)
            rest = first + panel
            if rest < width:
                zz = jnp.concatenate(z, axis=1)
                hi, lo = halves(zz)
                left = jnp.concatenate([hi, hi, lo], axis=0)
                right = jnp.concatenate([hi, lo, hi], axis=0)
                off = (rest // 128) * 128
                prod = contract(left[:, off:], right, 0, 0)[rest - off:, :]
                old = mat[c, rest:, :]
                cc = col_id[rest:, :]
                old = jnp.where((cc >= first) & (cc < rest), f32(0), old)
                mat[c, rest:, :] = old - prod
    sent = [pltpu.make_async_copy(factor_ref, factor_any, sems.at[count])]
    sent[0].start()
    for c in range(count):
        hi, lo = halves(t_ref[c])
        wh, wl = halves(inv_ref[c])
        b = jnp.dot(jnp.concatenate([wh, wh, wl], axis=1), jnp.concatenate([hi, lo, hi], axis=0), preferred_element_type=f32).astype(bf16)
        order_t = jnp.broadcast_to(order_ref[c:c + 1, :].astype(f32), (128, points)).T
        place = lax.broadcasted_iota(jnp.int32, (points, 128), 1).astype(f32)
        pick = jnp.concatenate([jnp.where(order_t == place + f32(128 * q), f32(1), f32(0)).astype(bf16) for q in range(points // 128)], axis=1)
        basis_ref[c] = contract(pick, b, 1, 1).astype(bf16)
        sent.append(pltpu.make_async_copy(basis_ref.at[c], basis_any.at[c], sems.at[c]))
        sent[-1].start()
    for copy in sent:
        copy.wait()

def finish(blocks, early, some, most, order, panel=32, micro=8):
    count, width, points = early.shape
    whole = pl.BlockSpec(memory_space=pltpu.VMEM)
    return pl.pallas_call(
        functools.partial(finish_body, panel=panel, micro=micro),
        in_specs=[whole] * 5,
        out_specs=(pl.BlockSpec(memory_space=pl.ANY),) * 2,
        out_shape=(
            jax.ShapeDtypeStruct((count, points, width), bf16),
            jax.ShapeDtypeStruct((count, width, width), f32),
        ),
        scratch_shapes=[
            pltpu.VMEM((count, width, points), f32),
            pltpu.VMEM((count, width, width), f32),
            pltpu.VMEM((count, width, width), f32),
            pltpu.VMEM((2, 8 * panel, 128), f32),
            pltpu.VMEM((8 * panel, 128), f32),
            pltpu.VMEM((count, points, width), bf16),
            pltpu.VMEM((count, width, width), f32),
            pltpu.SemaphoreType.DMA((count + 1,)),
        ],
        compiler_params=pltpu.CompilerParams(vmem_limit_bytes=28 * 2**20),
        name="finish",
    )(*(in_vmem(x) for x in (blocks, early, some, most)), order)


def in_vmem(x):
    return pltpu.with_memory_space_constraint(x, pltpu.VMEM)


def in_hbm(x):
    return pltpu.with_memory_space_constraint(x, pltpu.HBM)


PIECE_ROWS = 16
SOME_ROWS = 432


def prepare_body(offsets_any, sketch_any, full_ref, some_ref, most_ref, offsets_ref, sketch_ref, sems):
    count, points, width = sketch_ref.shape
    fetch = pltpu.make_async_copy(offsets_any, offsets_ref, sems.at[count])
    copies = [pltpu.make_async_copy(sketch_any.at[c], sketch_ref.at[c], sems.at[c]) for c in range(count)]
    fetch.start()
    for copy in copies:
        copy.start()
    fetch.wait()
    stacked = jnp.concatenate([offsets_ref[axis] for axis in range(3)], axis=0)
    stacked = jnp.concatenate([stacked, jnp.zeros((PIECE_ROWS - 3 * count, points), f32)], axis=0)
    parts = jnp.concatenate(pieces(stacked), axis=0).astype(bf16)
    full_ref[count * width:, :] = parts
    some_ref[SOME_ROWS:, :] = parts
    for c in range(count):
        copies[c].wait()
        turned = sketch_ref[c].T
        first = c * width
        full_ref[first:first + width, :] = turned
        cut = min(max(SOME_ROWS - first, 0), width)
        if cut > 0:
            some_ref[first:first + cut, :] = turned[:cut]
        if cut < width:
            most_ref[first + cut - SOME_ROWS:first + width - SOME_ROWS, :] = turned[cut:]


def prepare(offsets, sketch):
    count, points, width = sketch.shape
    whole = pl.BlockSpec(memory_space=pltpu.VMEM)
    far = pl.BlockSpec(memory_space=pl.ANY)
    extra = 3 * PIECE_ROWS
    return pl.pallas_call(
        prepare_body,
        in_specs=[far, far],
        out_specs=[whole] * 3,
        out_shape=tuple(
            pltpu.VMEM((n, points), bf16) for n in (count * width + extra, SOME_ROWS + extra, count * width - SOME_ROWS)
        ),
        scratch_shapes=[
            pltpu.VMEM(offsets.shape, f32),
            pltpu.VMEM(sketch.shape, bf16),
            pltpu.SemaphoreType.DMA((count + 1,)),
        ],
        compiler_params=pltpu.CompilerParams(vmem_limit_bytes=16 * 2**20),
        name="prepare",
    )(in_hbm(offsets), in_hbm(sketch))


class Pairs:
    def __init__(self, own_any, own_ref, pattern_any, pattern_ref, sems, partner_ref, window, listed, odd, total):
        count, points = own_ref.shape[1:]
        self.columns = pattern_ref.shape[1]
        self.count, self.window, self.listed = count, window, listed
        copies = [
            pltpu.make_async_copy(own_any, own_ref, sems.at[0]),
            pltpu.make_async_copy(pattern_any, pattern_ref, sems.at[1]),
        ]
        for copy in copies:
            copy.start()
        me = lax.axis_index(AXES)
        first = me * count
        side = lax.rem(me, 2)
        odd_group = 2 * side
        window[...] = jnp.zeros_like(window)
        base = partner_ref.shape[0] - 3 * PIECE_ROWS
        parts = [
            partner_ref[base + PIECE_ROWS * i:base + PIECE_ROWS * (i + 1), :].astype(f32) for i in range(3)
        ]
        partner = (parts[0] + parts[1]) + parts[2]
        for copy in copies:
            copy.wait()
        partner_group = odd_group if odd else 2 - odd_group
        for group, get in (
            (partner_group, lambda axis, at: partner[count * axis + at:count * axis + at + 1, :]),
            (1, lambda axis, at: own_ref[axis, at:at + 1, :]),
        ):
            for at in range(count):
                slot = group * count + at
                index = (first + (slot - count)).astype(f32)
                window[slot, 0:1, :] = (get(0, at) + index) - index
                window[slot, 1:2, :] = get(1, at)
                window[slot, 2:3, :] = get(2, at)

        def note(pair, found):
            cluster, column, distance = self.of(pair)
            source = cluster + distance
            group = jnp.where(source < 0, 0, jnp.where(source < count, 1, 2))
            counted = (pattern_ref[cluster, column] != 0) & (first + source >= 0) & (first + source < total)
            counted = counted & ((group == odd_group) if odd else (group != odd_group))
            listed[found] = pair
            return found + counted.astype(jnp.int32)

        self.found = lax.fori_loop(0, count * self.columns, note, jnp.int32(0))

    def of(self, pair):
        cluster, column = pair // self.columns, lax.rem(pair, self.columns)
        return cluster, column, column - W + jnp.where(column >= W - 1, 3, 0)

    def at(self, step):
        return self.of(self.listed[jnp.clip(step, 0, jnp.maximum(self.found - 1, 0))])

    def measure(self, step):
        cluster, _, distance = self.at(step)
        target = self.count + cluster
        a, b = split_points(self.window[target], self.window[target + distance], distance)
        return contract(b, a, 0, 0)


def early_body(pattern_any, own_any, full_ref, even_ref, out_ref, window, here, there, ka, kb, sketches, listed, own_ref, pattern_ref, sems, *, total):
    count, width, points = out_ref.shape
    copies = [
        pltpu.make_async_copy(ref.at[pl.ds(0, count * width)], sketches.at[pl.ds(i * count * width, count * width)], sems.at[2 + i])
        for i, ref in enumerate((full_ref, even_ref))
    ]
    for copy in copies:
        copy.start()
    pairs = Pairs(own_any, own_ref, pattern_any, pattern_ref, sems, even_ref, window, listed, False, total)
    out_ref[...] = jnp.zeros_like(out_ref)
    kb[...] = jnp.zeros_like(kb)
    here[...] = pairs.measure(jnp.int32(0))
    for copy in copies:
        copy.wait()

    def evaluate(squares, block):
        block[...] = kernel_values(squares[...], points).astype(bf16)

    def add(step, block):
        cluster, _, distance = pairs.at(step)
        source = cluster + distance
        slot = jnp.where(source < 0, source + 2 * count, source)
        rows_of = sketches[pl.ds(pl.multiple_of(slot * width, width), width), :]
        out_ref[cluster] += jnp.dot(rows_of, block[...], preferred_element_type=f32)

    def two_steps(twice, carry):
        at = 2 * twice
        there[...] = pairs.measure(at + 1)
        evaluate(here, ka)
        add(at - 1, kb)
        here[...] = pairs.measure(at + 2)
        evaluate(there, kb)
        add(at, ka)
        return carry

    lax.fori_loop(0, pairs.found // 2, two_steps, 0)
    add(pairs.found // 2 * 2 - 1, kb)

    @pl.when(lax.rem(pairs.found, 2) == 1)
    def _():
        evaluate(here, ka)
        add(pairs.found - 1, ka)


def late_body(pattern_any, own_any, odd_ref, out_ref, window, here, there, listed, own_ref, pattern_ref, sems, *, total):
    points = out_ref.shape[1]
    pairs = Pairs(own_any, own_ref, pattern_any, pattern_ref, sems, odd_ref, window, listed, True, total)
    out_ref[...] = jnp.zeros_like(out_ref)
    here[...] = pairs.measure(jnp.int32(0))
    half = pairs.columns // 2

    def evaluate(step, squares):
        cluster, column, _ = pairs.at(step)
        out_ref[half * cluster + lax.rem(column, half)] = kernel_values(squares[...], points).astype(bf16)

    def two_steps(twice, carry):
        at = 2 * twice
        there[...] = pairs.measure(at + 1)
        evaluate(at, here)
        here[...] = pairs.measure(at + 2)
        evaluate(at + 1, there)
        return carry

    lax.fori_loop(0, pairs.found // 2, two_steps, 0)

    @pl.when(lax.rem(pairs.found, 2) == 1)
    def _():
        evaluate(pairs.found - 1, here)


def block_call(kernel, name, weight, pattern, own, arrays, shape, dtype, extra):
    count, points = own.shape[1:]
    values = weight * pattern.size * points * points // 16
    whole = pl.BlockSpec(memory_space=pltpu.VMEM)
    far = pl.BlockSpec(memory_space=pl.ANY)
    return pl.pallas_call(
        kernel,
        in_specs=[far, far] + [whole] * len(arrays),
        out_specs=whole,
        scratch_shapes=[
            pltpu.VMEM((3 * count, 8, points), f32),
            pltpu.VMEM((points, points), f32),
            pltpu.VMEM((points, points), f32),
            *extra,
            pltpu.SMEM((pattern.size + 1,), jnp.int32),
            pltpu.VMEM(own.shape, f32),
            pltpu.SMEM(pattern.shape, jnp.int32),
            pltpu.SemaphoreType.DMA((4,)),
        ],
        out_shape=pltpu.VMEM(shape, dtype),
        cost_estimate=pl.CostEstimate(flops=40 * values, bytes_accessed=2 * values, transcendentals=3 * values),
        compiler_params=pltpu.CompilerParams(vmem_limit_bytes=16 * 2**20),
        name=name,
    )(in_hbm(pattern), in_hbm(own), *(in_vmem(x) for x in arrays))


def body(offsets, sketch, pattern, point_order):
    count, points, width = sketch.shape
    total = count * lax.axis_size(AXES)
    offsets = offsets.transpose(1, 0, 2)
    full, some, most = prepare(offsets, sketch)
    even_full = exchanged(full, 0)
    odd_some = exchanged(some, 1)
    odd_most = exchanged(most, 1)
    block = pltpu.VMEM((points, points), bf16)
    early = block_call(
        functools.partial(early_body, total=total), "early", 0, pattern, offsets, (full, even_full),
        (count, width, points), f32, [block, block, pltpu.VMEM((2 * count * width, points), bf16)],
    )
    odd_some, early = lax.optimization_barrier((odd_some, early))
    late = block_call(
        functools.partial(late_body, total=total), "late", 200, pattern, offsets, (odd_some,),
        (pattern.size // 2, points, points), bf16, [],
    )
    return finish(late, early, odd_some, odd_most, point_order)


def solution(mesh):
    rows = P(AXES, None, None)
    flat = P(AXES, None)
    return jax.shard_map(
        body,
        mesh=mesh,
        in_specs=(rows, rows, flat, flat),
        out_specs=(rows, rows),
        check_vma=False,
    )
```

```python
import functools
import math

import jax
import jax.numpy as jnp
from jax import lax
from jax.experimental import pallas as pl
from jax.experimental.pallas import tpu as pltpu
from jax.sharding import PartitionSpec as P

W = 4
AXES = ("grp", "dev")
f32 = jnp.float32
bf16 = jnp.bfloat16

wave_number = 40.0
decay_length = 4.0
softening = 0.5
turns = wave_number / (2.0 * math.pi)

SINE = (4.44287957, -7.30781674, 3.5977744, -0.79119941)


def exchanged(array, start):
    peers = lax.axis_size(AXES)
    pairs = [(i, i + 1) for i in range(start, peers - 1, 2)]
    return lax.ppermute(array, AXES, pairs + [(j, i) for i, j in pairs])


def offset_table(reach):
    return [-value for value in range(reach, 1, -1)] + list(range(2, reach + 1))


def kernel_values(turn_squared, points):
    scale = turns / math.sqrt(points)
    turn = turn_squared * lax.rsqrt(turn_squared)
    part = turn - jnp.round(turn)
    square = part * part
    sine = f32(SINE[-1] * math.sqrt(scale))
    for value in SINE[-2::-1]:
        sine = sine * square + f32(value * math.sqrt(scale))
    sine = sine * part
    level = jnp.exp2(turn * f32(-math.log2(math.e) / (decay_length * turns)))
    level = level * pltpu.reciprocal(turn + f32(softening * turns), approx=True)
    return level * (f32(scale) - sine * sine)


def pieces(x):
    high = x.astype(bf16).astype(f32)
    middle = (x - high).astype(bf16).astype(f32)
    low = (x - high - middle).astype(bf16).astype(f32)
    return high, middle, low


def split_points(target, source, distance):
    row = lax.broadcasted_iota(jnp.int32, target.shape, 0)
    half = distance.astype(f32) * f32(0.5)

    def shifted(x, along):
        moved = x + jnp.where(row == 0, along, jnp.where(row < 3, f32(-0.5), f32(0)))
        moved = moved * f32(turns)
        return moved, jnp.sum(moved * moved, axis=0, keepdims=True)

    left, left_norm = shifted(target, -half - f32(0.5))
    right, right_norm = shifted(source, half - f32(0.5))
    left = jnp.where(row == 3, left_norm, jnp.where(row == 4, f32(1), left))
    right = jnp.where(row == 4, right_norm, jnp.where(row == 3, f32(1), f32(-2) * right))
    lh, lm, ll = pieces(left)
    rh, rm, rl = pieces(right)
    a = jnp.concatenate([lh, lh, lm, lm, lh, ll, lm, ll], axis=0).astype(bf16)
    b = jnp.concatenate([rh, rm, rh, rm, rl, rh, rl, rm], axis=0).astype(bf16)
    return a, b


def halves(x):
    hi = x.astype(bf16)
    return hi, (x - hi.astype(f32)).astype(bf16)

def contract(a, b, da, db):
    return lax.dot_general(a, b, (((da,), (db,)), ((), ())), preferred_element_type=f32)

def lane_of(x, lane):
    return jnp.broadcast_to(x[:, lane:lane + 1], x.shape)

def factor_panel(rows, ups, first, panel, micro):
    half = first // 128
    base = first % 128
    pair = micro // 2
    lanes = lax.broadcasted_iota(jnp.int32, (8, 128), 1)
    lower = lax.broadcasted_iota(jnp.int32, (8, 128), 0) < 4

    def packed(x, y):
        return jnp.where(lower, x, pltpu.roll(y, 4, axis=0))

    for start in range(0, panel, micro):
        lane0 = base + start
        inside = (lanes >= lane0) & (lanes < lane0 + micro)
        raw = [rows[half, 8 * (start + j):8 * (start + j) + 8, :] for j in range(micro)]
        other = [rows[1 - half, 8 * (start + j):8 * (start + j) + 8, :] for j in range(micro)]
        a = [[None] * micro for _ in range(micro)]
        for i in range(pair):
            both = packed(raw[i], raw[i + pair])
            for k in range(i + pair + 1):
                value = lane_of(both, lane0 + k)
                if k <= i:
                    a[i][k] = value
                a[i + pair][k] = pltpu.roll(value, 4, axis=0)
        low = [[None] * micro for _ in range(micro)]
        inv = [None] * micro
        for k in range(micro):
            inv[k] = lax.rsqrt(a[k][k])
            for i in range(k + 1, micro):
                low[i][k] = a[i][k] * inv[k]
            for i in range(k + 1, micro):
                for m in range(k + 1, i + 1):
                    a[i][m] = a[i][m] - low[i][k] * low[m][k]
        solved = [jnp.where(inside, jnp.where(lanes == lane0 + j, f32(1), f32(0)), raw[j]) for j in range(micro)]
        for k in range(micro):
            raw[k] = raw[k] * inv[k]
            solved[k] = solved[k] * inv[k]
            other[k] = other[k] * inv[k]
            for i in range(k + 1, micro):
                raw[i] = raw[i] - low[i][k] * raw[k]
                solved[i] = solved[i] - low[i][k] * solved[k]
                other[i] = other[i] - low[i][k] * other[k]
        for j in range(micro):
            at = slice(8 * (start + j), 8 * (start + j) + 8)
            ups[at, :] = raw[j]
            rows[half, at, :] = solved[j]
            rows[1 - half, at, :] = other[j]
        if start + micro < panel:
            raw = [packed(raw[j], raw[j + pair]) for j in range(pair)]
            solved = [packed(solved[j], solved[j + pair]) for j in range(pair)]
            other = [packed(other[j], other[j + pair]) for j in range(pair)]
        for i in range(start + micro, panel):
            at = slice(8 * i, 8 * i + 8)
            x = jnp.where(inside, f32(0), rows[half, at, :])
            y = rows[1 - half, at, :]
            tx = ty = None
            for j in range(pair):
                c = lane_of(raw[j], base + i)
                tx = c * solved[j] if tx is None else tx + c * solved[j]
                ty = c * other[j] if ty is None else ty + c * other[j]
            rows[half, at, :] = x - (tx + pltpu.roll(tx, 4, axis=0))
            rows[1 - half, at, :] = y - (ty + pltpu.roll(ty, 4, axis=0))

def finish_body(k_ref, early_ref, some_ref, most_ref, order_ref, basis_any, factor_any, t_ref, mat, inv_ref, rows, ups, basis_ref, factor_ref, sems, *, panel, micro):
    count, width, points = early_ref.shape
    row_id = lax.broadcasted_iota(jnp.int32, (width, width), 0)
    col_id = lax.broadcasted_iota(jnp.int32, (width, width), 1)

    def fill(columns, shift):
        for c in range(count):
            samples = early_ref[c]
            for column in columns:
                slot = c + offset_table(W)[column] + shift
                if 0 <= slot < count:
                    at = slot * width
                    cut = min(max(SOME_ROWS - at, 0), width)
                    rows_of = [some_ref[at:at + cut, :]] if cut > 0 else []
                    if cut < width:
                        rows_of.append(most_ref[at + cut - SOME_ROWS:at + width - SOME_ROWS, :])
                    rows_of = jnp.concatenate(rows_of, axis=0)
                    block = k_ref[len(columns) * c + column % len(columns)]
                    samples = samples + jnp.dot(rows_of, block, preferred_element_type=f32)
            t_ref[c] = samples

    side = lax.rem(lax.axis_index(AXES), 2)
    reach = len(offset_table(W)) // 2
    pl.when(side == 1)(lambda: fill(range(reach, 2 * reach), -count))
    pl.when(side == 0)(lambda: fill(range(reach), count))
    for c in range(count):
        hi, lo = halves(t_ref[c])
        gram = contract(jnp.concatenate([hi, hi, lo], axis=1), jnp.concatenate([hi, lo, hi], axis=1), 1, 1)
        shift = f32(0.01) * jnp.sum(jnp.where(row_id == col_id, gram, f32(0))) / f32(width) + f32(1e-5)
        mat[c] = gram + jnp.where(row_id == col_id, shift, f32(0))
    for first in range(0, width, panel):
        half = first // 128
        base = first % 128
        for c in range(count):
            for h in range(2):
                for t in range(0, panel, 8):
                    tile = mat[c, first + t:first + t + 8, 128 * h:128 * h + 128]
                    rows[h, pl.ds(8 * t + c, 8, stride=8), :] = tile
        factor_panel(rows, ups, first, panel, micro)
        prow = lax.broadcasted_iota(jnp.int32, (panel, 128), 0) + base
        pcol = lax.broadcasted_iota(jnp.int32, (panel, 128), 1)
        for c in range(count):
            z = [rows[h, pl.ds(c, panel, stride=8), :] for h in range(2)]
            u = ups[pl.ds(c, panel, stride=8), :]
            u = jnp.where(pcol >= prow, u, f32(0))
            wz = jnp.where((pcol <= prow) | (pcol >= base + panel), z[half], f32(0))
            w = jnp.where(pcol <= prow, z[half], f32(0))
            z[half] = wz
            factor_ref[c, first:first + panel, 128 * half:128 * half + 128] = u
            factor_ref[c, first:first + panel, 128 * (1 - half):128 * (1 - half) + 128] = z[1] if half == 0 else jnp.zeros_like(u)
            inv_ref[c, first:first + panel, 128 * half:128 * half + 128] = w
            inv_ref[c, first:first + panel, 128 * (1 - half):128 * (1 - half) + 128] = z[0] if half == 1 else jnp.zeros_like(u)
            rest = first + panel
            if rest < width:
                zz = jnp.concatenate(z, axis=1)
                hi, lo = halves(zz)
                left = jnp.concatenate([hi, hi, lo], axis=0)
                right = jnp.concatenate([hi, lo, hi], axis=0)
                off = (rest // 128) * 128
                prod = contract(left[:, off:], right, 0, 0)[rest - off:, :]
                old = mat[c, rest:, :]
                cc = col_id[rest:, :]
                old = jnp.where((cc >= first) & (cc < rest), f32(0), old)
                mat[c, rest:, :] = old - prod
    sent = [pltpu.make_async_copy(factor_ref, factor_any, sems.at[count])]
    sent[0].start()
    for c in range(count):
        hi, lo = halves(t_ref[c])
        wh, wl = halves(inv_ref[c])
        b = jnp.dot(jnp.concatenate([wh, wh, wl], axis=1), jnp.concatenate([hi, lo, hi], axis=0), preferred_element_type=f32).astype(bf16)
        order_t = jnp.broadcast_to(order_ref[c:c + 1, :].astype(f32), (128, points)).T
        place = lax.broadcasted_iota(jnp.int32, (points, 128), 1).astype(f32)
        pick = jnp.concatenate([jnp.where(order_t == place + f32(128 * q), f32(1), f32(0)).astype(bf16) for q in range(points // 128)], axis=1)
        basis_ref[c] = contract(pick, b, 1, 1).astype(bf16)
        sent.append(pltpu.make_async_copy(basis_ref.at[c], basis_any.at[c], sems.at[c]))
        sent[-1].start()
    for copy in sent:
        copy.wait()

def finish(blocks, early, some, most, order, panel=32, micro=8):
    count, width, points = early.shape
    whole = pl.BlockSpec(memory_space=pltpu.VMEM)
    return pl.pallas_call(
        functools.partial(finish_body, panel=panel, micro=micro),
        in_specs=[whole] * 5,
        out_specs=(pl.BlockSpec(memory_space=pl.ANY),) * 2,
        out_shape=(
            jax.ShapeDtypeStruct((count, points, width), bf16),
            jax.ShapeDtypeStruct((count, width, width), f32),
        ),
        scratch_shapes=[
            pltpu.VMEM((count, width, points), f32),
            pltpu.VMEM((count, width, width), f32),
            pltpu.VMEM((count, width, width), f32),
            pltpu.VMEM((2, 8 * panel, 128), f32),
            pltpu.VMEM((8 * panel, 128), f32),
            pltpu.VMEM((count, points, width), bf16),
            pltpu.VMEM((count, width, width), f32),
            pltpu.SemaphoreType.DMA((count + 1,)),
        ],
        compiler_params=pltpu.CompilerParams(vmem_limit_bytes=28 * 2**20),
        name="finish",
    )(*(in_vmem(x) for x in (blocks, early, some, most)), order)


def in_vmem(x):
    return pltpu.with_memory_space_constraint(x, pltpu.VMEM)


def in_hbm(x):
    return pltpu.with_memory_space_constraint(x, pltpu.HBM)


PIECE_ROWS = 16
SOME_ROWS = 432


def prepare_body(offsets_any, sketch_any, full_ref, some_ref, most_ref, offsets_ref, sketch_ref, sems):
    count, points, width = sketch_ref.shape
    fetch = pltpu.make_async_copy(offsets_any, offsets_ref, sems.at[count])
    copies = [pltpu.make_async_copy(sketch_any.at[c], sketch_ref.at[c], sems.at[c]) for c in range(count)]
    fetch.start()
    for copy in copies:
        copy.start()
    fetch.wait()
    stacked = jnp.concatenate([offsets_ref[axis] for axis in range(3)], axis=0)
    stacked = jnp.concatenate([stacked, jnp.zeros((PIECE_ROWS - 3 * count, points), f32)], axis=0)
    parts = jnp.concatenate(pieces(stacked), axis=0).astype(bf16)
    full_ref[count * width:, :] = parts
    some_ref[SOME_ROWS:, :] = parts
    for c in range(count):
        copies[c].wait()
        turned = sketch_ref[c].T
        first = c * width
        full_ref[first:first + width, :] = turned
        cut = min(max(SOME_ROWS - first, 0), width)
        if cut > 0:
            some_ref[first:first + cut, :] = turned[:cut]
        if cut < width:
            most_ref[first + cut - SOME_ROWS:first + width - SOME_ROWS, :] = turned[cut:]


def prepare(offsets, sketch):
    count, points, width = sketch.shape
    whole = pl.BlockSpec(memory_space=pltpu.VMEM)
    far = pl.BlockSpec(memory_space=pl.ANY)
    extra = 3 * PIECE_ROWS
    return pl.pallas_call(
        prepare_body,
        in_specs=[far, far],
        out_specs=[whole] * 3,
        out_shape=tuple(
            pltpu.VMEM((n, points), bf16) for n in (count * width + extra, SOME_ROWS + extra, count * width - SOME_ROWS)
        ),
        scratch_shapes=[
            pltpu.VMEM(offsets.shape, f32),
            pltpu.VMEM(sketch.shape, bf16),
            pltpu.SemaphoreType.DMA((count + 1,)),
        ],
        compiler_params=pltpu.CompilerParams(vmem_limit_bytes=16 * 2**20),
        name="prepare",
    )(in_hbm(offsets), in_hbm(sketch))


class Pairs:
    def __init__(self, own_any, own_ref, pattern_any, pattern_ref, sems, partner_ref, window, listed, odd, total, meanwhile):
        count, points = own_ref.shape[1:]
        self.columns = pattern_ref.shape[1]
        self.count, self.window, self.listed = count, window, listed
        copies = [
            pltpu.make_async_copy(own_any, own_ref, sems.at[0]),
            pltpu.make_async_copy(pattern_any, pattern_ref, sems.at[1]),
        ]
        for copy in copies:
            copy.start()
        meanwhile()
        me = lax.axis_index(AXES)
        first = me * count
        side = lax.rem(me, 2)
        odd_group = 2 * side
        window[...] = jnp.zeros_like(window)
        base = partner_ref.shape[0] - 3 * PIECE_ROWS
        parts = [
            partner_ref[base + PIECE_ROWS * i:base + PIECE_ROWS * (i + 1), :].astype(f32) for i in range(3)
        ]
        partner = (parts[0] + parts[1]) + parts[2]
        for copy in copies:
            copy.wait()
        partner_group = odd_group if odd else 2 - odd_group
        for group, get in (
            (partner_group, lambda axis, at: partner[count * axis + at:count * axis + at + 1, :]),
            (1, lambda axis, at: own_ref[axis, at:at + 1, :]),
        ):
            for at in range(count):
                slot = group * count + at
                index = (first + (slot - count)).astype(f32)
                window[slot, 0:1, :] = (get(0, at) + index) - index
                window[slot, 1:2, :] = get(1, at)
                window[slot, 2:3, :] = get(2, at)

        self.found = jnp.int32(0)
        for pair in range(count * self.columns):
            cluster, column = divmod(pair, self.columns)
            source = cluster + offset_table(W)[column]
            group = 0 if source < 0 else 1 if source < count else 2
            counted = (pattern_ref[cluster, column] != 0) & (first + source >= 0) & (first + source < total)
            counted = counted & ((odd_group == group) if odd else (odd_group != group))
            listed[self.found] = pair
            self.found = self.found + counted.astype(jnp.int32)

    def of(self, pair):
        cluster, column = pair // self.columns, lax.rem(pair, self.columns)
        return cluster, column, column - W + jnp.where(column >= W - 1, 3, 0)

    def at(self, step):
        return self.of(self.listed[jnp.clip(step, 0, jnp.maximum(self.found - 1, 0))])

    def measure(self, step):
        cluster, _, distance = self.at(step)
        target = self.count + cluster
        a, b = split_points(self.window[target], self.window[target + distance], distance)
        return contract(b, a, 0, 0)


def early_body(pattern_any, own_any, full_ref, even_ref, out_ref, window, here, there, ka, kb, sketches, listed, own_ref, pattern_ref, sems, *, total):
    count, width, points = out_ref.shape
    copies = [
        pltpu.make_async_copy(ref.at[pl.ds(0, count * width)], sketches.at[pl.ds(i * count * width, count * width)], sems.at[2 + i])
        for i, ref in enumerate((full_ref, even_ref))
    ]
    for copy in copies:
        copy.start()

    def clear():
        out_ref[...] = jnp.zeros_like(out_ref)
        kb[...] = jnp.zeros_like(kb)

    pairs = Pairs(
        own_any, own_ref, pattern_any, pattern_ref, sems, even_ref, window, listed, False, total, clear
    )
    here[...] = pairs.measure(jnp.int32(0))
    for copy in copies:
        copy.wait()

    def evaluate(squares, block):
        block[...] = kernel_values(squares[...], points).astype(bf16)

    def add(step, block):
        cluster, _, distance = pairs.at(step)
        source = cluster + distance
        slot = jnp.where(source < 0, source + 2 * count, source)
        rows_of = sketches[pl.ds(pl.multiple_of(slot * width, width), width), :]
        out_ref[cluster] += jnp.dot(rows_of, block[...], preferred_element_type=f32)

    def two_steps(twice, carry):
        at = 2 * twice
        there[...] = pairs.measure(at + 1)
        evaluate(here, ka)
        add(at - 1, kb)
        here[...] = pairs.measure(at + 2)
        evaluate(there, kb)
        add(at, ka)
        return carry

    lax.fori_loop(0, pairs.found // 2, two_steps, 0)
    add(pairs.found // 2 * 2 - 1, kb)

    @pl.when(lax.rem(pairs.found, 2) == 1)
    def _():
        evaluate(here, ka)
        add(pairs.found - 1, ka)


def late_body(pattern_any, own_any, odd_ref, out_ref, window, here, there, listed, own_ref, pattern_ref, sems, *, total):
    points = out_ref.shape[1]

    def clear():
        out_ref[...] = jnp.zeros_like(out_ref)

    pairs = Pairs(
        own_any, own_ref, pattern_any, pattern_ref, sems, odd_ref, window, listed, True, total, clear
    )
    here[...] = pairs.measure(jnp.int32(0))
    half = pairs.columns // 2

    def evaluate(step, squares):
        cluster, column, _ = pairs.at(step)
        out_ref[half * cluster + lax.rem(column, half)] = kernel_values(squares[...], points).astype(bf16)

    def two_steps(twice, carry):
        at = 2 * twice
        there[...] = pairs.measure(at + 1)
        evaluate(at, here)
        here[...] = pairs.measure(at + 2)
        evaluate(at + 1, there)
        return carry

    lax.fori_loop(0, pairs.found // 2, two_steps, 0)

    @pl.when(lax.rem(pairs.found, 2) == 1)
    def _():
        evaluate(pairs.found - 1, here)


def block_call(kernel, name, weight, pattern, own, arrays, shape, dtype, extra):
    count, points = own.shape[1:]
    values = weight * pattern.size * points * points // 16
    whole = pl.BlockSpec(memory_space=pltpu.VMEM)
    far = pl.BlockSpec(memory_space=pl.ANY)
    return pl.pallas_call(
        kernel,
        in_specs=[far, far] + [whole] * len(arrays),
        out_specs=whole,
        scratch_shapes=[
            pltpu.VMEM((3 * count, 8, points), f32),
            pltpu.VMEM((points, points), f32),
            pltpu.VMEM((points, points), f32),
            *extra,
            pltpu.SMEM((pattern.size + 1,), jnp.int32),
            pltpu.VMEM(own.shape, f32),
            pltpu.SMEM(pattern.shape, jnp.int32),
            pltpu.SemaphoreType.DMA((4,)),
        ],
        out_shape=pltpu.VMEM(shape, dtype),
        cost_estimate=pl.CostEstimate(flops=40 * values, bytes_accessed=2 * values, transcendentals=3 * values),
        compiler_params=pltpu.CompilerParams(vmem_limit_bytes=16 * 2**20),
        name=name,
    )(in_hbm(pattern), in_hbm(own), *(in_vmem(x) for x in arrays))


def body(offsets, sketch, pattern, point_order):
    count, points, width = sketch.shape
    total = count * lax.axis_size(AXES)
    offsets = offsets.transpose(1, 0, 2)
    full, some, most = prepare(offsets, sketch)
    even_full = exchanged(full, 0)
    odd_some = exchanged(some, 1)
    odd_most = exchanged(most, 1)
    block = pltpu.VMEM((points, points), bf16)
    early = block_call(
        functools.partial(early_body, total=total), "early", 0, pattern, offsets, (full, even_full),
        (count, width, points), f32, [block, block, pltpu.VMEM((2 * count * width, points), bf16)],
    )
    odd_some, early = lax.optimization_barrier((odd_some, early))
    late = block_call(
        functools.partial(late_body, total=total), "late", 200, pattern, offsets, (odd_some,),
        (pattern.size // 2, points, points), bf16, [],
    )
    return finish(late, early, odd_some, odd_most, point_order)


def solution(mesh):
    rows = P(AXES, None, None)
    flat = P(AXES, None)
    return jax.shard_map(
        body,
        mesh=mesh,
        in_specs=(rows, rows, flat, flat),
        out_specs=(rows, rows),
        check_vma=False,
    )
```

```python
import functools
import math

import jax
import jax.numpy as jnp
from jax import lax
from jax.experimental import pallas as pl
from jax.experimental.pallas import tpu as pltpu
from jax.sharding import PartitionSpec as P

W = 4
AXES = ("grp", "dev")
f32 = jnp.float32
bf16 = jnp.bfloat16

wave_number = 40.0
decay_length = 4.0
softening = 0.5
turns = wave_number / (2.0 * math.pi)

SINE = (4.44287957, -7.30781674, 3.5977744, -0.79119941)


def exchanged(array, start):
    peers = lax.axis_size(AXES)
    pairs = [(i, i + 1) for i in range(start, peers - 1, 2)]
    return lax.ppermute(array, AXES, pairs + [(j, i) for i, j in pairs])


def offset_table(reach):
    return [-value for value in range(reach, 1, -1)] + list(range(2, reach + 1))


def kernel_values(turn_squared, points):
    scale = turns / math.sqrt(points)
    turn = turn_squared * lax.rsqrt(turn_squared)
    part = turn - jnp.round(turn)
    square = part * part
    sine = f32(SINE[-1] * math.sqrt(scale))
    for value in SINE[-2::-1]:
        sine = sine * square + f32(value * math.sqrt(scale))
    sine = sine * part
    level = jnp.exp2(turn * f32(-math.log2(math.e) / (decay_length * turns)))
    level = level * pltpu.reciprocal(turn + f32(softening * turns), approx=True)
    return level * (f32(scale) - sine * sine)


def pieces(x):
    high = x.astype(bf16).astype(f32)
    middle = (x - high).astype(bf16).astype(f32)
    low = (x - high - middle).astype(bf16).astype(f32)
    return high, middle, low


def split_points(target, source, distance):
    row = lax.broadcasted_iota(jnp.int32, target.shape, 0)
    half = distance.astype(f32) * f32(0.5)

    def shifted(x, along):
        moved = x + jnp.where(row == 0, along, jnp.where(row < 3, f32(-0.5), f32(0)))
        moved = moved * f32(turns)
        return moved, jnp.sum(moved * moved, axis=0, keepdims=True)

    left, left_norm = shifted(target, -half - f32(0.5))
    right, right_norm = shifted(source, half - f32(0.5))
    left = jnp.where(row == 3, left_norm, jnp.where(row == 4, f32(1), left))
    right = jnp.where(row == 4, right_norm, jnp.where(row == 3, f32(1), f32(-2) * right))
    lh, lm, ll = pieces(left)
    rh, rm, rl = pieces(right)
    a = jnp.concatenate([lh, lh, lm, lm, lh, ll, lm, ll], axis=0).astype(bf16)
    b = jnp.concatenate([rh, rm, rh, rm, rl, rh, rl, rm], axis=0).astype(bf16)
    return a, b


def halves(x):
    hi = x.astype(bf16)
    return hi, (x - hi.astype(f32)).astype(bf16)

def contract(a, b, da, db):
    return lax.dot_general(a, b, (((da,), (db,)), ((), ())), preferred_element_type=f32)

def lane_of(x, lane):
    return jnp.broadcast_to(x[:, lane:lane + 1], x.shape)

def factor_panel(rows, ups, first, panel, micro):
    half = first // 128
    base = first % 128
    pair = micro // 2
    lanes = lax.broadcasted_iota(jnp.int32, (8, 128), 1)
    lower = lax.broadcasted_iota(jnp.int32, (8, 128), 0) < 4

    def packed(x, y):
        return jnp.where(lower, x, pltpu.roll(y, 4, axis=0))

    for start in range(0, panel, micro):
        lane0 = base + start
        inside = (lanes >= lane0) & (lanes < lane0 + micro)
        raw = [rows[half, 8 * (start + j):8 * (start + j) + 8, :] for j in range(micro)]
        other = [rows[1 - half, 8 * (start + j):8 * (start + j) + 8, :] for j in range(micro)]
        a = [[None] * micro for _ in range(micro)]
        for i in range(pair):
            both = packed(raw[i], raw[i + pair])
            for k in range(i + pair + 1):
                value = lane_of(both, lane0 + k)
                if k <= i:
                    a[i][k] = value
                a[i + pair][k] = pltpu.roll(value, 4, axis=0)
        low = [[None] * micro for _ in range(micro)]
        inv = [None] * micro
        for k in range(micro):
            inv[k] = lax.rsqrt(a[k][k])
            for i in range(k + 1, micro):
                low[i][k] = a[i][k] * inv[k]
            for i in range(k + 1, micro):
                for m in range(k + 1, i + 1):
                    a[i][m] = a[i][m] - low[i][k] * low[m][k]
        solved = [jnp.where(inside, jnp.where(lanes == lane0 + j, f32(1), f32(0)), raw[j]) for j in range(micro)]
        for k in range(micro):
            raw[k] = raw[k] * inv[k]
            solved[k] = solved[k] * inv[k]
            other[k] = other[k] * inv[k]
            for i in range(k + 1, micro):
                raw[i] = raw[i] - low[i][k] * raw[k]
                solved[i] = solved[i] - low[i][k] * solved[k]
                other[i] = other[i] - low[i][k] * other[k]
        for j in range(micro):
            at = slice(8 * (start + j), 8 * (start + j) + 8)
            ups[at, :] = raw[j]
            rows[half, at, :] = solved[j]
            rows[1 - half, at, :] = other[j]
        if start + micro < panel:
            raw = [packed(raw[j], raw[j + pair]) for j in range(pair)]
            solved = [packed(solved[j], solved[j + pair]) for j in range(pair)]
            other = [packed(other[j], other[j + pair]) for j in range(pair)]
        for i in range(start + micro, panel):
            at = slice(8 * i, 8 * i + 8)
            x = jnp.where(inside, f32(0), rows[half, at, :])
            y = rows[1 - half, at, :]
            tx = ty = None
            for j in range(pair):
                c = lane_of(raw[j], base + i)
                tx = c * solved[j] if tx is None else tx + c * solved[j]
                ty = c * other[j] if ty is None else ty + c * other[j]
            rows[half, at, :] = x - (tx + pltpu.roll(tx, 4, axis=0))
            rows[1 - half, at, :] = y - (ty + pltpu.roll(ty, 4, axis=0))

def finish_body(k_ref, early_ref, some_ref, most_ref, order_ref, basis_any, factor_any, t_ref, mat, inv_ref, rows, ups, basis_ref, factor_ref, sems, *, panel, micro):
    count, width, points = early_ref.shape
    row_id = lax.broadcasted_iota(jnp.int32, (width, width), 0)
    col_id = lax.broadcasted_iota(jnp.int32, (width, width), 1)

    def fill(columns, shift):
        for c in range(count):
            samples = early_ref[c]
            for column in columns:
                slot = c + offset_table(W)[column] + shift
                if 0 <= slot < count:
                    at = slot * width
                    cut = min(max(SOME_ROWS - at, 0), width)
                    rows_of = [some_ref[at:at + cut, :]] if cut > 0 else []
                    if cut < width:
                        rows_of.append(most_ref[at + cut - SOME_ROWS:at + width - SOME_ROWS, :])
                    rows_of = jnp.concatenate(rows_of, axis=0)
                    block = k_ref[len(columns) * c + column % len(columns)]
                    samples = samples + jnp.dot(rows_of, block, preferred_element_type=f32)
            t_ref[c] = samples

    side = lax.rem(lax.axis_index(AXES), 2)
    reach = len(offset_table(W)) // 2
    pl.when(side == 1)(lambda: fill(range(reach, 2 * reach), -count))
    pl.when(side == 0)(lambda: fill(range(reach), count))
    for c in range(count):
        hi, lo = halves(t_ref[c])
        gram = contract(jnp.concatenate([hi, hi, lo], axis=1), jnp.concatenate([hi, lo, hi], axis=1), 1, 1)
        shift = f32(0.01) * jnp.sum(jnp.where(row_id == col_id, gram, f32(0))) / f32(width) + f32(1e-5)
        mat[c] = gram + jnp.where(row_id == col_id, shift, f32(0))
    for first in range(0, width, panel):
        half = first // 128
        base = first % 128
        for c in range(count):
            for h in range(2):
                for t in range(0, panel, 8):
                    tile = mat[c, first + t:first + t + 8, 128 * h:128 * h + 128]
                    rows[h, pl.ds(8 * t + c, 8, stride=8), :] = tile
        factor_panel(rows, ups, first, panel, micro)
        prow = lax.broadcasted_iota(jnp.int32, (panel, 128), 0) + base
        pcol = lax.broadcasted_iota(jnp.int32, (panel, 128), 1)
        for c in range(count):
            z = [rows[h, pl.ds(c, panel, stride=8), :] for h in range(2)]
            u = ups[pl.ds(c, panel, stride=8), :]
            u = jnp.where(pcol >= prow, u, f32(0))
            wz = jnp.where((pcol <= prow) | (pcol >= base + panel), z[half], f32(0))
            w = jnp.where(pcol <= prow, z[half], f32(0))
            z[half] = wz
            factor_ref[c, first:first + panel, 128 * half:128 * half + 128] = u
            factor_ref[c, first:first + panel, 128 * (1 - half):128 * (1 - half) + 128] = z[1] if half == 0 else jnp.zeros_like(u)
            inv_ref[c, first:first + panel, 128 * half:128 * half + 128] = w
            inv_ref[c, first:first + panel, 128 * (1 - half):128 * (1 - half) + 128] = z[0] if half == 1 else jnp.zeros_like(u)
            rest = first + panel
            if rest < width:
                zz = jnp.concatenate(z, axis=1)
                hi, lo = halves(zz)
                left = jnp.concatenate([hi, hi, lo], axis=0)
                right = jnp.concatenate([hi, lo, hi], axis=0)
                off = (rest // 128) * 128
                prod = contract(left[:, off:], right, 0, 0)[rest - off:, :]
                old = mat[c, rest:, :]
                cc = col_id[rest:, :]
                old = jnp.where((cc >= first) & (cc < rest), f32(0), old)
                mat[c, rest:, :] = old - prod
    sent = [pltpu.make_async_copy(factor_ref, factor_any, sems.at[count])]
    sent[0].start()
    for c in range(count):
        hi, lo = halves(t_ref[c])
        wh, wl = halves(inv_ref[c])
        b = jnp.dot(jnp.concatenate([wh, wh, wl], axis=1), jnp.concatenate([hi, lo, hi], axis=0), preferred_element_type=f32).astype(bf16)
        order_t = jnp.broadcast_to(order_ref[c:c + 1, :].astype(f32), (128, points)).T
        place = lax.broadcasted_iota(jnp.int32, (points, 128), 1).astype(f32)
        pick = jnp.concatenate([jnp.where(order_t == place + f32(128 * q), f32(1), f32(0)).astype(bf16) for q in range(points // 128)], axis=1)
        basis_ref[c] = contract(pick, b, 1, 1).astype(bf16)
        sent.append(pltpu.make_async_copy(basis_ref.at[c], basis_any.at[c], sems.at[c]))
        sent[-1].start()
    for copy in sent:
        copy.wait()

def finish(blocks, early, some, most, order, panel=32, micro=8):
    count, width, points = early.shape
    whole = pl.BlockSpec(memory_space=pltpu.VMEM)
    return pl.pallas_call(
        functools.partial(finish_body, panel=panel, micro=micro),
        in_specs=[whole] * 5,
        out_specs=(pl.BlockSpec(memory_space=pl.ANY),) * 2,
        out_shape=(
            jax.ShapeDtypeStruct((count, points, width), bf16),
            jax.ShapeDtypeStruct((count, width, width), f32),
        ),
        scratch_shapes=[
            pltpu.VMEM((count, width, points), f32),
            pltpu.VMEM((count, width, width), f32),
            pltpu.VMEM((count, width, width), f32),
            pltpu.VMEM((2, 8 * panel + 8, 128), f32),
            pltpu.VMEM((8 * panel + 8, 128), f32),
            pltpu.VMEM((count, points, width), bf16),
            pltpu.VMEM((count, width, width), f32),
            pltpu.SemaphoreType.DMA((count + 1,)),
        ],
        compiler_params=pltpu.CompilerParams(vmem_limit_bytes=28 * 2**20),
        name="finish",
    )(*(in_vmem(x) for x in (blocks, early, some, most)), order)


def in_vmem(x):
    return pltpu.with_memory_space_constraint(x, pltpu.VMEM)


def in_hbm(x):
    return pltpu.with_memory_space_constraint(x, pltpu.HBM)


PIECE_ROWS = 16
SOME_ROWS = 432


def prepare_body(offsets_any, sketch_any, full_ref, some_ref, most_ref, offsets_ref, sketch_ref, sems):
    count, points, width = sketch_ref.shape
    fetch = pltpu.make_async_copy(offsets_any, offsets_ref, sems.at[count])
    copies = [pltpu.make_async_copy(sketch_any.at[c], sketch_ref.at[c], sems.at[c]) for c in range(count)]
    fetch.start()
    for copy in copies:
        copy.start()
    fetch.wait()
    stacked = jnp.concatenate([offsets_ref[axis] for axis in range(3)], axis=0)
    stacked = jnp.concatenate([stacked, jnp.zeros((PIECE_ROWS - 3 * count, points), f32)], axis=0)
    parts = jnp.concatenate(pieces(stacked), axis=0).astype(bf16)
    full_ref[count * width:, :] = parts
    some_ref[SOME_ROWS:, :] = parts
    for c in range(count):
        copies[c].wait()
        turned = sketch_ref[c].T
        first = c * width
        full_ref[first:first + width, :] = turned
        cut = min(max(SOME_ROWS - first, 0), width)
        if cut > 0:
            some_ref[first:first + cut, :] = turned[:cut]
        if cut < width:
            most_ref[first + cut - SOME_ROWS:first + width - SOME_ROWS, :] = turned[cut:]


def prepare(offsets, sketch):
    count, points, width = sketch.shape
    whole = pl.BlockSpec(memory_space=pltpu.VMEM)
    far = pl.BlockSpec(memory_space=pl.ANY)
    extra = 3 * PIECE_ROWS
    return pl.pallas_call(
        prepare_body,
        in_specs=[far, far],
        out_specs=[whole] * 3,
        out_shape=tuple(
            pltpu.VMEM((n, points), bf16) for n in (count * width + extra, SOME_ROWS + extra, count * width - SOME_ROWS)
        ),
        scratch_shapes=[
            pltpu.VMEM(offsets.shape, f32),
            pltpu.VMEM(sketch.shape, bf16),
            pltpu.SemaphoreType.DMA((count + 1,)),
        ],
        compiler_params=pltpu.CompilerParams(vmem_limit_bytes=16 * 2**20),
        name="prepare",
    )(in_hbm(offsets), in_hbm(sketch))


class Pairs:
    def __init__(self, own_any, own_ref, pattern_any, pattern_ref, sems, partner_ref, window, listed, odd, total, meanwhile):
        count, points = own_ref.shape[1:]
        self.columns = pattern_ref.shape[1]
        self.count, self.window, self.listed = count, window, listed
        copies = [
            pltpu.make_async_copy(own_any, own_ref, sems.at[0]),
            pltpu.make_async_copy(pattern_any, pattern_ref, sems.at[1]),
        ]
        for copy in copies:
            copy.start()
        meanwhile()
        me = lax.axis_index(AXES)
        first = me * count
        side = lax.rem(me, 2)
        odd_group = 2 * side
        window[...] = jnp.zeros_like(window)
        base = partner_ref.shape[0] - 3 * PIECE_ROWS
        parts = [
            partner_ref[base + PIECE_ROWS * i:base + PIECE_ROWS * (i + 1), :].astype(f32) for i in range(3)
        ]
        partner = (parts[0] + parts[1]) + parts[2]
        for copy in copies:
            copy.wait()
        partner_group = odd_group if odd else 2 - odd_group
        for group, get in (
            (partner_group, lambda axis, at: partner[count * axis + at:count * axis + at + 1, :]),
            (1, lambda axis, at: own_ref[axis, at:at + 1, :]),
        ):
            for at in range(count):
                slot = group * count + at
                index = (first + (slot - count)).astype(f32)
                window[slot, 0:1, :] = (get(0, at) + index) - index
                window[slot, 1:2, :] = get(1, at)
                window[slot, 2:3, :] = get(2, at)

        self.found = jnp.int32(0)
        for pair in range(count * self.columns):
            cluster, column = divmod(pair, self.columns)
            source = cluster + offset_table(W)[column]
            group = 0 if source < 0 else 1 if source < count else 2
            counted = (pattern_ref[cluster, column] != 0) & (first + source >= 0) & (first + source < total)
            counted = counted & ((odd_group == group) if odd else (odd_group != group))
            listed[self.found] = pair
            self.found = self.found + counted.astype(jnp.int32)

    def of(self, pair):
        cluster, column = pair // self.columns, lax.rem(pair, self.columns)
        return cluster, column, column - W + jnp.where(column >= W - 1, 3, 0)

    def at(self, step):
        return self.of(self.listed[jnp.clip(step, 0, jnp.maximum(self.found - 1, 0))])

    def measure(self, step):
        cluster, _, distance = self.at(step)
        target = self.count + cluster
        a, b = split_points(self.window[target], self.window[target + distance], distance)
        return contract(b, a, 0, 0)


def early_body(pattern_any, own_any, full_ref, even_ref, out_ref, window, here, there, ka, kb, sketches, listed, own_ref, pattern_ref, sems, *, total):
    count, width, points = out_ref.shape
    copies = [
        pltpu.make_async_copy(ref.at[pl.ds(0, count * width)], sketches.at[pl.ds(i * count * width, count * width)], sems.at[2 + i])
        for i, ref in enumerate((full_ref, even_ref))
    ]
    for copy in copies:
        copy.start()

    def clear():
        out_ref[...] = jnp.zeros_like(out_ref)
        kb[...] = jnp.zeros_like(kb)

    pairs = Pairs(
        own_any, own_ref, pattern_any, pattern_ref, sems, even_ref, window, listed, False, total, clear
    )
    here[...] = pairs.measure(jnp.int32(0))
    for copy in copies:
        copy.wait()

    def evaluate(squares, block):
        block[...] = kernel_values(squares[...], points).astype(bf16)

    def add(step, block):
        cluster, _, distance = pairs.at(step)
        source = cluster + distance
        slot = jnp.where(source < 0, source + 2 * count, source)
        rows_of = sketches[pl.ds(pl.multiple_of(slot * width, width), width), :]
        out_ref[cluster] += jnp.dot(rows_of, block[...], preferred_element_type=f32)

    def two_steps(twice, carry):
        at = 2 * twice
        there[...] = pairs.measure(at + 1)
        evaluate(here, ka)
        add(at - 1, kb)
        here[...] = pairs.measure(at + 2)
        evaluate(there, kb)
        add(at, ka)
        return carry

    lax.fori_loop(0, pairs.found // 2, two_steps, 0)
    add(pairs.found // 2 * 2 - 1, kb)

    @pl.when(lax.rem(pairs.found, 2) == 1)
    def _():
        evaluate(here, ka)
        add(pairs.found - 1, ka)


def late_body(pattern_any, own_any, odd_ref, out_ref, window, here, there, listed, own_ref, pattern_ref, sems, *, total):
    points = out_ref.shape[1]

    def clear():
        out_ref[...] = jnp.zeros_like(out_ref)

    pairs = Pairs(
        own_any, own_ref, pattern_any, pattern_ref, sems, odd_ref, window, listed, True, total, clear
    )
    here[...] = pairs.measure(jnp.int32(0))
    half = pairs.columns // 2

    def evaluate(step, squares):
        cluster, column, _ = pairs.at(step)
        out_ref[half * cluster + lax.rem(column, half)] = kernel_values(squares[...], points).astype(bf16)

    def two_steps(twice, carry):
        at = 2 * twice
        there[...] = pairs.measure(at + 1)
        evaluate(at, here)
        here[...] = pairs.measure(at + 2)
        evaluate(at + 1, there)
        return carry

    lax.fori_loop(0, pairs.found // 2, two_steps, 0)

    @pl.when(lax.rem(pairs.found, 2) == 1)
    def _():
        evaluate(pairs.found - 1, here)


def block_call(kernel, name, weight, pattern, own, arrays, shape, dtype, extra):
    count, points = own.shape[1:]
    values = weight * pattern.size * points * points // 16
    whole = pl.BlockSpec(memory_space=pltpu.VMEM)
    far = pl.BlockSpec(memory_space=pl.ANY)
    return pl.pallas_call(
        kernel,
        in_specs=[far, far] + [whole] * len(arrays),
        out_specs=whole,
        scratch_shapes=[
            pltpu.VMEM((3 * count, 8, points), f32),
            pltpu.VMEM((points, points), f32),
            pltpu.VMEM((points, points), f32),
            *extra,
            pltpu.SMEM((pattern.size + 1,), jnp.int32),
            pltpu.VMEM(own.shape, f32),
            pltpu.SMEM(pattern.shape, jnp.int32),
            pltpu.SemaphoreType.DMA((4,)),
        ],
        out_shape=pltpu.VMEM(shape, dtype),
        cost_estimate=pl.CostEstimate(flops=40 * values, bytes_accessed=2 * values, transcendentals=3 * values),
        compiler_params=pltpu.CompilerParams(vmem_limit_bytes=16 * 2**20),
        name=name,
    )(in_hbm(pattern), in_hbm(own), *(in_vmem(x) for x in arrays))


def body(offsets, sketch, pattern, point_order):
    count, points, width = sketch.shape
    total = count * lax.axis_size(AXES)
    offsets = offsets.transpose(1, 0, 2)
    full, some, most = prepare(offsets, sketch)
    even_full = exchanged(full, 0)
    odd_some = exchanged(some, 1)
    odd_most = exchanged(most, 1)
    block = pltpu.VMEM((points, points), bf16)
    early = block_call(
        functools.partial(early_body, total=total), "early", 0, pattern, offsets, (full, even_full),
        (count, width, points), f32, [block, block, pltpu.VMEM((2 * count * width, points), bf16)],
    )
    odd_some, early = lax.optimization_barrier((odd_some, early))
    late = block_call(
        functools.partial(late_body, total=total), "late", 200, pattern, offsets, (odd_some,),
        (pattern.size // 2, points, points), bf16, [],
    )
    return finish(late, early, odd_some, odd_most, point_order)


def solution(mesh):
    rows = P(AXES, None, None)
    flat = P(AXES, None)
    return jax.shard_map(
        body,
        mesh=mesh,
        in_specs=(rows, rows, flat, flat),
        out_specs=(rows, rows),
        check_vma=False,
    )
```
